128 devices in a mesh: grp: 16 (over x, z_hi, core), seq: 8 (over y, z_lo).
Axes of the slice: x: 4, y: 4, z: 4 (z_hi: 2, z_lo: 2; z = z_hi * 2 + z_lo), core: 2. Of those that a mesh axis runs over, the one named last changes fastest.
Arguments:
- prompt_hidden: bfloat16 [16, 8192, 5120], P('grp', 'seq'), may hold values from -6 to 6
- resp_hidden: bfloat16 [16, 1024, 5120], P('grp', 'seq'), may hold values from -6 to 6
- queries: bfloat16 [16, 1024, 1024], P('grp', 'seq'), may hold values from -180 to 180
- grad_out: bfloat16 [16, 1024, 1024], P('grp', 'seq'), may hold values from -6 to 6
- kv_weight: bfloat16 [5120, 256], P(('grp', 'seq')), may hold values from -0.078125 to 0.078125
- prompt_lengths: int32 [16], P('grp'), may hold values from 4096 to 8192
- response_lengths: int32 [16, 8], P('grp'), may hold values from 1 to 128, 640 in all within a row
Outputs:
- attended: bfloat16 [16, 1024, 1024], P('grp', 'seq')
- query_grad: bfloat16 [16, 1024, 1024], P('grp', 'seq')
- prompt_kv_grad: bfloat16 [16, 8192, 256], P('grp', 'seq')
- weight_grad: float32 [5120, 256], P(('grp', 'seq'))
The draws below stay inside these ranges and needn't reach their ends.
Inputs may be any that keep to these rules, and one draw needn't show every extreme that they name: `response_lengths`: every prompt has one response of exactly 128 live tokens.
All inputs are finite; a program needn't handle non-finite values.
Results may differ from the reference program's by a relative error of at most 0.025.
The reference program's roundings to bfloat16 on the way count: a program that leaves them out, or rounds other values in their place, can miss the bound.
Values may be sent and summed in bfloat16 or wider, within the bound.
No kernel may reach another device: no remote copies, remote signals or barrier semaphores. Data moves between devices by JAX's collectives and lax.ppermute only.
A program may use at most 128 MiB of HBM per device.

```python
import math
import jax
import jax.numpy as jnp
import numpy as np
from jax import lax

D = 5120
DH = 128
HQ = 8
RT_DEV = 128
PROMPTS = 16
PLEN = 8192
RESP = 1024
N_SEQ = 8


def draw_queries(key, part):
    key = jax.random.fold_in(key, 11)
    base = jnp.clip(jax.random.normal(key, (PROMPTS, RESP, HQ * DH), jnp.float32), -6.0, 6.0)
    return base.astype(jnp.bfloat16)


def plant(values, key, smallest, top_value):
    place = [jax.random.randint(jax.random.fold_in(key, axis), (), 0, length) for axis, length in enumerate(values.shape)]
    widest = values.shape.index(max(values.shape))
    beside = place[:widest] + [(place[widest] + 1) % values.shape[widest]] + place[widest + 1:]
    return values.at[tuple(place)].set(smallest).at[tuple(beside)].set(top_value)


def block_levels(own_key, extent, split, least, largest):
    def one(dim, shards_of):
        draws = jax.random.uniform(jax.random.fold_in(jax.random.fold_in(own_key, 6), dim), (shards_of,), jnp.float32, least / len(split), largest / len(split))
        return jnp.repeat(jnp.exp(draws), extent[dim] // shards_of).reshape((-1,) + (1,) * (len(extent) - dim - 1))

    level = one(*split[0])
    for cut in split[1:]:
        level = level * one(*cut)
    return level


def profile(count, total, bound, skew):
    weights = [(1 << 20) // math.isqrt(rank ** skew) + 1 for rank in range(2, count + 1)]
    spare, holding = total - bound - (count - 1), [1] * (count - 1)
    while spare > 0:
        movable = [i for i in range(count - 1) if holding[i] < bound]
        pool, left = sum([weights[i] for i in movable]), spare
        for i in movable:
            addition = min(bound - holding[i], max(1, left * weights[i] // pool), spare)
            holding[i] = holding[i] + addition
            spare = spare - addition
    return np.array([bound] + holding)


def uneven(key, amount, total, bound, slope):
    if amount == 2:
        one = jax.random.randint(key, (), max(1, total - bound), min(bound, total - 1) + 1)
        return jnp.stack([one, total - one])
    sizes = jnp.asarray(profile(amount, total, bound, slope), jnp.int32)
    couples = (amount - 1) // 2
    giver, taker = sizes[1:1 + 2 * couples:2], sizes[2:2 + 2 * couples:2]
    slack = jnp.minimum(giver - 1, bound - taker)
    shifted = jax.random.randint(jax.random.fold_in(key, 1), (couples,), 0, 1 << 20) % (slack + 1)
    sizes = sizes.at[1:1 + 2 * couples:2].set(giver - shifted).at[2:2 + 2 * couples:2].set(taker + shifted)
    return sizes[jax.random.permutation(jax.random.fold_in(key, 2), amount)]


def centred(key, dims, spread, reach, split=(), dtype=jnp.bfloat16):
    level = block_levels(key, dims, split, -0.22, 0.18) if split else 1.0
    result = jax.random.normal(key, dims, jnp.float32) * spread * level
    return jnp.minimum(jnp.maximum(result, -reach), reach).astype(dtype)


def setup_inputs(seed: int = 0) -> dict:
    streams_of = jax.random.split(jax.random.key(seed), 8)
    return {
        "prompt_hidden": centred(streams_of[0], (PROMPTS, PLEN, D), 1.0, 6.0, ((0, 16), (1, 8))),
        "resp_hidden": centred(streams_of[1], (PROMPTS, RESP, D), 1.0, 6.0, ((0, 16), (1, 8))),
        "queries": draw_queries(jax.random.fold_in(streams_of[7], 71), 0),
        "grad_out": centred(streams_of[3], (PROMPTS, RESP, HQ * DH), 1.0, 6.0, ((0, 16), (1, 8))),
        "kv_weight": centred(streams_of[4], (D, 2 * DH), D ** -0.5, 0.078125, ((0, 128),)),
        "prompt_lengths": plant(jax.random.randint(streams_of[5], (PROMPTS,), PLEN // 2, PLEN + 1), jax.random.fold_in(streams_of[5], 1), PLEN // 2, PLEN).astype(jnp.int32),
        "response_lengths": jax.vmap(lambda own: uneven(own, N_SEQ, N_SEQ * RT_DEV * 5 // 8, RT_DEV, 2))(jax.random.split(streams_of[6], PROMPTS)).reshape((PROMPTS, N_SEQ)).astype(jnp.int32),
    }


def respond(q_rows, grad_rows, prompt_kv, resp_kv, prompt_len, resp_len):
    slots = q_rows.shape[0]
    plen_all = prompt_kv.shape[0]
    scale = DH ** -0.5
    keys = jnp.concatenate([prompt_kv[:, :DH], resp_kv[:, :DH]], 0).astype(jnp.float32)
    values = jnp.concatenate([prompt_kv[:, DH:], resp_kv[:, DH:]], 0).astype(jnp.float32)
    position = jnp.arange(slots)
    live = position < resp_len
    prompt_ok = jnp.arange(plen_all) < prompt_len
    allowed = jnp.concatenate([jnp.broadcast_to(prompt_ok[None, :], (slots, plen_all)), position[None, :] <= position[:, None]], 1)
    grad_live = jnp.where(live[:, None], grad_rows, jnp.zeros_like(grad_rows))
    q_heads = q_rows.reshape(slots, HQ, DH).astype(jnp.float32)
    g_heads = grad_live.reshape(slots, HQ, DH).astype(jnp.float32)
    scores = jnp.einsum('thd,kd->htk', q_heads, keys) * scale
    scores = jnp.where(allowed[None], scores, -jnp.inf)
    top = jnp.max(scores, 2, keepdims=True)
    expo = jnp.exp(scores - top)
    probs = expo / jnp.sum(expo, 2, keepdims=True)
    probs_b = lax.optimization_barrier(probs.astype(jnp.bfloat16)).astype(jnp.float32)
    attended = jnp.einsum('htk,kd->thd', probs_b, values)
    attended = jnp.where(live[:, None, None], attended, jnp.zeros_like(attended)).astype(jnp.bfloat16)
    delta = jnp.sum(g_heads * attended.astype(jnp.float32), 2).T
    dprob = jnp.einsum('thd,kd->htk', g_heads, values)
    dscore = probs * (dprob - delta[:, :, None]) * scale
    dscore = lax.optimization_barrier(dscore.astype(jnp.bfloat16)).astype(jnp.float32)
    query_grad = jnp.einsum('htk,kd->thd', dscore, keys).astype(jnp.bfloat16)
    key_grad = jnp.einsum('htk,thd->kd', dscore, q_heads)
    value_grad = jnp.einsum('htk,thd->kd', probs_b, g_heads)
    kv_grad = jnp.concatenate([key_grad, value_grad], 1)
    return attended.reshape(slots, HQ * DH), query_grad.reshape(slots, HQ * DH), kv_grad[:plen_all], kv_grad[plen_all:]


def reference(prompt_hidden, resp_hidden, queries, grad_out, kv_weight, prompt_lengths, response_lengths):
    def one_group(items):
        hidden_p, hidden_r, q_group, g_group, prompt_len, lengths_row = items
        prompt_kv = jnp.dot(hidden_p, kv_weight, preferred_element_type=jnp.float32).astype(jnp.bfloat16)
        resp_kv = jnp.dot(hidden_r, kv_weight, preferred_element_type=jnp.float32).astype(jnp.bfloat16)

        def one_resp(pieces):
            q_rows, g_rows, kv_rows, resp_len = pieces
            return respond(q_rows, g_rows, prompt_kv, kv_rows, prompt_len, resp_len)

        attended, query_grad, prompt_parts, resp_grad = lax.map(one_resp, (
            q_group.reshape(N_SEQ, RT_DEV, HQ * DH), g_group.reshape(N_SEQ, RT_DEV, HQ * DH),
            resp_kv.reshape(N_SEQ, RT_DEV, 2 * DH), lengths_row))
        prompt_grad = jnp.sum(prompt_parts, 0).astype(jnp.bfloat16)
        resp_grad = resp_grad.reshape(RESP, 2 * DH).astype(jnp.bfloat16)
        weight_part = jnp.dot(hidden_p.T, prompt_grad, preferred_element_type=jnp.float32)
        weight_part = weight_part + jnp.dot(hidden_r.T, resp_grad, preferred_element_type=jnp.float32)
        return attended.reshape(RESP, HQ * DH), query_grad.reshape(RESP, HQ * DH), prompt_grad, weight_part

    attended, query_grad, prompt_kv_grad, weight_parts = lax.map(one_group, (
        prompt_hidden, resp_hidden, queries, grad_out, prompt_lengths, response_lengths))
    weight_grad = jnp.sum(weight_parts, 0)
    return attended, query_grad, prompt_kv_grad, weight_grad
```

```python
import functools

import jax
import jax.numpy as jnp
from jax import lax
from jax.experimental import pallas as pl
from jax.experimental.pallas import tpu as pltpu
from jax.sharding import Mesh
from jax.sharding import PartitionSpec as P

AXES = ("x", "zh", "c", "y", "zl")
GRP = ("x", "zh", "c")
SEQ = ("y", "zl")
CHIPS = ("x", "zh", "y", "zl")
N_SEQ = 8
HEADS = 8
DH = 128
SLOTS = 64
ROWS = SLOTS * HEADS
NEG = -1e30
LOG2E = 1.4426950408889634
NT = (((1,), (1,)), ((), ()))
F32 = jnp.float32
BF16 = jnp.bfloat16


def stack_heads(block, first):
    return jnp.concatenate(
        [block[:, (first + h) * DH : (first + h + 1) * DH] for h in range(HEADS)], 0
    )


def stats_kernel(coef, valid_ref, qg_ref, kv_ref, limit_ref, out_ref, stat_ref):
    plen = kv_ref.shape[0] - DH
    valid = valid_ref[0]
    bias = jnp.where(lax.broadcasted_iota(jnp.int32, (1, plen), 1) < valid, 0.0, NEG)
    lane = lax.broadcasted_iota(jnp.int32, (SLOTS, DH), 1)
    causal = jnp.where(lane <= limit_ref[...], 0.0, NEG)
    half = HEADS // 2
    causal = jnp.concatenate([causal] * half, 0)
    columns = lax.broadcasted_iota(jnp.int32, (half * SLOTS, DH), 1)
    for part in range(2):
        base = part * half
        q = jnp.concatenate(
            [qg_ref[:, (base + h) * DH : (base + h + 1) * DH] for h in range(half)], 0
        )
        g = jnp.concatenate(
            [qg_ref[:, (HEADS + base + h) * DH : (HEADS + base + h + 1) * DH] for h in range(half)],
            0,
        )
        s = lax.dot_general(q, kv_ref[:plen, :DH], NT, preferred_element_type=F32) + bias
        sr = lax.dot_general(q, kv_ref[plen:, :DH], NT, preferred_element_type=F32) + causal
        top = jnp.maximum(jnp.max(s, 1, keepdims=True), jnp.max(sr, 1, keepdims=True))
        p = jnp.exp2((s - top) * coef)
        pr = jnp.exp2((sr - top) * coef)
        total = jnp.sum(p, 1, keepdims=True) + jnp.sum(pr, 1, keepdims=True)
        o = jnp.dot(p.astype(BF16), kv_ref[:plen, DH:], preferred_element_type=F32)
        o = o + jnp.dot(pr.astype(BF16), kv_ref[plen:, DH:], preferred_element_type=F32)
        o = o / total
        d = jnp.sum(o * g.astype(F32), 1, keepdims=True)
        for h in range(half):
            out_ref[:, (base + h) * DH : (base + h + 1) * DH] = o[
                h * SLOTS : (h + 1) * SLOTS
            ].astype(BF16)
        table = jnp.where(columns == 0, top * coef, jnp.where(columns == 1, total, d))
        stat_ref[:, part * half * SLOTS : (part + 1) * half * SLOTS] = table.T[:8]


def grad_kernel(
    coef, scale, valid_ref, qg_ref, kv_ref, limit_ref, stat_ref, out_ref,
    att_ref, qgrad_ref, kvgrad_ref, acc_ref,
):
    step = pl.program_id(0)
    plen = kv_ref.shape[0] - DH
    valid = valid_ref[0]
    top = stat_ref[0:1]
    inv = stat_ref[1:2]
    delta = stat_ref[2:3]
    mine = stat_ref[3:4]
    q = stack_heads(qg_ref, 0)
    g = stack_heads(qg_ref, HEADS)

    @pl.when(step == 0)
    def _():
        acc_ref[...] = jnp.zeros_like(acc_ref)

    weight = jnp.broadcast_to(mine, (DH, ROWS)).T
    for h in range(HEADS):
        cols = pl.ds(h * DH, DH)
        att_ref[:, cols] = (
            out_ref[:, cols].astype(F32) * weight[h * SLOTS : (h + 1) * SLOTS]
        ).astype(BF16)

    chunk = 256
    bounds = [(i, min(chunk, plen - i)) for i in range(0, plen, chunk)] + [(plen, DH)]
    dq = jnp.zeros((ROWS, DH), F32)
    for start, size in bounds:
        rows = pl.ds(start, size)
        k = kv_ref[rows, :DH]
        v = kv_ref[rows, DH:]
        s = lax.dot_general(k, q, NT, preferred_element_type=F32)
        place = lax.broadcasted_iota(jnp.int32, (size, ROWS), 0)
        if start < plen:
            seen = place < valid - start
        else:
            seen = place <= limit_ref[0:1]
        s = jnp.where(seen, s * coef - top, NEG)
        p = jnp.exp2(s) * inv
        dp = lax.dot_general(v, g, NT, preferred_element_type=F32)
        ds = (p * (dp - delta) * scale).astype(BF16)
        acc_ref[rows, :DH] += jnp.dot(ds, q, preferred_element_type=F32)
        acc_ref[rows, DH:] += jnp.dot(p.astype(BF16), g, preferred_element_type=F32)
        dq = dq + lax.dot_general(ds, k, (((0,), (0,)), ((), ())), preferred_element_type=F32)
    for h in range(HEADS):
        qgrad_ref[:, h * DH : (h + 1) * DH] = dq[h * SLOTS : (h + 1) * SLOTS].astype(BF16)

    @pl.when(step == pl.num_programs(0) - 1)
    def _():
        kvgrad_ref[...] = acc_ref[...].astype(BF16)


def spread(block, axes, count):
    copies = jnp.broadcast_to(block[None], (count,) + block.shape)
    return lax.all_to_all(copies, axes, 0, 0, tiled=True)


def per_device(
    prompt_hidden, resp_hidden, queries, grad_out, kv_weight, prompt_lengths, response_lengths
):
    rank = lax.axis_index(SEQ)
    core = lax.axis_index("c")
    slots = resp_hidden.shape[1]
    plen = prompt_hidden.shape[1]
    model = prompt_hidden.shape[2]
    width = queries.shape[2]
    scale = DH ** (-0.5)
    coef = scale * LOG2E
    prompt_rows = prompt_hidden[0]
    resp_rows = resp_hidden[0]
    swap = [(0, 1), (1, 0)]

    shard = kv_weight.shape[0]
    near = spread(kv_weight, CHIPS, 64).reshape(8, 8, shard, 2 * DH)
    far = lax.ppermute(near, "c", swap)
    first = jnp.where(core == 0, near, far)
    second = jnp.where(core == 0, far, near)
    weight = jnp.stack([first, second], 1).reshape(model, 2 * DH)

    own_kv = jnp.dot(prompt_rows, weight, preferred_element_type=F32).astype(BF16)
    resp_kv = jnp.dot(resp_rows, weight, preferred_element_type=F32).astype(BF16)
    kv = jnp.concatenate([own_kv, resp_kv], 0)

    lengths = response_lengths[0]
    live_all = slots * N_SEQ * 5 // 8
    ends = jnp.cumsum(lengths)
    starts = ends - lengths
    slot_id = jnp.arange(N_SEQ * slots)
    of_resp = slot_id // slots
    offset = slot_id % slots
    dest = jnp.where(offset < lengths[of_resp], starts[of_resp] + offset, -1)
    pick = (jnp.arange(live_all)[:, None] == dest[None, :]).astype(BF16)
    packed_id = jnp.arange(live_all)
    my_start = jnp.sum(jnp.where(jnp.arange(N_SEQ) == rank, starts, 0))
    my_len = jnp.sum(jnp.where(jnp.arange(N_SEQ) == rank, lengths, 0))
    in_mine = (packed_id >= my_start) & (packed_id < my_start + my_len)
    limit = jnp.where(in_mine, packed_id - my_start, -1).astype(jnp.int32)

    qg_own = jnp.concatenate([queries[0], grad_out[0]], 1)
    qg_all = spread(qg_own, SEQ, N_SEQ).reshape(N_SEQ * slots, 2 * width)
    qg = jnp.dot(pick, qg_all, preferred_element_type=F32).astype(BF16)

    valid = (prompt_lengths - plen * rank).astype(jnp.int32)
    steps = live_all // SLOTS
    total_rows = live_all * HEADS
    keys = plen + slots
    limit_cols = jnp.broadcast_to(limit[:, None], (live_all, DH))
    limit_rows = jnp.broadcast_to(
        limit.reshape(steps, 1, SLOTS), (steps, HEADS, SLOTS)
    ).reshape(1, total_rows)
    limit_rows = jnp.broadcast_to(limit_rows, (8, total_rows))

    smem = pl.BlockSpec(memory_space=pltpu.SMEM)
    row_block = lambda cols: pl.BlockSpec((SLOTS, cols), lambda i: (i, 0))
    lane_block = pl.BlockSpec((8, ROWS), lambda i: (0, i))
    whole = pl.BlockSpec((keys, 2 * DH), lambda i: (0, 0))
    out, stat = pl.pallas_call(
        functools.partial(stats_kernel, coef),
        grid=(steps,),
        in_specs=[smem, row_block(2 * width), whole, row_block(DH)],
        out_specs=[row_block(width), lane_block],
        out_shape=[
            jax.ShapeDtypeStruct((live_all, width), BF16),
            jax.ShapeDtypeStruct((8, total_rows), F32),
        ],
        compiler_params=pltpu.CompilerParams(vmem_limit_bytes=48 << 20),
        cost_estimate=pl.CostEstimate(
            flops=4 * total_rows * keys * DH, bytes_accessed=8 << 20, transcendentals=total_rows * keys
        ),
        name="attend_stats",
    )(valid, qg, kv, limit_cols)

    own_stat = stat[:3].reshape(3 * total_rows // DH, DH)
    stats = spread(own_stat, SEQ, N_SEQ).reshape(N_SEQ, 3, total_rows)
    top = jnp.max(stats[:, 0], 0)
    share = stats[:, 1] * jnp.exp2(stats[:, 0] - top)
    total = jnp.sum(share, 0)
    inv = 1.0 / total
    delta = jnp.sum(share * stats[:, 2], 0) * inv
    mine = stat[1] * jnp.exp2(stat[0] - top) * inv
    merged = jnp.stack([top, inv, delta, mine, mine, mine, mine, mine], 0)

    att, qgrad, kvgrad = pl.pallas_call(
        functools.partial(grad_kernel, coef, scale),
        grid=(steps,),
        in_specs=[smem, row_block(2 * width), whole, lane_block, lane_block, row_block(width)],
        out_specs=[row_block(width), row_block(width), whole],
        out_shape=[
            jax.ShapeDtypeStruct((live_all, width), BF16),
            jax.ShapeDtypeStruct((live_all, width), BF16),
            jax.ShapeDtypeStruct((keys, 2 * DH), BF16),
        ],
        scratch_shapes=[pltpu.VMEM((keys, 2 * DH), F32)],
        compiler_params=pltpu.CompilerParams(vmem_limit_bytes=48 << 20),
        cost_estimate=pl.CostEstimate(
            flops=10 * total_rows * keys * DH, bytes_accessed=8 << 20, transcendentals=total_rows * keys
        ),
        name="attend_grads",
    )(valid, qg, kv, limit_rows, merged, out)

    both = jnp.concatenate([att, qgrad], 1)
    both = lax.dot_general(
        pick, both, (((0,), (0,)), ((), ())), preferred_element_type=F32
    ).astype(BF16)
    both = lax.all_to_all(both.reshape(N_SEQ, slots, 2 * width), SEQ, 0, 0, tiled=True)
    both = jnp.sum(both.astype(F32), 0).astype(BF16)
    attended = both[:, :width]
    query_grad = both[:, width:]

    contract = (((0,), (0,)), ((), ()))
    prompt_grad = kvgrad[:plen]
    resp_grad = kvgrad[plen:]
    term = lax.dot_general(prompt_rows, prompt_grad, contract, preferred_element_type=F32)
    term = term + lax.dot_general(resp_rows, resp_grad, contract, preferred_element_type=F32)
    term = term.reshape(8, 2, 8, shard, 2 * DH)
    keep = jnp.where(core == 0, term[:, 0], term[:, 1])
    give = jnp.where(core == 0, term[:, 1], term[:, 0]).astype(BF16)
    got = lax.ppermute(give, "c", swap)
    chip_sum = (keep + got.astype(F32)).astype(BF16).reshape(64, shard, 2 * DH)
    parts = lax.all_to_all(chip_sum, CHIPS, 0, 0, tiled=True)
    weight_grad = jnp.sum(parts.astype(F32), 0)
    return attended[None], query_grad[None], prompt_grad[None], weight_grad


def solution(mesh):
    fine = Mesh(mesh.devices.reshape(4, 2, 2, 4, 2), AXES)
    return jax.shard_map(
        per_device,
        mesh=fine,
        in_specs=(
            P(GRP, SEQ, None),
            P(GRP, SEQ, None),
            P(GRP, SEQ, None),
            P(GRP, SEQ, None),
            P(AXES, None),
            P(GRP),
            P(GRP, None),
        ),
        out_specs=(
            P(GRP, SEQ, None),
            P(GRP, SEQ, None),
            P(GRP, SEQ, None),
            P(AXES, None),
        ),
        check_vma=False,
    )
```

```python
import functools

import jax
import jax.numpy as jnp
from jax import lax
from jax.experimental import pallas as pl
from jax.experimental.pallas import tpu as pltpu
from jax.sharding import Mesh
from jax.sharding import PartitionSpec as P

AXES = ("x", "zh", "c", "y", "zl")
GRP = ("x", "zh", "c")
SEQ = ("y", "zl")
CHIPS = ("x", "zh", "y", "zl")
N_SEQ = 8
HEADS = 8
HALF = 4
DH = 128
SLOTS = 128
PAIRS = 8
NEG = -1e30
LOG2E = 1.4426950408889634
NT = (((1,), (1,)), ((), ()))
TN = (((0,), (0,)), ((), ()))
F32 = jnp.float32
BF16 = jnp.bfloat16
SWAP = [(0, 1), (1, 0)]


def params():
    return pltpu.CompilerParams(vmem_limit_bytes=48 << 20)


def stack_heads(ref, first):
    return jnp.concatenate(
        [ref[:, (first + h) * DH : (first + h + 1) * DH] for h in range(HALF)], 0
    )


def project_kernel(core_ref, near_ref, far_ref, prompt_ref, resp_ref, kv_ref, acc_ref):
    step = pl.program_id(0)
    plen = prompt_ref.shape[0]
    swapped = core_ref[0] == 1
    near = near_ref[0]
    far = far_ref[0]
    weight = jnp.concatenate(
        [jnp.where(swapped, far, near), jnp.where(swapped, near, far)], 0
    )

    @pl.when(step == 0)
    def _():
        acc_ref[...] = jnp.zeros_like(acc_ref)

    acc_ref[:plen] += jnp.dot(prompt_ref[...], weight, preferred_element_type=F32)
    acc_ref[plen:] += jnp.dot(resp_ref[...], weight, preferred_element_type=F32)

    @pl.when(step == pl.num_programs(0) - 1)
    def _():
        kv_ref[...] = acc_ref[...].astype(BF16)


def stats_kernel(coef, valid_ref, q_ref, kv_ref, limit_ref, out_ref, stat_ref):
    plen = kv_ref.shape[0] - DH
    valid = valid_ref[0]
    bias = jnp.where(lax.broadcasted_iota(jnp.int32, (1, plen), 1) < valid, 0.0, NEG)
    lane = lax.broadcasted_iota(jnp.int32, (SLOTS, DH), 1)
    causal = jnp.where(lane <= limit_ref[...], 0.0, NEG)
    causal = jnp.concatenate([causal] * HALF, 0)
    table = jnp.zeros((SLOTS, DH), F32)
    for base in (0, HALF):
        q = stack_heads(q_ref, base)
        s = lax.dot_general(q, kv_ref[:plen, :DH], NT, preferred_element_type=F32) + bias
        sr = lax.dot_general(q, kv_ref[plen:, :DH], NT, preferred_element_type=F32) + causal
        top = jnp.maximum(jnp.max(s, 1, keepdims=True), jnp.max(sr, 1, keepdims=True))
        p = jnp.exp2((s - top) * coef)
        pr = jnp.exp2((sr - top) * coef)
        total = jnp.sum(p, 1, keepdims=True) + jnp.sum(pr, 1, keepdims=True)
        o = jnp.dot(p.astype(BF16), kv_ref[:plen, DH:], preferred_element_type=F32)
        o = o + jnp.dot(pr.astype(BF16), kv_ref[plen:, DH:], preferred_element_type=F32)
        o = o / total
        top = top * coef
        for h in range(HALF):
            rows = slice(h * SLOTS, (h + 1) * SLOTS)
            head = base + h
            out_ref[:, head * DH : (head + 1) * DH] = o[rows].astype(BF16)
            table = jnp.where(lane == head, top[rows], table)
            table = jnp.where(lane == HEADS + head, total[rows], table)
    stat_ref[...] = table.T[: 2 * HEADS]


def delta_kernel(out_ref, g_ref, delta_ref):
    lane = lax.broadcasted_iota(jnp.int32, (SLOTS, DH), 1)
    table = jnp.zeros((SLOTS, DH), F32)
    for h in range(HEADS):
        cols = slice(h * DH, (h + 1) * DH)
        d = jnp.sum(out_ref[:, cols].astype(F32) * g_ref[:, cols].astype(F32), 1, keepdims=True)
        table = jnp.where(lane == h, d, table)
    delta_ref[...] = table.T[:HEADS]


def grad_kernel(
    coef, scale, valid_ref, q_ref, g_ref, kv_ref, limit_ref, stat_ref,
    qgrad_ref, kvgrad_ref, acc_ref,
):
    step = pl.program_id(0)
    plen = kv_ref.shape[0] - DH
    valid = valid_ref[0]
    tops = stat_ref[:, :HEADS]
    top_all = jnp.max(tops, 0)
    share = stat_ref[:, HEADS : 2 * HEADS] * jnp.exp2(tops - top_all)
    inv_all = 1.0 / jnp.sum(share, 0)
    delta_all = jnp.sum(share * stat_ref[:, 2 * HEADS :], 0) * inv_all

    @pl.when(step == 0)
    def _():
        acc_ref[...] = jnp.zeros_like(acc_ref)

    chunk = 256
    bounds = [(i, min(chunk, plen - i)) for i in range(0, plen, chunk)] + [(plen, DH)]
    limit = jnp.concatenate([limit_ref[0:1]] * HALF, 1)
    for base in (0, HALF):
        q = stack_heads(q_ref, base)
        g = stack_heads(g_ref, base)
        line = lambda t: jnp.concatenate([t[base + h : base + h + 1] for h in range(HALF)], 1)
        top, inv, delta = line(top_all), line(inv_all), line(delta_all)
        dq = jnp.zeros((HALF * SLOTS, DH), F32)
        for start, size in bounds:
            rows = pl.ds(start, size)
            k = kv_ref[rows, :DH]
            v = kv_ref[rows, DH:]
            s = lax.dot_general(k, q, NT, preferred_element_type=F32)
            place = lax.broadcasted_iota(jnp.int32, (size, HALF * SLOTS), 0)
            seen = place < valid - start if start < plen else place <= limit
            p = jnp.exp2(jnp.where(seen, s * coef - top, NEG)) * inv
            dp = lax.dot_general(v, g, NT, preferred_element_type=F32)
            ds = (p * (dp - delta) * scale).astype(BF16)
            acc_ref[rows, :DH] += jnp.dot(ds, q, preferred_element_type=F32)
            acc_ref[rows, DH:] += jnp.dot(p.astype(BF16), g, preferred_element_type=F32)
            dq = dq + lax.dot_general(ds, k, TN, preferred_element_type=F32)
        for h in range(HALF):
            qgrad_ref[:, (base + h) * DH : (base + h + 1) * DH] = dq[
                h * SLOTS : (h + 1) * SLOTS
            ].astype(BF16)

    @pl.when(step == pl.num_programs(0) - 1)
    def _():
        kvgrad_ref[...] = acc_ref[...].astype(BF16)


def weight_kernel(core_ref, grad_ref, prompt_ref, resp_ref, keep_ref, give_ref):
    plen = prompt_ref.shape[0]
    part = prompt_ref.shape[1] // 2
    swapped = core_ref[0] == 1
    t = lax.dot_general(grad_ref[:plen], prompt_ref[...], TN, preferred_element_type=F32)
    t = t + lax.dot_general(grad_ref[plen:], resp_ref[...], TN, preferred_element_type=F32)
    t = t.T
    keep_ref[0] = jnp.where(swapped, t[part:], t[:part])
    give_ref[0] = jnp.where(swapped, t[:part], t[part:]).astype(BF16)


def spread(block, axes, count):
    copies = jnp.broadcast_to(block[None], (count,) + block.shape)
    return lax.all_to_all(copies, axes, 0, 0, tiled=True)


def per_device(
    prompt_hidden, resp_hidden, queries, grad_out, kv_weight, prompt_lengths, response_lengths
):
    rank = lax.axis_index(SEQ)
    core = lax.axis_index("c")
    core_id = core.astype(jnp.int32).reshape(1)
    slots = resp_hidden.shape[1]
    plen = prompt_hidden.shape[1]
    model = prompt_hidden.shape[2]
    width = queries.shape[2]
    scale = DH ** (-0.5)
    coef = scale * LOG2E
    prompt_rows = prompt_hidden[0]
    resp_rows = resp_hidden[0]
    keys = plen + slots
    smem = pl.BlockSpec(memory_space=pltpu.SMEM)

    q_all = spread(queries[0], SEQ, N_SEQ).reshape(N_SEQ * slots, width)
    g_all = spread(grad_out[0], SEQ, N_SEQ).reshape(N_SEQ * slots, width)

    shard = kv_weight.shape[0]
    near = spread(kv_weight, CHIPS, 64).reshape(PAIRS, 8 * shard, 2 * DH)
    far = lax.ppermute(near, "c", SWAP)
    wide = model // PAIRS
    kv = pl.pallas_call(
        project_kernel,
        grid=(PAIRS,),
        in_specs=[
            smem,
            pl.BlockSpec((1, 8 * shard, 2 * DH), lambda i: (i, 0, 0)),
            pl.BlockSpec((1, 8 * shard, 2 * DH), lambda i: (i, 0, 0)),
            pl.BlockSpec((plen, wide), lambda i: (0, i)),
            pl.BlockSpec((slots, wide), lambda i: (0, i)),
        ],
        out_specs=pl.BlockSpec((keys, 2 * DH), lambda i: (0, 0)),
        out_shape=jax.ShapeDtypeStruct((keys, 2 * DH), BF16),
        scratch_shapes=[pltpu.VMEM((keys, 2 * DH), F32)],
        compiler_params=params(),
        cost_estimate=pl.CostEstimate(
            flops=2 * keys * model * 2 * DH, bytes_accessed=2 * keys * model, transcendentals=0
        ),
        name="project",
    )(core_id, near, far, prompt_rows, resp_rows)

    lengths = response_lengths[0]
    live_all = slots * N_SEQ * 5 // 8
    ends = jnp.cumsum(lengths)
    packed = jnp.arange(live_all)
    past = packed[:, None] >= ends[None, :]
    source = packed + jnp.sum(jnp.where(past, slots - lengths[None, :], 0), 1)
    pick = (source[:, None] == jnp.arange(N_SEQ * slots)[None, :]).astype(BF16)
    offset = source - rank * slots
    limit = jnp.where((offset >= 0) & (offset < slots), offset, -1).astype(jnp.int32)
    limit_cols = jnp.broadcast_to(limit[:, None], (live_all, DH))
    limit_rows = jnp.broadcast_to(limit[None, :], (8, live_all))
    valid = (prompt_lengths - plen * rank).astype(jnp.int32)

    q = jnp.dot(pick, q_all, preferred_element_type=F32).astype(BF16)
    steps = live_all // SLOTS
    rows = live_all * HEADS
    row_block = pl.BlockSpec((SLOTS, width), lambda i: (i, 0))
    whole = pl.BlockSpec((keys, 2 * DH), lambda i: (0, 0))
    out, stat = pl.pallas_call(
        functools.partial(stats_kernel, coef),
        grid=(steps,),
        in_specs=[smem, row_block, whole, pl.BlockSpec((SLOTS, DH), lambda i: (i, 0))],
        out_specs=[row_block, pl.BlockSpec((2 * HEADS, SLOTS), lambda i: (0, i))],
        out_shape=[
            jax.ShapeDtypeStruct((live_all, width), BF16),
            jax.ShapeDtypeStruct((2 * HEADS, live_all), F32),
        ],
        compiler_params=params(),
        cost_estimate=pl.CostEstimate(
            flops=4 * rows * keys * DH, bytes_accessed=4 << 20, transcendentals=rows * keys
        ),
        name="attend_stats",
    )(valid, q, kv, limit_cols)

    g = jnp.dot(pick, g_all, preferred_element_type=F32).astype(BF16)
    delta = pl.pallas_call(
        delta_kernel,
        grid=(steps,),
        in_specs=[row_block, row_block],
        out_specs=pl.BlockSpec((HEADS, SLOTS), lambda i: (0, i)),
        out_shape=jax.ShapeDtypeStruct((HEADS, live_all), F32),
        compiler_params=params(),
        name="partial_delta",
    )(out, g)
    stats = spread(jnp.concatenate([stat, delta], 0), SEQ, N_SEQ)

    parts = lax.dot_general(pick, out, TN, preferred_element_type=F32).astype(BF16)
    parts = lax.all_to_all(parts.reshape(N_SEQ, slots, width), SEQ, 0, 0, tiled=True)

    qgrad, kvgrad = pl.pallas_call(
        functools.partial(grad_kernel, coef, scale),
        grid=(steps,),
        in_specs=[
            smem, row_block, row_block, whole,
            pl.BlockSpec((8, SLOTS), lambda i: (0, i)),
            pl.BlockSpec((N_SEQ, 3 * HEADS, SLOTS), lambda i: (0, 0, i)),
        ],
        out_specs=[row_block, whole],
        out_shape=[
            jax.ShapeDtypeStruct((live_all, width), BF16),
            jax.ShapeDtypeStruct((keys, 2 * DH), BF16),
        ],
        scratch_shapes=[pltpu.VMEM((keys, 2 * DH), F32)],
        compiler_params=params(),
        cost_estimate=pl.CostEstimate(
            flops=10 * rows * keys * DH, bytes_accessed=8 << 20, transcendentals=rows * keys
        ),
        name="attend_grads",
    )(valid, q, g, kv, limit_rows, stats)

    back = lax.dot_general(pick, qgrad, TN, preferred_element_type=F32).astype(BF16)
    back = lax.all_to_all(back.reshape(N_SEQ, slots, width), SEQ, 0, 0, tiled=True)
    query_grad = jnp.sum(back.astype(F32), 0).astype(BF16)

    keep, give = pl.pallas_call(
        weight_kernel,
        grid=(PAIRS,),
        in_specs=[
            smem,
            whole,
            pl.BlockSpec((plen, wide), lambda i: (0, i)),
            pl.BlockSpec((slots, wide), lambda i: (0, i)),
        ],
        out_specs=[
            pl.BlockSpec((1, 8 * shard, 2 * DH), lambda i: (i, 0, 0)),
            pl.BlockSpec((1, 8 * shard, 2 * DH), lambda i: (i, 0, 0)),
        ],
        out_shape=[
            jax.ShapeDtypeStruct((PAIRS, 8 * shard, 2 * DH), F32),
            jax.ShapeDtypeStruct((PAIRS, 8 * shard, 2 * DH), BF16),
        ],
        compiler_params=params(),
        cost_estimate=pl.CostEstimate(
            flops=2 * keys * model * 2 * DH, bytes_accessed=2 * keys * model, transcendentals=0
        ),
        name="weight_grad",
    )(core_id, kvgrad, prompt_rows, resp_rows)
    got = lax.ppermute(give, "c", SWAP)
    chip_sum = (keep + got.astype(F32)).astype(BF16).reshape(64, shard, 2 * DH)
    shares = lax.all_to_all(chip_sum, CHIPS, 0, 0, tiled=True)
    weight_grad = jnp.sum(shares.astype(F32), 0)

    top = jnp.max(stats[:, :HEADS], 0)
    share = stats[:, HEADS : 2 * HEADS] * jnp.exp2(stats[:, :HEADS] - top)
    share = share / jnp.sum(share, 0)
    my_len = jnp.sum(jnp.where(jnp.arange(N_SEQ) == rank, lengths, 0))
    my_start = jnp.sum(jnp.where(jnp.arange(N_SEQ) == rank, ends, 0)) - my_len
    share = lax.dynamic_slice_in_dim(
        jnp.pad(share, ((0, 0), (0, 0), (0, slots))), my_start, slots, 2
    )
    share = jnp.where(jnp.arange(slots) < my_len, share, 0.0).transpose(0, 2, 1)
    parts = parts.astype(F32).reshape(N_SEQ, slots, HEADS, DH) * share[..., None]
    attended = jnp.sum(parts, 0).astype(BF16).reshape(slots, width)
    return attended[None], query_grad[None], kvgrad[None, :plen], weight_grad


def solution(mesh):
    fine = Mesh(mesh.devices.reshape(4, 2, 2, 4, 2), AXES)
    return jax.shard_map(
        per_device,
        mesh=fine,
        in_specs=(
            P(GRP, SEQ, None),
            P(GRP, SEQ, None),
            P(GRP, SEQ, None),
            P(GRP, SEQ, None),
            P(AXES, None),
            P(GRP),
            P(GRP, None),
        ),
        out_specs=(
            P(GRP, SEQ, None),
            P(GRP, SEQ, None),
            P(GRP, SEQ, None),
            P(AXES, None),
        ),
        check_vma=False,
    )
```

```python
import functools

import jax
import jax.numpy as jnp
from jax import lax
from jax.experimental import pallas as pl
from jax.experimental.pallas import tpu as pltpu
from jax.sharding import Mesh
from jax.sharding import PartitionSpec as P

AXES = ("x", "zh", "c", "y", "zl")
GRP = ("x", "zh", "c")
SEQ = ("y", "zl")
CHIPS = ("x", "zh", "y", "zl")
N_SEQ = 8
HEADS = 8
HALF = 4
DH = 128
SLOTS = 128
PAIRS = 8
NEG = -1e30
LOG2E = 1.4426950408889634
NT = (((1,), (1,)), ((), ()))
TN = (((0,), (0,)), ((), ()))
F32 = jnp.float32
BF16 = jnp.bfloat16
SWAP = [(0, 1), (1, 0)]


def params(mib):
    return pltpu.CompilerParams(vmem_limit_bytes=mib << 20)


def shift(k):
    return [((i + k) % 4, i) for i in range(4)]


def stack_heads(ref, first):
    return jnp.concatenate(
        [ref[:, (first + h) * DH : (first + h + 1) * DH] for h in range(HALF)], 0
    )


def fetch(source_a, source_b, buf, sems, order_ref, wide):
    split = source_a.shape[0]
    copies = []
    for i in range(PAIRS):
        there = pl.ds(pl.multiple_of(order_ref[i] * wide, DH), wide)
        here = pl.ds(i * wide, wide)
        pair = (
            pltpu.make_async_copy(source_a.at[:, there], buf.at[:split, here], sems.at[i, 0]),
            pltpu.make_async_copy(source_b.at[:, there], buf.at[split:, here], sems.at[i, 1]),
        )
        for copy in pair:
            copy.start()
        copies.append(pair)
    return copies


def project_kernel(core_ref, order_ref, *refs):
    nears, fars = refs[:4], refs[4:8]
    prompt_ref, resp_ref, kv_ref, buf, weight, acc, sems = refs[8:]
    wide = weight.shape[0] // PAIRS
    half = wide // 2
    copies = fetch(prompt_ref, resp_ref, buf, sems, order_ref, wide)
    swapped = core_ref[0] == 1
    for i in range(PAIRS):
        near = nears[i // 2][i % 2]
        far = fars[i // 2][i % 2]
        weight[i * wide : i * wide + half] = jnp.where(swapped, far, near)
        weight[i * wide + half : (i + 1) * wide] = jnp.where(swapped, near, far)
    groups = 4
    each = PAIRS // groups
    for part in range(groups):
        for pair in copies[part * each : (part + 1) * each]:
            for copy in pair:
                copy.wait()
        cols = slice(part * each * wide, (part + 1) * each * wide)
        t = jnp.dot(buf[:, cols], weight[cols], preferred_element_type=F32)
        if part == 0:
            acc[...] = t
        elif part < groups - 1:
            acc[...] += t
        else:
            kv_ref[...] = (acc[...] + t).astype(BF16)


def stats_kernel(coef, valid_ref, q_ref, kv_ref, limit_ref, out_ref, stat_ref):
    plen = kv_ref.shape[0] - DH
    valid = valid_ref[0]
    bias = jnp.where(lax.broadcasted_iota(jnp.int32, (1, plen), 1) < valid, 0.0, NEG)
    lane = lax.broadcasted_iota(jnp.int32, (SLOTS, DH), 1)
    causal = jnp.where(lane <= limit_ref[...], 0.0, NEG)
    causal = jnp.concatenate([causal] * HALF, 0)
    table = jnp.zeros((SLOTS, DH), F32)
    for base in (0, HALF):
        q = stack_heads(q_ref, base)
        s = lax.dot_general(q, kv_ref[:plen, :DH], NT, preferred_element_type=F32) + bias
        sr = lax.dot_general(q, kv_ref[plen:, :DH], NT, preferred_element_type=F32) + causal
        top = jnp.maximum(jnp.max(s, 1, keepdims=True), jnp.max(sr, 1, keepdims=True))
        p = jnp.exp2((s - top) * coef)
        pr = jnp.exp2((sr - top) * coef)
        total = jnp.sum(p, 1, keepdims=True) + jnp.sum(pr, 1, keepdims=True)
        o = jnp.dot(p.astype(BF16), kv_ref[:plen, DH:], preferred_element_type=F32)
        o = o + jnp.dot(pr.astype(BF16), kv_ref[plen:, DH:], preferred_element_type=F32)
        o = o / total
        top = top * coef
        for h in range(HALF):
            rows = slice(h * SLOTS, (h + 1) * SLOTS)
            head = base + h
            out_ref[:, head * DH : (head + 1) * DH] = o[rows].astype(BF16)
            table = jnp.where(lane == head, top[rows], table)
            table = jnp.where(lane == HEADS + head, total[rows], table)
    stat_ref[...] = table.T[: 2 * HEADS]


def delta_kernel(out_ref, g_ref, delta_ref):
    lane = lax.broadcasted_iota(jnp.int32, (SLOTS, DH), 1)
    table = jnp.zeros((SLOTS, DH), F32)
    for h in range(HEADS):
        cols = slice(h * DH, (h + 1) * DH)
        d = jnp.sum(out_ref[:, cols].astype(F32) * g_ref[:, cols].astype(F32), 1, keepdims=True)
        table = jnp.where(lane == h, d, table)
    delta_ref[...] = table.T[:HEADS]


def grad_kernel(
    coef, scale, valid_ref, q_ref, g_ref, kv_ref, limit_ref, stat_ref,
    qgrad_ref, kvgrad_ref, acc_ref,
):
    step = pl.program_id(0)
    plen = kv_ref.shape[0] - DH
    valid = valid_ref[0]
    tops = stat_ref[:, :HEADS]
    top_all = jnp.max(tops, 0)
    share = stat_ref[:, HEADS : 2 * HEADS] * jnp.exp2(tops - top_all)
    inv_all = 1.0 / jnp.sum(share, 0)
    delta_all = jnp.sum(share * stat_ref[:, 2 * HEADS :], 0) * inv_all

    @pl.when(step == 0)
    def _():
        acc_ref[...] = jnp.zeros_like(acc_ref)

    chunk = 256
    bounds = [(i, min(chunk, plen - i)) for i in range(0, plen, chunk)] + [(plen, DH)]
    limit = jnp.concatenate([limit_ref[0:1]] * HALF, 1)
    for base in (0, HALF):
        q = stack_heads(q_ref, base)
        g = stack_heads(g_ref, base)
        line = lambda t: jnp.concatenate([t[base + h : base + h + 1] for h in range(HALF)], 1)
        top, inv, delta = line(top_all), line(inv_all), line(delta_all)
        dq = jnp.zeros((HALF * SLOTS, DH), F32)
        for start, size in bounds:
            rows = pl.ds(start, size)
            k = kv_ref[rows, :DH]
            v = kv_ref[rows, DH:]
            s = lax.dot_general(k, q, NT, preferred_element_type=F32)
            place = lax.broadcasted_iota(jnp.int32, (size, HALF * SLOTS), 0)
            seen = place < valid - start if start < plen else place <= limit
            p = jnp.exp2(jnp.where(seen, s * coef - top, NEG)) * inv
            dp = lax.dot_general(v, g, NT, preferred_element_type=F32)
            ds = (p * (dp - delta) * scale).astype(BF16)
            acc_ref[rows, :DH] += jnp.dot(ds, q, preferred_element_type=F32)
            acc_ref[rows, DH:] += jnp.dot(p.astype(BF16), g, preferred_element_type=F32)
            dq = dq + lax.dot_general(ds, k, TN, preferred_element_type=F32)
        for h in range(HALF):
            qgrad_ref[:, (base + h) * DH : (base + h + 1) * DH] = dq[
                h * SLOTS : (h + 1) * SLOTS
            ].astype(BF16)

    @pl.when(step == pl.num_programs(0) - 1)
    def _():
        kvgrad_ref[...] = acc_ref[...].astype(BF16)


def weight_kernel(core_ref, order_ref, grad_ref, prompt_ref, resp_ref, keep_ref, give_ref, buf, sems):
    wide = buf.shape[1] // PAIRS
    half = wide // 2
    copies = fetch(prompt_ref, resp_ref, buf, sems, order_ref, wide)
    swapped = core_ref[0] == 1
    grad = grad_ref[...].T
    for i in range(PAIRS):
        for copy in copies[i]:
            copy.wait()
        t = jnp.dot(grad, buf[:, i * wide : (i + 1) * wide], preferred_element_type=F32).T
        keep_ref[i // 2, i % 2] = jnp.where(swapped, t[half:], t[:half])
        give_ref[i // 2, i % 2] = jnp.where(swapped, t[:half], t[half:]).astype(BF16)


def weigh_kernel(parts_ref, share_ref, out_ref):
    share = share_ref[...].T
    for h in range(HEADS):
        cols = slice(h * DH, (h + 1) * DH)
        total = jnp.zeros((out_ref.shape[0], DH), F32)
        for j in range(N_SEQ):
            column = j * HEADS + h
            total = total + parts_ref[j, :, cols].astype(F32) * share[:, column : column + 1]
        out_ref[:, cols] = total.astype(BF16)


def spread(block, axes, count):
    copies = jnp.broadcast_to(block[None], (count,) + block.shape)
    return lax.all_to_all(copies, axes, 0, 0, tiled=True)


def per_device(
    prompt_hidden, resp_hidden, queries, grad_out, kv_weight, prompt_lengths, response_lengths
):
    rank = lax.axis_index(SEQ)
    core = lax.axis_index("c")
    core_id = core.astype(jnp.int32).reshape(1)
    slots = resp_hidden.shape[1]
    plen = prompt_hidden.shape[1]
    model = prompt_hidden.shape[2]
    width = queries.shape[2]
    scale = DH ** (-0.5)
    coef = scale * LOG2E
    prompt_rows = prompt_hidden[0]
    resp_rows = resp_hidden[0]
    keys = plen + slots
    smem = pl.BlockSpec(memory_space=pltpu.SMEM)

    q_all = spread(queries[0], SEQ, N_SEQ).reshape(N_SEQ * slots, width)
    g_all = spread(grad_out[0], SEQ, N_SEQ).reshape(N_SEQ * slots, width)

    shard = kv_weight.shape[0]
    x, zh, y, zl = (lax.axis_index(axis) for axis in ("x", "zh", "y", "zl"))
    order = jnp.stack(
        [((x + i // 2) % 4) * 2 + (zh + i % 2) % 2 for i in range(PAIRS)]
    ).astype(jnp.int32)
    other = lax.ppermute(kv_weight, "zl", SWAP)
    pair = jnp.where(
        zl == 0, jnp.concatenate([kv_weight, other], 0), jnp.concatenate([other, kv_weight], 0)
    )
    run = [pair] + [lax.ppermute(pair, "y", shift(k)) for k in range(1, 4)]
    block = lax.dynamic_slice_in_dim(
        jnp.concatenate(run + run, 0), ((4 - y) % 4) * 2 * shard, 8 * shard, 0
    )
    both = jnp.stack([block, lax.ppermute(block, "zh", SWAP)], 0)
    nears = [both] + [lax.ppermute(both, "x", shift(k)) for k in range(1, 4)]
    fars = [lax.ppermute(piece, "c", SWAP) for piece in nears]
    wide = model // PAIRS
    vmem = pl.BlockSpec(memory_space=pltpu.VMEM)
    anywhere = pl.BlockSpec(memory_space=pl.ANY)
    kv = pl.pallas_call(
        project_kernel,
        in_specs=[smem, smem] + [vmem] * 8 + [anywhere] * 2,
        out_specs=vmem,
        out_shape=jax.ShapeDtypeStruct((keys, 2 * DH), BF16),
        scratch_shapes=[
            pltpu.VMEM((keys, model), BF16),
            pltpu.VMEM((model, 2 * DH), BF16),
            pltpu.VMEM((keys, 2 * DH), F32),
            pltpu.SemaphoreType.DMA((PAIRS, 2)),
        ],
        compiler_params=params(32),
        cost_estimate=pl.CostEstimate(
            flops=2 * keys * model * 2 * DH, bytes_accessed=2 * keys * model, transcendentals=0
        ),
        name="project",
    )(core_id, order, *nears, *fars, prompt_rows, resp_rows)

    lengths = response_lengths[0]
    live_all = slots * N_SEQ * 5 // 8
    ends = jnp.cumsum(lengths)
    packed = jnp.arange(live_all)
    past = packed[:, None] >= ends[None, :]
    source = packed + jnp.sum(jnp.where(past, slots - lengths[None, :], 0), 1)
    pick = (source[:, None] == jnp.arange(N_SEQ * slots)[None, :]).astype(BF16)
    offset = source - rank * slots
    limit = jnp.where((offset >= 0) & (offset < slots), offset, -1).astype(jnp.int32)
    limit_cols = jnp.broadcast_to(limit[:, None], (live_all, DH))
    limit_rows = jnp.broadcast_to(limit[None, :], (8, live_all))
    valid = (prompt_lengths - plen * rank).astype(jnp.int32)

    q = jnp.dot(pick, q_all, preferred_element_type=F32).astype(BF16)
    steps = live_all // SLOTS
    rows = live_all * HEADS
    row_block = pl.BlockSpec((SLOTS, width), lambda i: (i, 0))
    whole = pl.BlockSpec((keys, 2 * DH), lambda i: (0, 0))
    out, stat = pl.pallas_call(
        functools.partial(stats_kernel, coef),
        grid=(steps,),
        in_specs=[smem, row_block, whole, pl.BlockSpec((SLOTS, DH), lambda i: (i, 0))],
        out_specs=[row_block, pl.BlockSpec((2 * HEADS, SLOTS), lambda i: (0, i))],
        out_shape=[
            jax.ShapeDtypeStruct((live_all, width), BF16),
            jax.ShapeDtypeStruct((2 * HEADS, live_all), F32),
        ],
        compiler_params=params(24),
        cost_estimate=pl.CostEstimate(
            flops=4 * rows * keys * DH, bytes_accessed=4 << 20, transcendentals=rows * keys
        ),
        name="attend_stats",
    )(valid, q, kv, limit_cols)

    g = jnp.dot(pick, g_all, preferred_element_type=F32).astype(BF16)
    delta = pl.pallas_call(
        delta_kernel,
        grid=(steps,),
        in_specs=[row_block, row_block],
        out_specs=pl.BlockSpec((HEADS, SLOTS), lambda i: (0, i)),
        out_shape=jax.ShapeDtypeStruct((HEADS, live_all), F32),
        compiler_params=params(24),
        name="partial_delta",
    )(out, g)
    stats = spread(jnp.concatenate([stat, delta], 0), SEQ, N_SEQ)

    parts = lax.dot_general(pick, out, TN, preferred_element_type=F32).astype(BF16)
    parts = lax.all_to_all(parts.reshape(N_SEQ, slots, width), SEQ, 0, 0, tiled=True)

    qgrad, kvgrad = pl.pallas_call(
        functools.partial(grad_kernel, coef, scale),
        grid=(steps,),
        in_specs=[
            smem, row_block, row_block, whole,
            pl.BlockSpec((8, SLOTS), lambda i: (0, i)),
            pl.BlockSpec((N_SEQ, 3 * HEADS, SLOTS), lambda i: (0, 0, i)),
        ],
        out_specs=[row_block, whole],
        out_shape=[
            jax.ShapeDtypeStruct((live_all, width), BF16),
            jax.ShapeDtypeStruct((keys, 2 * DH), BF16),
        ],
        scratch_shapes=[pltpu.VMEM((keys, 2 * DH), F32)],
        compiler_params=params(24),
        cost_estimate=pl.CostEstimate(
            flops=10 * rows * keys * DH, bytes_accessed=8 << 20, transcendentals=rows * keys
        ),
        name="attend_grads",
    )(valid, q, g, kv, limit_rows, stats)

    back = lax.dot_general(pick, qgrad, TN, preferred_element_type=F32).astype(BF16)
    back = lax.all_to_all(back.reshape(N_SEQ, slots, width), SEQ, 0, 0, tiled=True)
    query_grad = jnp.sum(back.astype(F32), 0).astype(BF16)

    keep, give = pl.pallas_call(
        weight_kernel,
        in_specs=[smem, smem, vmem, anywhere, anywhere],
        out_specs=[vmem, vmem],
        out_shape=[
            jax.ShapeDtypeStruct((4, 2, 8 * shard, 2 * DH), F32),
            jax.ShapeDtypeStruct((4, 2, 8 * shard, 2 * DH), BF16),
        ],
        scratch_shapes=[
            pltpu.VMEM((keys, model), BF16),
            pltpu.SemaphoreType.DMA((PAIRS, 2)),
        ],
        compiler_params=params(32),
        cost_estimate=pl.CostEstimate(
            flops=2 * keys * model * 2 * DH, bytes_accessed=2 * keys * model, transcendentals=0
        ),
        name="weight_grad",
    )(core_id, order, kvgrad, prompt_rows, resp_rows)
    got = [lax.ppermute(give[k], "c", SWAP) for k in range(4)]
    line = keep[0] + got[0].astype(F32)
    for k in range(1, 4):
        piece = (keep[k] + got[k].astype(F32)).astype(BF16)
        line = line + lax.ppermute(piece, "x", shift(-k)).astype(F32)
    line = line.astype(BF16)
    line = jnp.where(zh == 0, line, line[::-1]).reshape(16, shard, 2 * DH)
    shares = lax.all_to_all(line, ("zh", "y", "zl"), 0, 0, tiled=True)
    weight_grad = jnp.sum(shares.astype(F32), 0)

    top = jnp.max(stats[:, :HEADS], 0)
    share = stats[:, HEADS : 2 * HEADS] * jnp.exp2(stats[:, :HEADS] - top)
    share = share / jnp.sum(share, 0)
    my_len = jnp.sum(jnp.where(jnp.arange(N_SEQ) == rank, lengths, 0))
    my_start = jnp.sum(jnp.where(jnp.arange(N_SEQ) == rank, ends, 0)) - my_len
    share = lax.dynamic_slice_in_dim(
        jnp.pad(share, ((0, 0), (0, 0), (0, slots))), my_start, slots, 2
    )
    share = jnp.where(jnp.arange(slots) < my_len, share, 0.0).reshape(N_SEQ * HEADS, slots)
    attended = pl.pallas_call(
        weigh_kernel,
        in_specs=[vmem, vmem],
        out_specs=vmem,
        out_shape=jax.ShapeDtypeStruct((slots, width), BF16),
        compiler_params=params(16),
        name="weigh",
    )(parts, share)
    return attended[None], query_grad[None], kvgrad[None, :plen], weight_grad


def solution(mesh):
    fine = Mesh(mesh.devices.reshape(4, 2, 2, 4, 2), AXES)
    return jax.shard_map(
        per_device,
        mesh=fine,
        in_specs=(
            P(GRP, SEQ, None),
            P(GRP, SEQ, None),
            P(GRP, SEQ, None),
            P(GRP, SEQ, None),
            P(AXES, None),
            P(GRP),
            P(GRP, None),
        ),
        out_specs=(
            P(GRP, SEQ, None),
            P(GRP, SEQ, None),
            P(GRP, SEQ, None),
            P(AXES, None),
        ),
        check_vma=False,
    )
```

```python
import functools

import jax
import jax.numpy as jnp
from jax import lax
from jax.experimental import pallas as pl
from jax.experimental.pallas import tpu as pltpu
from jax.sharding import Mesh
from jax.sharding import PartitionSpec as P

AXES = ("x", "zh", "c", "y", "zl")
GRP = ("x", "zh", "c")
SEQ = ("y", "zl")
PLANE = ("zh", "y", "zl")
N_SEQ = 8
NX = 4
NY = 4
HEADS = 8
HALF = 4
DH = 128
SLOTS = 128
ROWS = HALF * SLOTS
NEG = -1e30
LOG2E = 1.4426950408889634
NT = (((1,), (1,)), ((), ()))
TN = (((0,), (0,)), ((), ()))
F32 = jnp.float32
BF16 = jnp.bfloat16
SWAP = [(0, 1), (1, 0)]


def params(mib):
    return pltpu.CompilerParams(vmem_limit_bytes=mib << 20)


def shift(k):
    return [((i + k) % 4, i) for i in range(4)]


def stack_heads(ref):
    return jnp.concatenate([ref[:, h * DH : (h + 1) * DH] for h in range(HALF)], 0)


def project_kernel(place_ref, *refs):
    nears, fars = refs[:NX], refs[NX : 2 * NX]
    prompt_ref, resp_ref, kv_ref, weight, acc = refs[2 * NX :]
    plen = prompt_ref.shape[0]
    wide = weight.shape[0] // NX
    part = wide // 4
    x, core = place_ref[0], place_ref[1]
    for k in range(NX):
        for z in range(2):
            base = k * wide + z * 2 * part
            weight[pl.ds(pl.multiple_of(base + core * part, part), part)] = nears[k][z]
            weight[pl.ds(pl.multiple_of(base + (1 - core) * part, part), part)] = fars[k][z]
    for k in range(NX):
        cols = pl.ds(pl.multiple_of(lax.rem(x + k, NX) * wide, DH), wide)
        w = weight[k * wide : (k + 1) * wide]
        a = jnp.dot(prompt_ref[:, cols], w, preferred_element_type=F32)
        b = jnp.dot(resp_ref[:, cols], w, preferred_element_type=F32)
        if k == 0:
            acc[:plen], acc[plen:] = a, b
        elif k < NX - 1:
            acc[:plen] += a
            acc[plen:] += b
        else:
            kv_ref[:plen] = (acc[:plen] + a).astype(BF16)
            kv_ref[plen:] = (acc[plen:] + b).astype(BF16)


def first_pass(coef, carried, last, valid_ref, limit_ref, q_ref, kv_ref, *refs):
    refs = list(refs)
    if carried:
        prev_out_ref, prev_stat_ref = refs.pop(0), refs.pop(0)
    if last:
        g_ref = refs.pop(0)
    out_ref, stat_ref, bias, values = refs
    plen = kv_ref.shape[0] - DH

    @pl.when(pl.program_id(0) == 0)
    def _():
        place = lax.broadcasted_iota(jnp.int32, (plen, DH), 0)
        bias[...] = jnp.where(place < valid_ref[0], 0.0, NEG)
        values[...] = kv_ref[:, DH:].T

    causal = jnp.where(
        lax.broadcasted_iota(jnp.int32, (DH, SLOTS), 0) <= limit_ref[0:1], 0.0, NEG
    )
    keys = kv_ref[:, :DH]
    bias_all = jnp.concatenate([bias[...], causal], 0)
    for h in range(HALF):
        lanes = slice(h * SLOTS, (h + 1) * SLOTS)
        cols = slice(h * DH, (h + 1) * DH)
        s = lax.dot_general(keys, q_ref[:, cols], NT, preferred_element_type=F32)
        s = s * coef + bias_all
        top = jnp.max(s, 0, keepdims=True)
        if carried:
            before = prev_stat_ref[0:1, lanes]
            top = jnp.maximum(top, before)
        p = jnp.exp2(s - top)
        total = jnp.sum(p, 0, keepdims=True)
        o = jnp.dot(values[...], p.astype(BF16), preferred_element_type=F32)
        if carried:
            alpha = jnp.exp2(before - top)
            total = total + prev_stat_ref[1:2, lanes] * alpha
            o = o + prev_out_ref[:, lanes] * alpha
        if last:
            o = o / total
            stat_ref[2:3, lanes] = jnp.sum(o * g_ref[:, cols].astype(F32).T, 0, keepdims=True)
        out_ref[:, lanes] = o
        stat_ref[0:1, lanes] = top
        stat_ref[1:2, lanes] = total


def second_pass(coef, scale, last, valid_ref, limit_ref, q_ref, g_ref, kv_ref, stat_ref, *refs):
    if last:
        own_stat_ref, out_ref, prev_ref, back_ref, kvgrad_ref, acc, bias = refs
    else:
        back_ref, kvgrad_ref, acc, bias = refs
    step = pl.program_id(0)
    plen = kv_ref.shape[0] - DH
    tops = stat_ref[:, 0:1]
    top = jnp.max(tops, 0)
    share = stat_ref[:, 1:2] * jnp.exp2(tops - top)
    inv = 1.0 / jnp.sum(share, 0)
    delta = jnp.sum(share * stat_ref[:, 2:3], 0) * inv
    row = lax.broadcasted_iota(jnp.int32, (8, ROWS), 0)
    columns = jnp.where(row == 0, top, jnp.where(row == 1, inv, delta))
    columns = jnp.concatenate([columns] * 16, 0).T

    @pl.when(step == 0)
    def _():
        acc[...] = jnp.zeros_like(acc)
        place = lax.broadcasted_iota(jnp.int32, (8, plen), 1)
        bias[...] = jnp.where(place < valid_ref[0], 0.0, NEG)

    if last:
        weight = own_stat_ref[1:2] * jnp.exp2(own_stat_ref[0:1] - top) * inv
        att = (out_ref[...] * weight).T
        for h in range(HALF):
            back_ref[:, h * DH : (h + 1) * DH] = att[h * SLOTS : (h + 1) * SLOTS].astype(BF16)

    c_top, c_inv, c_delta = columns[:, 0:1], columns[:, 1:2], columns[:, 2:3]
    q = stack_heads(q_ref)
    g = stack_heads(g_ref)
    qt = q.T
    gt = g.T
    lane = lax.broadcasted_iota(jnp.int32, (SLOTS, DH), 1)
    causal = jnp.concatenate([jnp.where(lane <= limit_ref[...], 0.0, NEG)] * HALF, 0)
    dq = jnp.zeros((ROWS, DH), F32)
    chunk = 256
    for start in list(range(0, plen, chunk)) + [plen]:
        size = chunk if start < plen else DH
        keys = slice(start, start + size)
        k = kv_ref[keys, :DH]
        v = kv_ref[keys, DH:]
        s = lax.dot_general(q, k, NT, preferred_element_type=F32)
        hidden = bias[0:1, keys] if start < plen else causal
        p = jnp.exp2(s * coef - c_top + hidden) * c_inv
        dp = lax.dot_general(g, v, NT, preferred_element_type=F32)
        ds = (p * (dp - c_delta) * scale).astype(BF16)
        acc[:DH, keys] += jnp.dot(qt, ds, preferred_element_type=F32)
        acc[DH:, keys] += jnp.dot(gt, p.astype(BF16), preferred_element_type=F32)
        dq = dq + jnp.dot(ds, k, preferred_element_type=F32)
    for h in range(HALF):
        rows = slice(h * SLOTS, (h + 1) * SLOTS)
        cols = slice(h * DH, (h + 1) * DH)
        if last:
            back_ref[:, ROWS + h * DH : ROWS + (h + 1) * DH] = (
                dq[rows] + prev_ref[:, cols]
            ).astype(BF16)
        else:
            back_ref[:, cols] = dq[rows]

    @pl.when(step == pl.num_programs(0) - 1)
    def _():
        kvgrad_ref[...] = acc[...].T.astype(kvgrad_ref.dtype)


def weight_kernel(place_ref, own_ref, got_ref, prompt_ref, resp_ref, kvgrad_ref, keep_ref, give_ref, whole):
    plen = prompt_ref.shape[0]
    wide = whole.shape[0]
    part = wide // 4
    x, core = place_ref[0], place_ref[1]
    grad = (own_ref[...] + got_ref[...].astype(F32)).astype(BF16)
    kvgrad_ref[...] = grad[:plen]
    for k in range(NX):
        cols = pl.ds(pl.multiple_of(lax.rem(x + k, NX) * wide, DH), wide)
        t = lax.dot_general(prompt_ref[:, cols], grad[:plen], TN, preferred_element_type=F32)
        whole[...] = t + lax.dot_general(
            resp_ref[:, cols], grad[plen:], TN, preferred_element_type=F32
        )
        for z in range(2):
            base = z * 2 * part
            mine = pl.ds(pl.multiple_of(base + core * part, part), part)
            theirs = pl.ds(pl.multiple_of(base + (1 - core) * part, part), part)
            keep_ref[k, z] = whole[mine]
            give_ref[k, z] = whole[theirs].astype(BF16)


def spread(block, axes, count):
    copies = jnp.broadcast_to(block[None], (count,) + block.shape)
    return lax.all_to_all(copies, axes, 0, 0, tiled=True)


def per_device(
    prompt_hidden, resp_hidden, queries, grad_out, kv_weight, prompt_lengths, response_lengths
):
    rank = lax.axis_index(SEQ)
    x = lax.axis_index("x")
    place = jnp.stack([x, lax.axis_index("c")]).astype(jnp.int32)
    slots = resp_hidden.shape[1]
    plen = prompt_hidden.shape[1]
    model = prompt_hidden.shape[2]
    width = queries.shape[2]
    half = width // 2
    scale = DH ** (-0.5)
    coef = scale * LOG2E
    prompt_rows = prompt_hidden[0]
    resp_rows = resp_hidden[0]
    keys = plen + slots
    shard = kv_weight.shape[0]
    smem = pl.BlockSpec(memory_space=pltpu.SMEM)
    vmem = pl.BlockSpec(memory_space=pltpu.VMEM)

    block = spread(kv_weight, PLANE, 16).reshape(2, 8 * shard, 2 * DH)
    q_own, g_own, block = lax.optimization_barrier((queries[0], grad_out[0], block))
    nears = [block] + [lax.ppermute(block, "x", shift(k)) for k in range(1, NX)]
    fars = [lax.ppermute(piece, "c", SWAP) for piece in nears]

    def halves(t):
        t = t.reshape(slots, 2, half).transpose(1, 0, 2)[None]
        t = jnp.broadcast_to(t, (NY, 2, slots, half)).reshape(N_SEQ, slots, half)
        return lax.all_to_all(t, SEQ, 0, 0, tiled=True).reshape(N_SEQ * slots, half)

    q_all = halves(q_own)
    g_own, q_all = lax.optimization_barrier((g_own, q_all))
    g_all = halves(g_own)

    kv = pl.pallas_call(
        project_kernel,
        in_specs=[smem] + [vmem] * (2 * NX + 2),
        out_specs=vmem,
        out_shape=jax.ShapeDtypeStruct((keys, 2 * DH), BF16),
        scratch_shapes=[
            pltpu.VMEM((model, 2 * DH), BF16),
            pltpu.VMEM((keys, 2 * DH), F32),
        ],
        compiler_params=params(32),
        cost_estimate=pl.CostEstimate(
            flops=2 * keys * model * 2 * DH, bytes_accessed=2 * keys * model, transcendentals=0
        ),
        name="project",
    )(place, *nears, *fars, prompt_rows, resp_rows)
    kv_other = lax.ppermute(kv, "zl", SWAP)

    lengths = response_lengths[0]
    live_all = slots * N_SEQ * 5 // 8
    ends = jnp.cumsum(lengths)
    packed = jnp.arange(live_all)
    past = packed[:, None] >= ends[None, :]
    source = packed + jnp.sum(jnp.where(past, slots - lengths[None, :], 0), 1)
    pick = (source[:, None] == jnp.arange(N_SEQ * slots)[None, :]).astype(BF16)

    def masks(owner):
        offset = source - owner * slots
        limit = jnp.where((offset >= 0) & (offset < slots), offset, -1).astype(jnp.int32)
        return (
            (prompt_lengths - plen * owner).astype(jnp.int32),
            jnp.broadcast_to(limit[None, :], (8, live_all)),
            jnp.broadcast_to(limit[:, None], (live_all, DH)),
        )

    valid, limit_rows, limit_cols = masks(rank)
    valid_other, limit_rows_other, limit_cols_other = masks(rank ^ 1)

    steps = live_all // SLOTS
    rows = live_all * HALF
    whole = pl.BlockSpec((keys, 2 * DH), lambda i: (0, 0))
    slot_block = pl.BlockSpec((SLOTS, half), lambda i: (i, 0))
    lane_block = pl.BlockSpec((DH, ROWS), lambda i: (0, i))
    limit_lane = pl.BlockSpec((8, SLOTS), lambda i: (0, i))
    limit_slot = pl.BlockSpec((SLOTS, DH), lambda i: (i, 0))
    stat_block = pl.BlockSpec((3, ROWS), lambda i: (0, i))

    def forward(valid, limit, q, kv, state, g):
        carried, last = state is not None, g is not None
        return pl.pallas_call(
            functools.partial(first_pass, coef, carried, last),
            grid=(steps,),
            in_specs=[smem, limit_lane, slot_block, whole]
            + [lane_block, stat_block] * carried
            + [slot_block] * last,
            out_specs=[lane_block, stat_block],
            out_shape=[
                jax.ShapeDtypeStruct((DH, rows), F32),
                jax.ShapeDtypeStruct((3, rows), F32),
            ],
            scratch_shapes=[pltpu.VMEM((plen, DH), F32), pltpu.VMEM((DH, keys), BF16)],
            compiler_params=params(24),
            cost_estimate=pl.CostEstimate(
                flops=4 * rows * keys * DH, bytes_accessed=4 << 20, transcendentals=rows * keys
            ),
            name="attend_more" if carried else "attend_own",
        )(valid, limit, q, kv, *(state or ()), *([g] if last else []))

    q = jnp.dot(pick, q_all, preferred_element_type=F32).astype(BF16)
    state = forward(valid, limit_rows, q, kv, None, None)
    g = jnp.dot(pick, g_all, preferred_element_type=F32).astype(BF16)
    out, stat = forward(valid_other, limit_rows_other, q, kv_other, state, g)
    stats = spread(stat, "y", NY)

    def backward(valid, limit, kv, more):
        last = bool(more)
        return pl.pallas_call(
            functools.partial(second_pass, coef, scale, last),
            grid=(steps,),
            in_specs=[
                smem, limit_slot, slot_block, slot_block, whole,
                pl.BlockSpec((NY, 3, ROWS), lambda i: (0, 0, i)),
            ] + [stat_block, lane_block, slot_block] * last,
            out_specs=[
                pl.BlockSpec((SLOTS, 2 * half), lambda i: (i, 0)) if last else slot_block,
                whole,
            ],
            out_shape=[
                jax.ShapeDtypeStruct((live_all, 2 * half), BF16)
                if last
                else jax.ShapeDtypeStruct((live_all, half), F32),
                jax.ShapeDtypeStruct((keys, 2 * DH), F32 if last else BF16),
            ],
            scratch_shapes=[pltpu.VMEM((2 * DH, keys), F32), pltpu.VMEM((8, plen), F32)],
            compiler_params=params(24),
            cost_estimate=pl.CostEstimate(
                flops=10 * rows * keys * DH, bytes_accessed=8 << 20, transcendentals=rows * keys
            ),
            name="grads_own" if last else "grads_other",
        )(valid, limit, q, g, kv, stats, *more)

    qgrad_part, kvgrad_other = backward(valid_other, limit_cols_other, kv_other, ())
    kvgrad_got = lax.ppermute(kvgrad_other, "zl", SWAP)
    back, kvgrad_own = backward(valid, limit_cols, kv, (stat, out, qgrad_part))

    back = lax.dot_general(pick, back, TN, preferred_element_type=F32).astype(BF16)
    back, kvgrad_own = lax.optimization_barrier((back, kvgrad_own))
    back = lax.all_to_all(back.reshape(N_SEQ, slots, 2 * half), SEQ, 0, 0, tiled=True)

    prompt_grad, keep, give = pl.pallas_call(
        weight_kernel,
        in_specs=[smem] + [vmem] * 4,
        out_specs=[vmem] * 3,
        out_shape=[
            jax.ShapeDtypeStruct((plen, 2 * DH), BF16),
            jax.ShapeDtypeStruct((NX, 2, 8 * shard, 2 * DH), F32),
            jax.ShapeDtypeStruct((NX, 2, 8 * shard, 2 * DH), BF16),
        ],
        scratch_shapes=[pltpu.VMEM((model // NX, 2 * DH), F32)],
        compiler_params=params(32),
        cost_estimate=pl.CostEstimate(
            flops=2 * keys * model * 2 * DH, bytes_accessed=2 * keys * model, transcendentals=0
        ),
        name="weight_grad",
    )(place, kvgrad_own, kvgrad_got, prompt_rows, resp_rows)
    got = [lax.ppermute(give[k], "c", SWAP) for k in range(NX)]
    line = keep[0] + got[0].astype(F32)
    for k in range(1, NX):
        piece = (keep[k] + got[k].astype(F32)).astype(BF16)
        line = line + lax.ppermute(piece, "x", shift(-k)).astype(F32)
    line = line.astype(BF16).reshape(16, shard, 2 * DH)
    line, back = lax.optimization_barrier((line, back))
    shares = lax.all_to_all(line, PLANE, 0, 0, tiled=True)
    weight_grad = jnp.sum(shares.astype(F32), 0)

    back = jnp.sum(back.reshape(NY, 2, slots, 2 * half).astype(F32), 0).astype(BF16)
    attended = jnp.concatenate([back[0, :, :half], back[1, :, :half]], 1)
    query_grad = jnp.concatenate([back[0, :, half:], back[1, :, half:]], 1)
    return attended[None], query_grad[None], prompt_grad[None], weight_grad


def solution(mesh):
    fine = Mesh(mesh.devices.reshape(4, 2, 2, 4, 2), AXES)
    return jax.shard_map(
        per_device,
        mesh=fine,
        in_specs=(
            P(GRP, SEQ, None),
            P(GRP, SEQ, None),
            P(GRP, SEQ, None),
            P(GRP, SEQ, None),
            P(AXES, None),
            P(GRP),
            P(GRP, None),
        ),
        out_specs=(
            P(GRP, SEQ, None),
            P(GRP, SEQ, None),
            P(GRP, SEQ, None),
            P(AXES, None),
        ),
        check_vma=False,
    )
```

```python
import functools

import jax
import jax.numpy as jnp
from jax import lax
from jax.experimental import pallas as pl
from jax.experimental.pallas import tpu as pltpu
from jax.sharding import Mesh
from jax.sharding import PartitionSpec as P

AXES = ("x", "zh", "c", "y", "zl")
GRP = ("x", "zh", "c")
SEQ = ("y", "zl")
N_SEQ = 8
NX = 4
NY = 4
HEADS = 8
HALF = 4
DH = 128
SLOTS = 128
ROWS = HALF * SLOTS
NEG = -1e30
LOG2E = 1.4426950408889634
NT = (((1,), (1,)), ((), ()))
TN = (((0,), (0,)), ((), ()))
F32 = jnp.float32
BF16 = jnp.bfloat16
SWAP = [(0, 1), (1, 0)]


def params(mib):
    return pltpu.CompilerParams(vmem_limit_bytes=mib << 20)


def shift(k):
    return [((i + k) % 4, i) for i in range(4)]


def stack_heads(ref):
    return jnp.concatenate([ref[:, h * DH : (h + 1) * DH] for h in range(HALF)], 0)


def fetch(steps, x, prompt_ref, resp_ref, buf, sems):
    plen = prompt_ref.shape[0]
    wide = prompt_ref.shape[1] // NX
    half = wide // 2
    copies = []
    for n, k in enumerate(steps):
        for part in range(2):
            there = pl.ds(pl.multiple_of(lax.rem(x + k, NX) * wide + part * half, DH), half)
            here = pl.ds(n * wide + part * half, half)
            sem = sems.at[n * 2 + part]
            pair = (
                pltpu.make_async_copy(prompt_ref.at[:, there], buf.at[:plen, here], sem.at[0]),
                pltpu.make_async_copy(resp_ref.at[:, there], buf.at[plen:, here], sem.at[1]),
            )
            for copy in pair:
                copy.start()
            copies.append(pair)
    return copies


def project_kernel(steps, first, last, place_ref, prompt_ref, resp_ref, *refs):
    refs = list(refs)
    nears = [refs.pop(0) for _ in steps]
    fars = [refs.pop(0) for _ in steps]
    prev_ref = None if first else refs.pop(0)
    kv_ref, buf, weight, sems = refs
    wide = prompt_ref.shape[1] // NX
    half = wide // 2
    part = wide // 4
    x, core = place_ref[0], place_ref[1]
    copies = fetch(steps, x, prompt_ref, resp_ref, buf, sems)
    for n in range(len(steps)):
        for z in range(2):
            base = n * wide + z * half
            weight[pl.ds(pl.multiple_of(base + core * part, part), part)] = nears[n][z]
            weight[pl.ds(pl.multiple_of(base + (1 - core) * part, part), part)] = fars[n][z]
    total = None
    for n, pair in enumerate(copies):
        for copy in pair:
            copy.wait()
        cols = slice(n * half, (n + 1) * half)
        t = jnp.dot(buf[:, cols], weight[cols], preferred_element_type=F32)
        total = t if total is None else total + t
    if not first:
        total = total + prev_ref[...]
    kv_ref[...] = total.astype(kv_ref.dtype)


def first_pass(coef, carried, last, valid_ref, limit_ref, q_ref, kv_ref, *refs):
    refs = list(refs)
    if carried:
        prev_out_ref, prev_stat_ref = refs.pop(0), refs.pop(0)
    if last:
        g_ref = refs.pop(0)
    out_ref, stat_ref, bias, values = refs
    plen = kv_ref.shape[0] - DH

    @pl.when(pl.program_id(0) == 0)
    def _():
        place = lax.broadcasted_iota(jnp.int32, (plen, DH), 0)
        bias[...] = jnp.where(place < valid_ref[0], 0.0, NEG)
        values[...] = kv_ref[:, DH:].T

    causal = jnp.where(
        lax.broadcasted_iota(jnp.int32, (DH, SLOTS), 0) <= limit_ref[0:1], 0.0, NEG
    )
    keys = kv_ref[:, :DH]
    bias_all = jnp.concatenate([bias[...], causal], 0)
    for h in range(HALF):
        lanes = slice(h * SLOTS, (h + 1) * SLOTS)
        cols = slice(h * DH, (h + 1) * DH)
        s = lax.dot_general(keys, q_ref[:, cols], NT, preferred_element_type=F32)
        s = s * coef + bias_all
        top = jnp.max(s, 0, keepdims=True)
        if carried:
            before = prev_stat_ref[0:1, lanes]
            top = jnp.maximum(top, before)
        p = jnp.exp2(s - top)
        total = jnp.sum(p, 0, keepdims=True)
        o = jnp.dot(values[...], p.astype(BF16), preferred_element_type=F32)
        if carried:
            alpha = jnp.exp2(before - top)
            total = total + prev_stat_ref[1:2, lanes] * alpha
            o = o + prev_out_ref[:, lanes] * alpha
        if last:
            o = o / total
            stat_ref[2:3, lanes] = jnp.sum(o * g_ref[:, cols].astype(F32).T, 0, keepdims=True)
        out_ref[:, lanes] = o
        stat_ref[0:1, lanes] = top
        stat_ref[1:2, lanes] = total


def second_pass(coef, scale, last, valid_ref, limit_ref, q_ref, g_ref, kv_ref, *refs):
    stat_refs, refs = refs[:NY], refs[NY:]
    if last:
        out_ref, prev_ref, back_ref, kvgrad_ref, acc, bias = refs
    else:
        back_ref, kvgrad_ref, acc, bias = refs
    step = pl.program_id(0)
    plen = kv_ref.shape[0] - DH
    tops = [ref[0:1] for ref in stat_refs]
    top = functools.reduce(jnp.maximum, tops)
    share = [ref[1:2] * jnp.exp2(t - top) for ref, t in zip(stat_refs, tops)]
    inv = 1.0 / sum(share)
    delta = sum(w * ref[2:3] for w, ref in zip(share, stat_refs)) * inv
    row = lax.broadcasted_iota(jnp.int32, (8, ROWS), 0)
    columns = jnp.where(row == 0, top, jnp.where(row == 1, inv, delta))
    columns = jnp.concatenate([columns] * 16, 0).T

    @pl.when(step == 0)
    def _():
        acc[...] = jnp.zeros_like(acc)
        place = lax.broadcasted_iota(jnp.int32, (8, plen), 1)
        bias[...] = jnp.where(place < valid_ref[0], 0.0, NEG)

    if last:
        weight = share[0] * inv
        att = (out_ref[...] * weight).T
        for h in range(HALF):
            back_ref[:, h * DH : (h + 1) * DH] = att[h * SLOTS : (h + 1) * SLOTS].astype(BF16)

    c_top, c_inv, c_delta = columns[:, 0:1], columns[:, 1:2], columns[:, 2:3]
    q = stack_heads(q_ref)
    g = stack_heads(g_ref)
    qt = q.T
    gt = g.T
    lane = lax.broadcasted_iota(jnp.int32, (SLOTS, DH), 1)
    causal = jnp.concatenate([jnp.where(lane <= limit_ref[...], 0.0, NEG)] * HALF, 0)
    dq = jnp.zeros((ROWS, DH), F32)
    chunk = 256
    for start in list(range(0, plen, chunk)) + [plen]:
        size = chunk if start < plen else DH
        keys = slice(start, start + size)
        k = kv_ref[keys, :DH]
        v = kv_ref[keys, DH:]
        s = lax.dot_general(q, k, NT, preferred_element_type=F32)
        hidden = bias[0:1, keys] if start < plen else causal
        p = jnp.exp2(s * coef - c_top + hidden) * c_inv
        dp = lax.dot_general(g, v, NT, preferred_element_type=F32)
        ds = (p * (dp - c_delta) * scale).astype(BF16)
        acc[:DH, keys] += jnp.dot(qt, ds, preferred_element_type=F32)
        acc[DH:, keys] += jnp.dot(gt, p.astype(BF16), preferred_element_type=F32)
        dq = dq + jnp.dot(ds, k, preferred_element_type=F32)
    for h in range(HALF):
        rows = slice(h * SLOTS, (h + 1) * SLOTS)
        cols = slice(h * DH, (h + 1) * DH)
        if last:
            back_ref[:, ROWS + h * DH : ROWS + (h + 1) * DH] = (
                dq[rows] + prev_ref[:, cols]
            ).astype(BF16)
        else:
            back_ref[:, cols] = dq[rows]

    @pl.when(step == pl.num_programs(0) - 1)
    def _():
        kvgrad_ref[...] = acc[...].T.astype(kvgrad_ref.dtype)


def weight_kernel(steps, first, place_ref, prompt_ref, resp_ref, *refs):
    refs = list(refs)
    plen = prompt_ref.shape[0]
    wide = prompt_ref.shape[1] // NX
    half = wide // 2
    part = wide // 4
    x, core = place_ref[0], place_ref[1]
    if first:
        own_ref, got_ref, prompt_grad_ref, resp_grad_ref = (refs.pop(i) for i in (0, 0, 0, 0))
    else:
        prompt_grad_ref, resp_grad_ref = refs.pop(0), refs.pop(0)
    keep_ref, give_ref, buf, whole, sems = refs
    copies = fetch(steps, x, prompt_ref, resp_ref, buf, sems)
    if first:
        grad = (own_ref[...] + got_ref[...].astype(F32)).astype(BF16)
        prompt_grad_ref[...] = grad[:plen]
        resp_grad_ref[...] = grad[plen:]
    else:
        grad = jnp.concatenate([prompt_grad_ref[...], resp_grad_ref[...]], 0)
    mine = pl.ds(pl.multiple_of(core * part, part), part)
    theirs = pl.ds(pl.multiple_of((1 - core) * part, part), part)
    for n, pair in enumerate(copies):
        for copy in pair:
            copy.wait()
        cols = slice(n * half, (n + 1) * half)
        whole[n] = lax.dot_general(buf[:, cols], grad, TN, preferred_element_type=F32)
        keep_ref[n // 2, n % 2] = whole[n, mine]
        give_ref[n // 2, n % 2] = whole[n, theirs].astype(BF16)


def per_device(
    prompt_hidden, resp_hidden, queries, grad_out, kv_weight, prompt_lengths, response_lengths
):
    rank = lax.axis_index(SEQ)
    x = lax.axis_index("x")
    place = jnp.stack([x, lax.axis_index("c")]).astype(jnp.int32)
    slots = resp_hidden.shape[1]
    plen = prompt_hidden.shape[1]
    model = prompt_hidden.shape[2]
    width = queries.shape[2]
    half = width // 2
    scale = DH ** (-0.5)
    coef = scale * LOG2E
    prompt_rows = prompt_hidden[0]
    resp_rows = resp_hidden[0]
    keys = plen + slots
    shard = kv_weight.shape[0]
    smem = pl.BlockSpec(memory_space=pltpu.SMEM)
    vmem = pl.BlockSpec(memory_space=pltpu.VMEM)

    y = lax.axis_index("y")
    z = lax.axis_index(("zh", "zl"))

    def gather(t, axis, place_of):
        run = [t] + [lax.ppermute(t, axis, shift(k)) for k in range(1, 4)]
        run = jnp.stack(run + run[:3], 0)
        return lax.dynamic_slice_in_dim(run, (4 - place_of) % 4, 4, 0)

    block = gather(kv_weight, "y", y)
    block = gather(block, ("zh", "zl"), z).reshape(2, 2, NY, shard, 2 * DH)
    block = block.transpose(0, 2, 1, 3, 4).reshape(2, 8 * shard, 2 * DH)

    def halves(t):
        return t.reshape(slots, 2, half).transpose(1, 0, 2)

    qg = jnp.concatenate([halves(queries[0]), halves(grad_out[0])], 2)
    qg = jnp.broadcast_to(qg[None], (NY, 2, slots, 2 * half)).reshape(N_SEQ, slots, 2 * half)
    qg, block = lax.optimization_barrier((qg, block))
    nears = [block] + [lax.ppermute(block, "x", shift(k)) for k in range(1, NX)]
    fars = [lax.ppermute(piece, "c", SWAP) for piece in nears]
    qg, fars[0] = lax.optimization_barrier((qg, fars[0]))
    qg_all = lax.all_to_all(qg, SEQ, 0, 0, tiled=True).reshape(N_SEQ * slots, 2 * half)

    hbm = pl.BlockSpec(memory_space=pltpu.HBM)

    def project(steps, prev, last):
        count = len(steps)
        return pl.pallas_call(
            functools.partial(project_kernel, steps, prev is None, last),
            in_specs=[smem, hbm, hbm] + [vmem] * (2 * count + (prev is not None)),
            out_specs=vmem,
            out_shape=jax.ShapeDtypeStruct((keys, 2 * DH), BF16 if last else F32),
            scratch_shapes=[
                pltpu.VMEM((keys, count * model // NX), BF16),
                pltpu.VMEM((count * model // NX, 2 * DH), BF16),
                pltpu.SemaphoreType.DMA((2 * count, 2)),
            ],
            compiler_params=params(24),
            cost_estimate=pl.CostEstimate(
                flops=2 * keys * model * DH * count // 2,
                bytes_accessed=keys * model * count // 2,
                transcendentals=0,
            ),
            name="project_last" if last else "project",
        )(
            place, prompt_rows, resp_rows, *[nears[k] for k in steps], *[fars[k] for k in steps],
            *(() if prev is None else (prev,)),
        )

    kv = project((0,), None, False)
    kv = project((3,), kv, False)
    kv = project((1, 2), kv, True)
    kv_other = lax.ppermute(kv, "zl", SWAP)

    lengths = response_lengths[0]
    live_all = slots * N_SEQ * 5 // 8
    ends = jnp.cumsum(lengths)
    packed = jnp.arange(live_all)
    past = packed[:, None] >= ends[None, :]
    source = packed + jnp.sum(jnp.where(past, slots - lengths[None, :], 0), 1)
    pick = (source[:, None] == jnp.arange(N_SEQ * slots)[None, :]).astype(BF16)

    def masks(owner):
        offset = source - owner * slots
        limit = jnp.where((offset >= 0) & (offset < slots), offset, -1).astype(jnp.int32)
        return (
            (prompt_lengths - plen * owner).astype(jnp.int32),
            jnp.broadcast_to(limit[None, :], (8, live_all)),
            jnp.broadcast_to(limit[:, None], (live_all, DH)),
        )

    valid, limit_rows, limit_cols = masks(rank)
    valid_other, limit_rows_other, limit_cols_other = masks(rank ^ 1)

    steps = live_all // SLOTS
    rows = live_all * HALF
    whole = pl.BlockSpec((keys, 2 * DH), lambda i: (0, 0))
    slot_block = pl.BlockSpec((SLOTS, half), lambda i: (i, 0))
    g_block = pl.BlockSpec((SLOTS, half), lambda i: (i, 1))
    lane_block = pl.BlockSpec((DH, ROWS), lambda i: (0, i))
    limit_lane = pl.BlockSpec((8, SLOTS), lambda i: (0, i))
    limit_slot = pl.BlockSpec((SLOTS, DH), lambda i: (i, 0))
    stat_block = pl.BlockSpec((3, ROWS), lambda i: (0, i))

    def forward(valid, limit, kv, state):
        carried = last = state is not None
        return pl.pallas_call(
            functools.partial(first_pass, coef, carried, last),
            grid=(steps,),
            in_specs=[smem, limit_lane, slot_block, whole]
            + [lane_block, stat_block] * carried
            + [g_block] * last,
            out_specs=[lane_block, stat_block],
            out_shape=[
                jax.ShapeDtypeStruct((DH, rows), F32),
                jax.ShapeDtypeStruct((3, rows), F32),
            ],
            scratch_shapes=[pltpu.VMEM((plen, DH), F32), pltpu.VMEM((DH, keys), BF16)],
            compiler_params=params(24),
            cost_estimate=pl.CostEstimate(
                flops=4 * rows * keys * DH, bytes_accessed=4 << 20, transcendentals=rows * keys
            ),
            name="attend_more" if carried else "attend_own",
        )(valid, limit, qg, kv, *(state or ()), *([qg] if last else []))

    qg = jnp.dot(pick, qg_all, preferred_element_type=F32).astype(BF16)
    state = forward(valid, limit_rows, kv, None)
    out, stat = forward(valid_other, limit_rows_other, kv_other, state)
    stats = [stat] + [lax.ppermute(stat, "y", shift(k)) for k in range(1, NY)]

    def backward(valid, limit, kv, more):
        last = bool(more)
        return pl.pallas_call(
            functools.partial(second_pass, coef, scale, last),
            grid=(steps,),
            in_specs=[
                smem, limit_slot, slot_block, g_block, whole,
            ] + [stat_block] * NY + [lane_block, slot_block] * last,
            out_specs=[
                pl.BlockSpec((SLOTS, 2 * half), lambda i: (i, 0)) if last else slot_block,
                whole,
            ],
            out_shape=[
                jax.ShapeDtypeStruct((live_all, 2 * half), BF16)
                if last
                else jax.ShapeDtypeStruct((live_all, half), F32),
                jax.ShapeDtypeStruct((keys, 2 * DH), F32 if last else BF16),
            ],
            scratch_shapes=[pltpu.VMEM((2 * DH, keys), F32), pltpu.VMEM((8, plen), F32)],
            compiler_params=params(24),
            cost_estimate=pl.CostEstimate(
                flops=10 * rows * keys * DH, bytes_accessed=8 << 20, transcendentals=rows * keys
            ),
            name="grads_own" if last else "grads_other",
        )(valid, limit, qg, qg, kv, *stats, *more)

    qgrad_part, kvgrad_other = backward(valid_other, limit_cols_other, kv_other, ())
    kvgrad_got = lax.ppermute(kvgrad_other, "zl", SWAP)
    back, kvgrad_own = backward(valid, limit_cols, kv, (out, qgrad_part))

    back = lax.dot_general(pick, back, TN, preferred_element_type=F32).astype(BF16)
    back, kvgrad_own = lax.optimization_barrier((back, kvgrad_own))
    back = lax.all_to_all(back.reshape(N_SEQ, slots, 2 * half), SEQ, 0, 0, tiled=True)

    def weight_part(steps, grads):
        first = grads is None
        count = len(steps)
        pieces = [
            jax.ShapeDtypeStruct((count, 2, 8 * shard, 2 * DH), F32),
            jax.ShapeDtypeStruct((count, 2, 8 * shard, 2 * DH), BF16),
        ]
        if first:
            grads = (kvgrad_own, kvgrad_got)
            pieces = [
                jax.ShapeDtypeStruct((plen, 2 * DH), BF16),
                jax.ShapeDtypeStruct((slots, 2 * DH), BF16),
            ] + pieces
        return pl.pallas_call(
            functools.partial(weight_kernel, steps, first),
            in_specs=[smem, hbm, hbm, vmem, vmem],
            out_specs=[vmem] * len(pieces),
            out_shape=pieces,
            scratch_shapes=[
                pltpu.VMEM((keys, count * model // NX), BF16),
                pltpu.VMEM((2 * count, model // NX // 2, 2 * DH), F32),
                pltpu.SemaphoreType.DMA((2 * count, 2)),
            ],
            compiler_params=params(32),
            cost_estimate=pl.CostEstimate(
                flops=2 * keys * model * DH * count // 2,
                bytes_accessed=keys * model * count // 2,
                transcendentals=0,
            ),
            name="weight_near" if first else "weight_far",
        )(place, prompt_rows, resp_rows, *grads)

    prompt_grad, resp_grad, keep, give = weight_part((1, 3), None)
    near_sum = [(keep[n], lax.ppermute(give[n], "c", SWAP)) for n in range(2)]
    keep, give = weight_part((2, 0), (prompt_grad, resp_grad))
    far_sum = [(keep[n], lax.ppermute(give[n], "c", SWAP)) for n in range(2)]
    line = far_sum[1][0] + far_sum[1][1].astype(F32)
    for k, (kept, got) in zip((1, 3, 2), near_sum + far_sum):
        piece = (kept + got.astype(F32)).astype(BF16)
        line = line + lax.ppermute(piece, "x", shift(-k)).astype(F32)

    def scatter(t, axis, place_of, dtype):
        t = lax.dynamic_slice_in_dim(jnp.concatenate([t, t[:3]], 0), place_of, 4, 0)
        total = t[0]
        for k in range(1, 4):
            total = total + lax.ppermute(t[k].astype(dtype), axis, shift(-k)).astype(F32)
        return total

    line = line.reshape(2, NY, 2, shard, 2 * DH).transpose(0, 2, 1, 3, 4)
    line = scatter(line.reshape(4, NY, shard, 2 * DH), ("zh", "zl"), z, BF16)
    weight_grad = scatter(line, "y", y, F32)

    back = jnp.sum(back.reshape(NY, 2, slots, 2 * half).astype(F32), 0).astype(BF16)
    attended = jnp.concatenate([back[0, :, :half], back[1, :, :half]], 1)
    query_grad = jnp.concatenate([back[0, :, half:], back[1, :, half:]], 1)
    return attended[None], query_grad[None], prompt_grad[None], weight_grad


def solution(mesh):
    fine = Mesh(mesh.devices.reshape(4, 2, 2, 4, 2), AXES)
    return jax.shard_map(
        per_device,
        mesh=fine,
        in_specs=(
            P(GRP, SEQ, None),
            P(GRP, SEQ, None),
            P(GRP, SEQ, None),
            P(GRP, SEQ, None),
            P(AXES, None),
            P(GRP),
            P(GRP, None),
        ),
        out_specs=(
            P(GRP, SEQ, None),
            P(GRP, SEQ, None),
            P(GRP, SEQ, None),
            P(AXES, None),
        ),
        check_vma=False,
    )
```

```python
import functools

import jax
import jax.numpy as jnp
from jax import lax
from jax.experimental import pallas as pl
from jax.experimental.pallas import tpu as pltpu
from jax.sharding import Mesh
from jax.sharding import PartitionSpec as P

AXES = ("x", "zh", "c", "y", "zl")
GRP = ("x", "zh", "c")
SEQ = ("y", "zl")
PLANE = ("zh", "y", "zl")
N_SEQ = 8
NX = 4
NY = 4
HEADS = 8
HALF = 4
DH = 128
SLOTS = 128
ROWS = HALF * SLOTS
NEG = -1e30
LOG2E = 1.4426950408889634
NT = (((1,), (1,)), ((), ()))
TN = (((0,), (0,)), ((), ()))
F32 = jnp.float32
BF16 = jnp.bfloat16
SWAP = [(0, 1), (1, 0)]


def params(mib):
    return pltpu.CompilerParams(vmem_limit_bytes=mib << 20)


def shift(k):
    return [((i + k) % 4, i) for i in range(4)]


def stack_heads(ref):
    return jnp.concatenate([ref[:, h * DH : (h + 1) * DH] for h in range(HALF)], 0)


def fetch(steps, x, prompt_ref, resp_ref, buf, sems):
    plen = prompt_ref.shape[0]
    wide = prompt_ref.shape[1] // NX
    half = wide // 2
    copies = []
    for n, k in enumerate(steps):
        for part in range(2):
            there = pl.ds(pl.multiple_of(lax.rem(x + k, NX) * wide + part * half, DH), half)
            here = pl.ds(n * wide + part * half, half)
            sem = sems.at[n * 2 + part]
            pair = (
                pltpu.make_async_copy(prompt_ref.at[:, there], buf.at[:plen, here], sem.at[0]),
                pltpu.make_async_copy(resp_ref.at[:, there], buf.at[plen:, here], sem.at[1]),
            )
            for copy in pair:
                copy.start()
            copies.append(pair)
    return copies


def project_kernel(steps, first, last, place_ref, prompt_ref, resp_ref, *refs):
    refs = list(refs)
    nears = [refs.pop(0) for _ in steps]
    fars = [refs.pop(0) for _ in steps]
    prev_ref = None if first else refs.pop(0)
    kv_ref, buf, weight, sems = refs
    wide = prompt_ref.shape[1] // NX
    half = wide // 2
    part = wide // 4
    x, core = place_ref[0], place_ref[1]
    copies = fetch(steps, x, prompt_ref, resp_ref, buf, sems)
    for n in range(len(steps)):
        for z in range(2):
            base = n * wide + z * half
            weight[pl.ds(pl.multiple_of(base + core * part, part), part)] = nears[n][z]
            weight[pl.ds(pl.multiple_of(base + (1 - core) * part, part), part)] = fars[n][z]
    total = None
    for n, pair in enumerate(copies):
        for copy in pair:
            copy.wait()
        cols = slice(n * half, (n + 1) * half)
        t = jnp.dot(buf[:, cols], weight[cols], preferred_element_type=F32)
        total = t if total is None else total + t
    if not first:
        total = total + prev_ref[...]
    kv_ref[...] = total.astype(kv_ref.dtype)


def first_pass(coef, carried, last, valid_ref, limit_ref, q_ref, kv_ref, *refs):
    refs = list(refs)
    if carried:
        prev_out_ref, prev_stat_ref = refs.pop(0), refs.pop(0)
    if last:
        g_ref = refs.pop(0)
    out_ref, stat_ref, bias, values = refs
    plen = kv_ref.shape[0] - DH

    @pl.when(pl.program_id(0) == 0)
    def _():
        place = lax.broadcasted_iota(jnp.int32, (plen, DH), 0)
        bias[...] = jnp.where(place < valid_ref[0], 0.0, NEG)
        values[...] = kv_ref[:, DH:].T

    causal = jnp.where(
        lax.broadcasted_iota(jnp.int32, (DH, SLOTS), 0) <= limit_ref[0:1], 0.0, NEG
    )
    keys = kv_ref[:, :DH]
    bias_all = jnp.concatenate([bias[...], causal], 0)
    for h in range(HALF):
        lanes = slice(h * SLOTS, (h + 1) * SLOTS)
        cols = slice(h * DH, (h + 1) * DH)
        s = lax.dot_general(keys, q_ref[:, cols], NT, preferred_element_type=F32)
        s = s * coef + bias_all
        top = jnp.max(s, 0, keepdims=True)
        if carried:
            before = prev_stat_ref[0:1, lanes]
            top = jnp.maximum(top, before)
        p = jnp.exp2(s - top)
        total = jnp.sum(p, 0, keepdims=True)
        o = jnp.dot(values[...], p.astype(BF16), preferred_element_type=F32)
        if carried:
            alpha = jnp.exp2(before - top)
            total = total + prev_stat_ref[1:2, lanes] * alpha
            o = o + prev_out_ref[:, lanes] * alpha
        if last:
            o = o / total
            stat_ref[2:3, lanes] = jnp.sum(o * g_ref[:, cols].astype(F32).T, 0, keepdims=True)
        out_ref[:, lanes] = o
        stat_ref[0:1, lanes] = top
        stat_ref[1:2, lanes] = total


def second_pass(coef, scale, last, valid_ref, limit_ref, q_ref, g_ref, kv_ref, *refs):
    stat_refs, refs = refs[:NY], refs[NY:]
    if last:
        out_ref, prev_ref, back_ref, kvgrad_ref, acc, bias = refs
    else:
        back_ref, kvgrad_ref, acc, bias = refs
    step = pl.program_id(0)
    plen = kv_ref.shape[0] - DH
    tops = [ref[0:1] for ref in stat_refs]
    top = functools.reduce(jnp.maximum, tops)
    share = [ref[1:2] * jnp.exp2(t - top) for ref, t in zip(stat_refs, tops)]
    inv = 1.0 / sum(share)
    delta = sum(w * ref[2:3] for w, ref in zip(share, stat_refs)) * inv
    row = lax.broadcasted_iota(jnp.int32, (8, ROWS), 0)
    columns = jnp.where(row == 0, top, jnp.where(row == 1, inv, delta))
    columns = jnp.concatenate([columns] * 16, 0).T

    @pl.when(step == 0)
    def _():
        acc[...] = jnp.zeros_like(acc)
        place = lax.broadcasted_iota(jnp.int32, (8, plen), 1)
        bias[...] = jnp.where(place < valid_ref[0], 0.0, NEG)

    if last:
        weight = share[0] * inv
        att = (out_ref[...] * weight).T
        for h in range(HALF):
            back_ref[:, h * DH : (h + 1) * DH] = att[h * SLOTS : (h + 1) * SLOTS].astype(BF16)

    c_top, c_inv, c_delta = columns[:, 0:1], columns[:, 1:2], columns[:, 2:3]
    q = stack_heads(q_ref)
    g = stack_heads(g_ref)
    qt = q.T
    gt = g.T
    lane = lax.broadcasted_iota(jnp.int32, (SLOTS, DH), 1)
    causal = jnp.concatenate([jnp.where(lane <= limit_ref[...], 0.0, NEG)] * HALF, 0)
    dq = jnp.zeros((ROWS, DH), F32)
    chunk = 256
    for start in list(range(0, plen, chunk)) + [plen]:
        size = chunk if start < plen else DH
        keys = slice(start, start + size)
        k = kv_ref[keys, :DH]
        v = kv_ref[keys, DH:]
        s = lax.dot_general(q, k, NT, preferred_element_type=F32)
        hidden = bias[0:1, keys] if start < plen else causal
        p = jnp.exp2(s * coef - c_top + hidden) * c_inv
        dp = lax.dot_general(g, v, NT, preferred_element_type=F32)
        ds = (p * (dp - c_delta) * scale).astype(BF16)
        acc[:DH, keys] += jnp.dot(qt, ds, preferred_element_type=F32)
        acc[DH:, keys] += jnp.dot(gt, p.astype(BF16), preferred_element_type=F32)
        dq = dq + jnp.dot(ds, k, preferred_element_type=F32)
    for h in range(HALF):
        rows = slice(h * SLOTS, (h + 1) * SLOTS)
        cols = slice(h * DH, (h + 1) * DH)
        if last:
            back_ref[:, ROWS + h * DH : ROWS + (h + 1) * DH] = (
                dq[rows] + prev_ref[:, cols]
            ).astype(BF16)
        else:
            back_ref[:, cols] = dq[rows]

    @pl.when(step == pl.num_programs(0) - 1)
    def _():
        kvgrad_ref[...] = acc[...].T.astype(kvgrad_ref.dtype)


def weight_kernel(steps, first, place_ref, prompt_ref, resp_ref, *refs):
    refs = list(refs)
    plen = prompt_ref.shape[0]
    wide = prompt_ref.shape[1] // NX
    half = wide // 2
    part = wide // 4
    x, core = place_ref[0], place_ref[1]
    if first:
        own_ref, got_ref, prompt_grad_ref, resp_grad_ref = (refs.pop(i) for i in (0, 0, 0, 0))
    else:
        prompt_grad_ref, resp_grad_ref = refs.pop(0), refs.pop(0)
    keep_ref, give_ref, buf, whole, sems = refs
    copies = fetch(steps, x, prompt_ref, resp_ref, buf, sems)
    if first:
        grad = (own_ref[...] + got_ref[...].astype(F32)).astype(BF16)
        prompt_grad_ref[...] = grad[:plen]
        resp_grad_ref[...] = grad[plen:]
    else:
        grad = jnp.concatenate([prompt_grad_ref[...], resp_grad_ref[...]], 0)
    mine = pl.ds(pl.multiple_of(core * part, part), part)
    theirs = pl.ds(pl.multiple_of((1 - core) * part, part), part)
    for n, pair in enumerate(copies):
        for copy in pair:
            copy.wait()
        cols = slice(n * half, (n + 1) * half)
        whole[n] = lax.dot_general(buf[:, cols], grad, TN, preferred_element_type=F32)
        keep_ref[n // 2, n % 2] = whole[n, mine]
        give_ref[n // 2, n % 2] = whole[n, theirs].astype(BF16)


def per_device(
    prompt_hidden, resp_hidden, queries, grad_out, kv_weight, prompt_lengths, response_lengths
):
    rank = lax.axis_index(SEQ)
    x = lax.axis_index("x")
    place = jnp.stack([x, lax.axis_index("c")]).astype(jnp.int32)
    slots = resp_hidden.shape[1]
    plen = prompt_hidden.shape[1]
    model = prompt_hidden.shape[2]
    width = queries.shape[2]
    half = width // 2
    scale = DH ** (-0.5)
    coef = scale * LOG2E
    prompt_rows = prompt_hidden[0]
    resp_rows = resp_hidden[0]
    keys = plen + slots
    shard = kv_weight.shape[0]
    smem = pl.BlockSpec(memory_space=pltpu.SMEM)
    vmem = pl.BlockSpec(memory_space=pltpu.VMEM)

    block = jnp.broadcast_to(kv_weight[None], (16,) + kv_weight.shape)
    block = lax.all_to_all(block, PLANE, 0, 0, tiled=True).reshape(2, 8 * shard, 2 * DH)

    def halves(t):
        return t.reshape(slots, 2, half).transpose(1, 0, 2)

    qg = jnp.concatenate([halves(queries[0]), halves(grad_out[0])], 2)
    qg = jnp.broadcast_to(qg[None], (NY, 2, slots, 2 * half)).reshape(N_SEQ, slots, 2 * half)
    qg, block = lax.optimization_barrier((qg, block))
    nears = [block] + [lax.ppermute(block, "x", shift(k)) for k in range(1, NX)]
    fars = [lax.ppermute(block, "c", SWAP)]
    qg_all = lax.all_to_all(qg, SEQ, 0, 0, tiled=True).reshape(N_SEQ * slots, 2 * half)

    hbm = pl.BlockSpec(memory_space=pltpu.HBM)

    def project(steps, prev, last):
        count = len(steps)
        return pl.pallas_call(
            functools.partial(project_kernel, steps, prev is None, last),
            in_specs=[smem, hbm, hbm] + [vmem] * (2 * count + (prev is not None)),
            out_specs=vmem,
            out_shape=jax.ShapeDtypeStruct((keys, 2 * DH), BF16 if last else F32),
            scratch_shapes=[
                pltpu.VMEM((keys, count * model // NX), BF16),
                pltpu.VMEM((count * model // NX, 2 * DH), BF16),
                pltpu.SemaphoreType.DMA((2 * count, 2)),
            ],
            compiler_params=params(54),
            cost_estimate=pl.CostEstimate(
                flops=2 * keys * model * DH * count // 2,
                bytes_accessed=keys * model * count // 2,
                transcendentals=0,
            ),
            name="project_last" if last else "project",
        )(
            place, prompt_rows, resp_rows, *[nears[k] for k in steps], *[fars[k] for k in steps],
            *(() if prev is None else (prev,)),
        )

    kv = project((0,), None, False)
    nears[3], kv = lax.optimization_barrier((nears[3], kv))
    fars = fars + [lax.ppermute(piece, "c", SWAP) for piece in nears[1:]]
    kv = project((3,), kv, False)
    kv = project((1, 2), kv, True)
    kv_other = lax.ppermute(kv, "zl", SWAP)

    lengths = response_lengths[0]
    live_all = slots * N_SEQ * 5 // 8
    ends = jnp.cumsum(lengths)
    packed = jnp.arange(live_all)
    past = packed[:, None] >= ends[None, :]
    source = packed + jnp.sum(jnp.where(past, slots - lengths[None, :], 0), 1)
    pick = (source[:, None] == jnp.arange(N_SEQ * slots)[None, :]).astype(BF16)

    def masks(owner):
        offset = source - owner * slots
        limit = jnp.where((offset >= 0) & (offset < slots), offset, -1).astype(jnp.int32)
        return (
            (prompt_lengths - plen * owner).astype(jnp.int32),
            jnp.broadcast_to(limit[None, :], (8, live_all)),
            jnp.broadcast_to(limit[:, None], (live_all, DH)),
        )

    valid, limit_rows, limit_cols = masks(rank)
    valid_other, limit_rows_other, limit_cols_other = masks(rank ^ 1)

    steps = live_all // SLOTS
    rows = live_all * HALF
    whole = pl.BlockSpec((keys, 2 * DH), lambda i: (0, 0))
    slot_block = pl.BlockSpec((SLOTS, half), lambda i: (i, 0))
    g_block = pl.BlockSpec((SLOTS, half), lambda i: (i, 1))
    lane_block = pl.BlockSpec((DH, ROWS), lambda i: (0, i))
    limit_lane = pl.BlockSpec((8, SLOTS), lambda i: (0, i))
    limit_slot = pl.BlockSpec((SLOTS, DH), lambda i: (i, 0))
    stat_block = pl.BlockSpec((3, ROWS), lambda i: (0, i))

    def forward(valid, limit, kv, state):
        carried = last = state is not None
        return pl.pallas_call(
            functools.partial(first_pass, coef, carried, last),
            grid=(steps,),
            in_specs=[smem, limit_lane, slot_block, whole]
            + [lane_block, stat_block] * carried
            + [g_block] * last,
            out_specs=[lane_block, stat_block],
            out_shape=[
                jax.ShapeDtypeStruct((DH, rows), F32),
                jax.ShapeDtypeStruct((3, rows), F32),
            ],
            scratch_shapes=[pltpu.VMEM((plen, DH), F32), pltpu.VMEM((DH, keys), BF16)],
            compiler_params=params(24),
            cost_estimate=pl.CostEstimate(
                flops=4 * rows * keys * DH, bytes_accessed=4 << 20, transcendentals=rows * keys
            ),
            name="attend_more" if carried else "attend_own",
        )(valid, limit, qg, kv, *(state or ()), *([qg] if last else []))

    qg = jnp.dot(pick, qg_all, preferred_element_type=F32).astype(BF16)
    state = forward(valid, limit_rows, kv, None)
    out, stat = forward(valid_other, limit_rows_other, kv_other, state)
    stats = [stat] + [lax.ppermute(stat, "y", shift(k)) for k in range(1, NY)]

    def backward(valid, limit, kv, more):
        last = bool(more)
        return pl.pallas_call(
            functools.partial(second_pass, coef, scale, last),
            grid=(steps,),
            in_specs=[
                smem, limit_slot, slot_block, g_block, whole,
            ] + [stat_block] * NY + [lane_block, slot_block] * last,
            out_specs=[
                pl.BlockSpec((SLOTS, 2 * half), lambda i: (i, 0)) if last else slot_block,
                whole,
            ],
            out_shape=[
                jax.ShapeDtypeStruct((live_all, 2 * half), BF16)
                if last
                else jax.ShapeDtypeStruct((live_all, half), F32),
                jax.ShapeDtypeStruct((keys, 2 * DH), F32 if last else BF16),
            ],
            scratch_shapes=[pltpu.VMEM((2 * DH, keys), F32), pltpu.VMEM((8, plen), F32)],
            compiler_params=params(24),
            cost_estimate=pl.CostEstimate(
                flops=10 * rows * keys * DH, bytes_accessed=8 << 20, transcendentals=rows * keys
            ),
            name="grads_own" if last else "grads_other",
        )(valid, limit, qg, qg, kv, *stats, *more)

    qgrad_part, kvgrad_other = backward(valid_other, limit_cols_other, kv_other, ())
    kvgrad_got = lax.ppermute(kvgrad_other, "zl", SWAP)
    back, kvgrad_own = backward(valid, limit_cols, kv, (out, qgrad_part))

    back = lax.dot_general(pick, back, TN, preferred_element_type=F32).astype(BF16)
    back, kvgrad_own = lax.optimization_barrier((back, kvgrad_own))
    back = lax.all_to_all(back.reshape(N_SEQ, slots, 2 * half), SEQ, 0, 0, tiled=True)

    def weight_part(steps, grads):
        first = grads is None
        count = len(steps)
        pieces = [
            jax.ShapeDtypeStruct((count, 2, 8 * shard, 2 * DH), F32),
            jax.ShapeDtypeStruct((count, 2, 8 * shard, 2 * DH), BF16),
        ]
        if first:
            grads = (kvgrad_own, kvgrad_got)
            pieces = [
                jax.ShapeDtypeStruct((plen, 2 * DH), BF16),
                jax.ShapeDtypeStruct((slots, 2 * DH), BF16),
            ] + pieces
        return pl.pallas_call(
            functools.partial(weight_kernel, steps, first),
            in_specs=[smem, hbm, hbm, vmem, vmem],
            out_specs=[vmem] * len(pieces),
            out_shape=pieces,
            scratch_shapes=[
                pltpu.VMEM((keys, count * model // NX), BF16),
                pltpu.VMEM((2 * count, model // NX // 2, 2 * DH), F32),
                pltpu.SemaphoreType.DMA((2 * count, 2)),
            ],
            compiler_params=params(54),
            cost_estimate=pl.CostEstimate(
                flops=2 * keys * model * DH * count // 2,
                bytes_accessed=keys * model * count // 2,
                transcendentals=0,
            ),
            name="weight_near" if first else "weight_far",
        )(place, prompt_rows, resp_rows, *grads)

    prompt_grad, resp_grad, keep, give = weight_part((1, 3), None)
    near_sum = [(keep[n], lax.ppermute(give[n], "c", SWAP)) for n in range(2)]
    keep, give = weight_part((2, 0), (prompt_grad, resp_grad))
    far_sum = [(keep[n], lax.ppermute(give[n], "c", SWAP)) for n in range(2)]
    line = far_sum[1][0] + far_sum[1][1].astype(F32)
    for k, (kept, got) in zip((1, 3, 2), near_sum + far_sum):
        piece = (kept + got.astype(F32)).astype(BF16)
        line = line + lax.ppermute(piece, "x", shift(-k)).astype(F32)

    line = line.astype(BF16).reshape(16, shard, 2 * DH)
    line, back = lax.optimization_barrier((line, back))
    shares = lax.all_to_all(line, PLANE, 0, 0, tiled=True)
    weight_grad = jnp.sum(shares.astype(F32), 0)

    back = jnp.sum(back.reshape(NY, 2, slots, 2 * half).astype(F32), 0).astype(BF16)
    attended = jnp.concatenate([back[0, :, :half], back[1, :, :half]], 1)
    query_grad = jnp.concatenate([back[0, :, half:], back[1, :, half:]], 1)
    return attended[None], query_grad[None], prompt_grad[None], weight_grad


def solution(mesh):
    fine = Mesh(mesh.devices.reshape(4, 2, 2, 4, 2), AXES)
    return jax.shard_map(
        per_device,
        mesh=fine,
        in_specs=(
            P(GRP, SEQ, None),
            P(GRP, SEQ, None),
            P(GRP, SEQ, None),
            P(GRP, SEQ, None),
            P(AXES, None),
            P(GRP),
            P(GRP, None),
        ),
        out_specs=(
            P(GRP, SEQ, None),
            P(GRP, SEQ, None),
            P(GRP, SEQ, None),
            P(AXES, None),
        ),
        check_vma=False,
    )
```

```python
import functools

import jax
import jax.numpy as jnp
from jax import lax
from jax.experimental import pallas as pl
from jax.experimental.pallas import tpu as pltpu
from jax.sharding import Mesh
from jax.sharding import PartitionSpec as P

AXES = ("x", "zh", "c", "y", "zl")
GRP = ("x", "zh", "c")
SEQ = ("y", "zl")
PLANE = ("zh", "y", "zl")
N_SEQ = 8
NX = 4
NY = 4
HEADS = 8
HALF = 4
DH = 128
SLOTS = 128
ROWS = HALF * SLOTS
NEG = -1e30
LOG2E = 1.4426950408889634
NT = (((1,), (1,)), ((), ()))
TN = (((0,), (0,)), ((), ()))
F32 = jnp.float32
BF16 = jnp.bfloat16
SWAP = [(0, 1), (1, 0)]


def params(mib):
    return pltpu.CompilerParams(vmem_limit_bytes=mib << 20)


def shift(k):
    return [((i + k) % 4, i) for i in range(4)]


def stack_heads(ref):
    return jnp.concatenate([ref[:, h * DH : (h + 1) * DH] for h in range(HALF)], 0)


def project_kernel(steps, first, last, place_ref, prompt_ref, resp_ref, *refs):
    refs = list(refs)
    nears = [refs.pop(0) for _ in steps]
    fars = [refs.pop(0) for _ in steps]
    prev_ref = None if first else refs.pop(0)
    kv_ref, weight = refs
    plen = prompt_ref.shape[0]
    wide = prompt_ref.shape[1] // NX
    half = wide // 2
    part = wide // 4
    x, core = place_ref[0], place_ref[1]
    tops, ends = [], []
    for n, k in enumerate(steps):
        for z in range(2):
            base = n * wide + z * half
            weight[pl.ds(pl.multiple_of(base + core * part, part), part)] = nears[n][z]
            weight[pl.ds(pl.multiple_of(base + (1 - core) * part, part), part)] = fars[n][z]
        cols = pl.ds(pl.multiple_of(lax.rem(x + k, NX) * wide, DH), wide)
        w = weight[n * wide : (n + 1) * wide]
        tops.append(jnp.dot(prompt_ref[:, cols], w, preferred_element_type=F32))
        ends.append(jnp.dot(resp_ref[:, cols], w, preferred_element_type=F32))
    top, end = sum(tops[1:], tops[0]), sum(ends[1:], ends[0])
    if not first:
        top, end = top + prev_ref[:plen], end + prev_ref[plen:]
    kv_ref[:plen] = top.astype(kv_ref.dtype)
    kv_ref[plen:] = end.astype(kv_ref.dtype)


def crossing(start_ref, r, block):
    start, end = start_ref[r], start_ref[r + 1]
    base = block * SLOTS
    meets = (start < base + SLOTS) & (end > base)

    def onehot(row_axis):
        row = lax.broadcasted_iota(jnp.int32, (SLOTS, SLOTS), row_axis) + base
        slot = lax.broadcasted_iota(jnp.int32, (SLOTS, SLOTS), 1 - row_axis) + start
        return jnp.where((row == slot) & (row < end), 1.0, 0.0).astype(BF16)

    return meets, onehot


def first_pass(coef, last, valid_ref, limit_ref, *refs):
    if last:
        q_ref, kv_ref, g_ref, prev_out_ref, prev_stat_ref, out_ref, stat_ref, bias, values = refs
    else:
        q_ref, kv_ref, out_ref, stat_ref, bias, values = refs
    plen = kv_ref.shape[0] - DH

    @pl.when(pl.program_id(0) == 0)
    def _():
        place = lax.broadcasted_iota(jnp.int32, (plen, DH), 0)
        bias[...] = jnp.where(place < valid_ref[0], 0.0, NEG)
        values[...] = kv_ref[:, DH:].T

    causal = jnp.where(
        lax.broadcasted_iota(jnp.int32, (DH, SLOTS), 0) <= limit_ref[0:1], 0.0, NEG
    )
    bias_all = jnp.concatenate([bias[...], causal], 0)
    bias_all = jnp.concatenate([bias_all] * 2, 1)
    keys = kv_ref[:, :DH]

    def scores(i):
        q = jnp.concatenate([q_ref[:, h * DH : (h + 1) * DH] for h in (2 * i, 2 * i + 1)], 0)
        return lax.dot_general(keys, q, NT, preferred_element_type=F32)

    following = scores(0)
    for i in range(HALF // 2):
        s = following * coef + bias_all
        if i + 1 < HALF // 2:
            following = scores(i + 1)
        lanes = slice(2 * i * SLOTS, 2 * (i + 1) * SLOTS)
        top = jnp.max(s, 0, keepdims=True)
        if last:
            before = prev_stat_ref[0:1, lanes]
            top = jnp.maximum(top, before)
        p = jnp.exp2(s - top)
        total = jnp.sum(p, 0, keepdims=True)
        o = jnp.dot(values[...], p.astype(BF16), preferred_element_type=F32)
        if last:
            alpha = jnp.exp2(before - top)
            total = total + prev_stat_ref[1:2, lanes] * alpha
            o = (o + prev_out_ref[:, lanes] * alpha) / total
            for j in range(2):
                h = 2 * i + j
                cols = slice(h * DH, (h + 1) * DH)
                part = o[:, j * SLOTS : (j + 1) * SLOTS]
                d = jnp.sum(part * g_ref[:, cols].astype(F32).T, 0, keepdims=True)
                stat_ref[2:3, h * SLOTS : (h + 1) * SLOTS] = d
                out_ref[:, cols] = part.T.astype(BF16)
        else:
            out_ref[:, lanes] = o
        stat_ref[0:1, lanes] = top
        stat_ref[1:2, lanes] = total


def second_pass(coef, scale, last, valid_ref, limit_ref, q_ref, g_ref, kv_ref, *refs):
    stat_refs, refs = refs[:NY], refs[NY:]
    if last:
        start_ref, out_ref, prev_ref, back_ref, kvgrad_ref, acc, bias = refs
    else:
        back_ref, kvgrad_ref, acc, bias = refs
    step = pl.program_id(0)
    plen = kv_ref.shape[0] - DH
    tops = [ref[0:1] for ref in stat_refs]
    top = functools.reduce(jnp.maximum, tops)
    share = [ref[1:2] * jnp.exp2(t - top) for ref, t in zip(stat_refs, tops)]
    inv = 1.0 / sum(share)
    delta = sum(w * ref[2:3] for w, ref in zip(share, stat_refs)) * inv
    row = lax.broadcasted_iota(jnp.int32, (8, ROWS), 0)
    weight = share[0] * inv
    columns = jnp.where(row == 0, top, jnp.where(row == 1, inv, jnp.where(row == 2, delta, weight)))
    columns = jnp.concatenate([columns] * 16, 0).T

    @pl.when(step == 0)
    def _():
        acc[...] = jnp.zeros_like(acc)
        place = lax.broadcasted_iota(jnp.int32, (8, plen), 1)
        bias[...] = jnp.where(place < valid_ref[0], 0.0, NEG)

    c_top, c_inv, c_delta = columns[:, 0:1], columns[:, 1:2], columns[:, 2:3]
    q = stack_heads(q_ref)
    g = stack_heads(g_ref)
    qt = q.T
    gt = g.T
    lane = lax.broadcasted_iota(jnp.int32, (SLOTS, DH), 1)
    causal = jnp.concatenate([jnp.where(lane <= limit_ref[...], 0.0, NEG)] * HALF, 0)
    chunk = 256
    cuts = [slice(i, i + chunk) for i in range(0, plen, chunk)] + [slice(plen, plen + DH)]

    def products(keys):
        s = lax.dot_general(q, kv_ref[keys, :DH], NT, preferred_element_type=F32)
        return s, lax.dot_general(g, kv_ref[keys, DH:], NT, preferred_element_type=F32)

    def weights(keys, s, dp):
        hidden = bias[0:1, keys] if keys.start < plen else causal
        p = jnp.exp2(s * coef - c_top + hidden) * c_inv
        return p.astype(BF16), (p * (dp - c_delta) * scale).astype(BF16)

    def gradients(keys, p, ds):
        acc[:DH, keys] += jnp.dot(qt, ds, preferred_element_type=F32)
        acc[DH:, keys] += jnp.dot(gt, p, preferred_element_type=F32)
        return jnp.dot(ds, kv_ref[keys, :DH], preferred_element_type=F32)

    dq = jnp.zeros((ROWS, DH), F32)
    following = products(cuts[0])
    for i, keys in enumerate(cuts):
        current = following
        if i + 1 < len(cuts):
            following = products(cuts[i + 1])
        if i:
            dq = dq + gradients(cuts[i - 1], *ready)
        ready = weights(keys, *current)
    dq = dq + gradients(cuts[-1], *ready)
    parts = [slice(h * SLOTS, (h + 1) * SLOTS) for h in range(HALF)]
    if last:
        att = [out_ref[:, r].astype(F32) * columns[r, 3:4] for r in parts]
        grad = [dq[r] + prev_ref[:, r] for r in parts]
        back = jnp.concatenate(att + grad, 1).astype(BF16)

        @pl.when(step == 0)
        def _():
            back_ref[...] = jnp.zeros_like(back_ref)

        for r in range(N_SEQ):
            meets, onehot = crossing(start_ref, r, step)

            @pl.when(meets)
            def _():
                rows = slice(r * SLOTS, (r + 1) * SLOTS)
                back_ref[rows] += jnp.dot(onehot(1), back, preferred_element_type=F32).astype(BF16)
    else:
        for r in parts:
            back_ref[:, r] = dq[r]

    @pl.when(step == pl.num_programs(0) - 1)
    def _():
        kvgrad_ref[...] = acc[...].T.astype(kvgrad_ref.dtype)


def weight_kernel(cuts, place_ref, own_ref, got_ref, prompt_ref, resp_ref, *refs):
    keeps, gives = refs[:NX], refs[NX : 2 * NX]
    prompt_grad_ref, buf, grad, whole, sems = refs[2 * NX :]
    plen = prompt_ref.shape[0]
    wide = prompt_ref.shape[1] // NX
    part = wide // 4
    copies = [
        pltpu.make_async_copy(prompt_ref.at[lo:hi], buf.at[lo:hi], sems.at[n])
        for n, (lo, hi) in enumerate(cuts)
    ]
    copies.append(pltpu.make_async_copy(resp_ref, buf.at[plen:], sems.at[len(cuts)]))
    for copy in copies:
        copy.start()
    x, core = place_ref[0], place_ref[1]
    grad[...] = (own_ref[...] + got_ref[...].astype(F32)).astype(BF16)
    prompt_grad_ref[...] = grad[:plen]
    spans = list(cuts[:-1]) + [(cuts[-1][0], buf.shape[0])]
    for n, (lo, hi) in enumerate(spans):
        copies[n].wait()
        if n + 1 == len(spans):
            copies[n + 1].wait()
        for k in range(NX):
            cols = pl.ds(pl.multiple_of(lax.rem(x + k, NX) * wide, DH), wide)
            t = lax.dot_general(buf[lo:hi, cols], grad[lo:hi], TN, preferred_element_type=F32)
            if n:
                t = t + whole[k]
            whole[k] = t
            if n + 1 == len(spans):
                for z in range(2):
                    base = z * 2 * part
                    mine = pl.ds(pl.multiple_of(base + core * part, part), part)
                    theirs = pl.ds(pl.multiple_of(base + (1 - core) * part, part), part)
                    keeps[k][z] = whole[k, mine]
                    gives[k][z] = whole[k, theirs].astype(BF16)


def finish_kernel(back_ref, attended_ref, query_grad_ref):
    width = back_ref.shape[2] // 2
    for side in range(2):
        total = sum(back_ref[2 * k + side].astype(F32) for k in range(NY)).astype(BF16)
        there = slice(side * width, (side + 1) * width)
        attended_ref[:, there] = total[:, :width]
        query_grad_ref[:, there] = total[:, width:]


def per_device(
    prompt_hidden, resp_hidden, queries, grad_out, kv_weight, prompt_lengths, response_lengths
):
    rank = lax.axis_index(SEQ)
    x = lax.axis_index("x")
    place = jnp.stack([x, lax.axis_index("c")]).astype(jnp.int32)
    slots = resp_hidden.shape[1]
    plen = prompt_hidden.shape[1]
    model = prompt_hidden.shape[2]
    width = queries.shape[2]
    half = width // 2
    scale = DH ** (-0.5)
    coef = scale * LOG2E
    prompt_rows = prompt_hidden[0]
    resp_rows = resp_hidden[0]
    keys = plen + slots
    shard = kv_weight.shape[0]
    smem = pl.BlockSpec(memory_space=pltpu.SMEM)
    vmem = pl.BlockSpec(memory_space=pltpu.VMEM)

    block = jnp.broadcast_to(kv_weight[None], (16,) + kv_weight.shape)
    block = lax.all_to_all(block, PLANE, 0, 0, tiled=True).reshape(2, 8 * shard, 2 * DH)

    def halves(t):
        return t.reshape(slots, 2, half).transpose(1, 0, 2)

    qg = jnp.concatenate([halves(queries[0]), halves(grad_out[0])], 2)
    qg = jnp.broadcast_to(qg[None], (NY, 2, slots, 2 * half)).reshape(N_SEQ, slots, 2 * half)
    qg, block = lax.optimization_barrier((qg, block))
    nears = [block] + [lax.ppermute(block, "x", shift(k)) for k in range(1, NX)]
    fars = [lax.ppermute(block, "c", SWAP)]
    qg_all = lax.all_to_all(qg, SEQ, 0, 0, tiled=True).reshape(N_SEQ * slots, 2 * half)

    def project(steps, prev, last):
        count = len(steps)
        return pl.pallas_call(
            functools.partial(project_kernel, steps, prev is None, last),
            in_specs=[smem] + [vmem] * (2 + 2 * count + (prev is not None)),
            out_specs=vmem,
            out_shape=jax.ShapeDtypeStruct((keys, 2 * DH), BF16 if last else F32),
            scratch_shapes=[pltpu.VMEM((count * model // NX, 2 * DH), BF16)],
            compiler_params=params(20),
            cost_estimate=pl.CostEstimate(
                flops=2 * keys * model * DH * count // 2,
                bytes_accessed=keys * model * count // 2,
                transcendentals=0,
            ),
            name="project_last" if last else "project",
        )(
            place, prompt_rows, resp_rows, *[nears[k] for k in steps], *[fars[k] for k in steps],
            *(() if prev is None else (prev,)),
        )

    kv = project((0,), None, False)
    nears[3], kv = lax.optimization_barrier((nears[3], kv))
    fars = fars + [lax.ppermute(piece, "c", SWAP) for piece in nears[1:]]
    kv = project((3,), kv, False)
    kv = project((1, 2), kv, True)
    kv_other = lax.ppermute(kv, "zl", SWAP)

    lengths = response_lengths[0]
    live_all = slots * N_SEQ * 5 // 8
    ends = jnp.cumsum(lengths)
    packed = jnp.arange(live_all)
    past = packed[:, None] >= ends[None, :]
    source = packed + jnp.sum(jnp.where(past, slots - lengths[None, :], 0), 1)
    starts = jnp.concatenate([jnp.zeros((1,), jnp.int32), ends.astype(jnp.int32)])

    def masks(owner):
        offset = source - owner * slots
        limit = jnp.where((offset >= 0) & (offset < slots), offset, -1).astype(jnp.int32)
        return (
            (prompt_lengths - plen * owner).astype(jnp.int32),
            jnp.broadcast_to(limit[None, :], (8, live_all)),
            jnp.broadcast_to(limit[:, None], (live_all, DH)),
        )

    valid, limit_rows, limit_cols = masks(rank)
    valid_other, limit_rows_other, limit_cols_other = masks(rank ^ 1)

    steps = live_all // SLOTS
    rows = live_all * HALF
    whole = pl.BlockSpec((keys, 2 * DH), lambda i: (0, 0))
    slot_block = pl.BlockSpec((SLOTS, half), lambda i: (i, 0))
    g_block = pl.BlockSpec((SLOTS, half), lambda i: (i, 1))
    lane_block = pl.BlockSpec((DH, ROWS), lambda i: (0, i))
    limit_lane = pl.BlockSpec((8, SLOTS), lambda i: (0, i))
    limit_slot = pl.BlockSpec((SLOTS, DH), lambda i: (i, 0))
    stat_block = pl.BlockSpec((3, ROWS), lambda i: (0, i))

    every = pl.BlockSpec((N_SEQ * slots, 2 * half), lambda i: (0, 0))

    def forward(valid, limit, kv, more):
        last = bool(more)
        return pl.pallas_call(
            functools.partial(first_pass, coef, last),
            grid=(steps,),
            in_specs=[smem, limit_lane, slot_block, whole]
            + [g_block, lane_block, stat_block] * last,
            out_specs=[slot_block if last else lane_block, stat_block],
            out_shape=[
                jax.ShapeDtypeStruct((live_all, half), BF16)
                if last
                else jax.ShapeDtypeStruct((DH, rows), F32),
                jax.ShapeDtypeStruct((3, rows), F32),
            ],
            scratch_shapes=[pltpu.VMEM((plen, DH), F32), pltpu.VMEM((DH, keys), BF16)],
            compiler_params=params(20),
            cost_estimate=pl.CostEstimate(
                flops=4 * rows * keys * DH, bytes_accessed=4 << 20, transcendentals=rows * keys
            ),
            name="attend_more" if last else "attend_own",
        )(valid, limit, qg, kv, *more)

    pick = (source[:, None] == jnp.arange(N_SEQ * slots)[None, :]).astype(BF16)
    qg = jnp.dot(pick, qg_all, preferred_element_type=F32).astype(BF16)
    state = forward(valid, limit_rows, kv, ())
    out, stat = forward(valid_other, limit_rows_other, kv_other, (qg, *state))
    stats = [stat] + [lax.ppermute(stat, "y", shift(k)) for k in range(1, NY)]

    def backward(valid, limit, kv, more):
        last = bool(more)
        return pl.pallas_call(
            functools.partial(second_pass, coef, scale, last),
            grid=(steps,),
            in_specs=[
                smem, limit_slot, slot_block, g_block, whole,
            ] + [stat_block] * NY + [smem, slot_block, slot_block] * last,
            out_specs=[
                every if last else slot_block,
                whole,
            ],
            out_shape=[
                jax.ShapeDtypeStruct((N_SEQ * slots, 2 * half), BF16)
                if last
                else jax.ShapeDtypeStruct((live_all, half), F32),
                jax.ShapeDtypeStruct((keys, 2 * DH), F32 if last else BF16),
            ],
            scratch_shapes=[pltpu.VMEM((2 * DH, keys), F32), pltpu.VMEM((8, plen), F32)],
            compiler_params=params(20),
            cost_estimate=pl.CostEstimate(
                flops=10 * rows * keys * DH, bytes_accessed=8 << 20, transcendentals=rows * keys
            ),
            name="grads_own" if last else "grads_other",
        )(valid, limit, qg, qg, kv, *stats, *more)

    qgrad_part, kvgrad_other = backward(valid_other, limit_cols_other, kv_other, ())
    kvgrad_got = lax.ppermute(kvgrad_other, "zl", SWAP)
    back, kvgrad_own = backward(valid, limit_cols, kv, (starts, out, qgrad_part))

    back, kvgrad_own = lax.optimization_barrier((back, kvgrad_own))
    back = lax.all_to_all(back.reshape(N_SEQ, slots, 2 * half), SEQ, 0, 0, tiled=True)

    cuts = ((0, plen // 4), (plen // 4, 3 * plen // 4), (3 * plen // 4, plen))
    piece = (2, 8 * shard, 2 * DH)
    *pieces, prompt_grad = pl.pallas_call(
        functools.partial(weight_kernel, cuts),
        in_specs=[smem] + [vmem] * 2 + [pl.BlockSpec(memory_space=pltpu.HBM)] * 2,
        out_specs=[vmem] * (2 * NX + 1),
        out_shape=[jax.ShapeDtypeStruct(piece, F32)] * NX
        + [jax.ShapeDtypeStruct(piece, BF16)] * NX
        + [jax.ShapeDtypeStruct((plen, 2 * DH), BF16)],
        scratch_shapes=[
            pltpu.VMEM((keys, model), BF16),
            pltpu.VMEM((keys, 2 * DH), BF16),
            pltpu.VMEM((NX, model // NX, 2 * DH), F32),
            pltpu.SemaphoreType.DMA((len(cuts) + 1,)),
        ],
        compiler_params=params(50),
        cost_estimate=pl.CostEstimate(
            flops=4 * keys * model * DH, bytes_accessed=2 * keys * model, transcendentals=0
        ),
        name="weight_grad",
    )(place, kvgrad_own, kvgrad_got, prompt_rows, resp_rows)
    keeps, gives = pieces[:NX], pieces[NX:]
    got = [lax.ppermute(give, "c", SWAP) for give in gives]
    line = keeps[0] + got[0].astype(F32)
    for k in range(1, NX):
        piece = (keeps[k] + got[k].astype(F32)).astype(BF16)
        line = line + lax.ppermute(piece, "x", shift(-k)).astype(F32)
    line = line.astype(BF16).reshape(16, shard, 2 * DH)
    line, back = lax.optimization_barrier((line, back))
    shares = lax.all_to_all(line, PLANE, 0, 0, tiled=True)
    weight_grad = jnp.sum(shares.astype(F32), 0)

    attended, query_grad = pl.pallas_call(
        finish_kernel,
        in_specs=[vmem],
        out_specs=[vmem] * 2,
        out_shape=[jax.ShapeDtypeStruct((slots, width), BF16)] * 2,
        compiler_params=params(16),
        name="finish",
    )(back)
    return attended[None], query_grad[None], prompt_grad[None], weight_grad


def solution(mesh):
    fine = Mesh(mesh.devices.reshape(4, 2, 2, 4, 2), AXES)
    return jax.shard_map(
        per_device,
        mesh=fine,
        in_specs=(
            P(GRP, SEQ, None),
            P(GRP, SEQ, None),
            P(GRP, SEQ, None),
            P(GRP, SEQ, None),
            P(AXES, None),
            P(GRP),
            P(GRP, None),
        ),
        out_specs=(
            P(GRP, SEQ, None),
            P(GRP, SEQ, None),
            P(GRP, SEQ, None),
            P(AXES, None),
        ),
        check_vma=False,
    )
```

```python
import functools

import jax
import jax.numpy as jnp
from jax import lax
from jax.experimental import pallas as pl
from jax.experimental.pallas import tpu as pltpu
from jax.sharding import Mesh
from jax.sharding import PartitionSpec as P

AXES = ("x", "zh", "c", "y", "zl")
GRP = ("x", "zh", "c")
SEQ = ("y", "zl")
PLANE = ("zh", "y", "zl")
N_SEQ = 8
NX = 4
NY = 4
HEADS = 8
HALF = 4
DH = 128
SLOTS = 128
ROWS = HALF * SLOTS
NEG = -1e30
LOG2E = 1.4426950408889634
NT = (((1,), (1,)), ((), ()))
TN = (((0,), (0,)), ((), ()))
F32 = jnp.float32
BF16 = jnp.bfloat16
SWAP = [(0, 1), (1, 0)]


def params(mib):
    return pltpu.CompilerParams(vmem_limit_bytes=mib << 20)


def shift(k):
    return [((i + k) % 4, i) for i in range(4)]


def stack_heads(ref):
    return jnp.concatenate([ref[:, h * DH : (h + 1) * DH] for h in range(HALF)], 0)


def copies_kernel(block_ref, out_ref):
    for i in range(out_ref.shape[0]):
        out_ref[i] = block_ref[...]


def halves_kernel(q_ref, g_ref, out_ref, buf, sems):
    half = q_ref.shape[1] // 2
    for side in range(2):
        cols = slice(side * half, (side + 1) * half)
        buf[side, :, :half] = q_ref[:, cols]
        buf[side, :, half:] = g_ref[:, cols]
    copies = [
        pltpu.make_async_copy(buf, out_ref.at[2 * k : 2 * k + 2], sems.at[k]) for k in range(NY)
    ]
    for copy in copies:
        copy.start()
    for copy in copies:
        copy.wait()


def project_kernel(steps, first, last, place_ref, prompt_ref, resp_ref, *refs):
    refs = list(refs)
    nears = [refs.pop(0) for _ in steps]
    fars = [refs.pop(0) for _ in steps]
    prev_ref = None if first else refs.pop(0)
    kv_ref, weight = refs
    plen = prompt_ref.shape[0]
    wide = prompt_ref.shape[1] // NX
    half = wide // 2
    part = wide // 4
    x, core = place_ref[0], place_ref[1]
    tops, ends = [], []
    for n, k in enumerate(steps):
        for z in range(2):
            base = n * wide + z * half
            weight[pl.ds(pl.multiple_of(base + core * part, part), part)] = nears[n][z]
            weight[pl.ds(pl.multiple_of(base + (1 - core) * part, part), part)] = fars[n][z]
        cols = pl.ds(pl.multiple_of(lax.rem(x + k, NX) * wide, DH), wide)
        w = weight[n * wide : (n + 1) * wide]
        tops.append(jnp.dot(prompt_ref[:, cols], w, preferred_element_type=F32))
        ends.append(jnp.dot(resp_ref[:, cols], w, preferred_element_type=F32))
    top, end = sum(tops[1:], tops[0]), sum(ends[1:], ends[0])
    if not first:
        top, end = top + prev_ref[:plen], end + prev_ref[plen:]
    kv_ref[:plen] = top.astype(kv_ref.dtype)
    kv_ref[plen:] = end.astype(kv_ref.dtype)


def one_hot(start_ref, r, block):
    row = lax.broadcasted_iota(jnp.int32, (SLOTS, SLOTS), 1) + block * SLOTS
    slot = lax.broadcasted_iota(jnp.int32, (SLOTS, SLOTS), 0) + start_ref[r]
    return jnp.where((row == slot) & (row < start_ref[r + 1]), 1.0, 0.0).astype(BF16)


def visible(start_ref, r, block, row_axis):
    row = lax.broadcasted_iota(jnp.int32, (SLOTS, SLOTS), row_axis) + block * SLOTS
    slot = lax.broadcasted_iota(jnp.int32, (SLOTS, SLOTS), 1 - row_axis) + start_ref[r]
    return (slot <= row) & (row < start_ref[r + 1])


def first_pass(coef, last, info_ref, start_ref, *refs):
    if last:
        q_ref, kv_ref, g_ref, prev_out_ref, prev_stat_ref, out_ref, stat_ref, bias, values = refs
    else:
        q_ref, kv_ref, out_ref, stat_ref, bias, values = refs
    plen = kv_ref.shape[0] - DH

    @pl.when(pl.program_id(0) == 0)
    def _():
        place = lax.broadcasted_iota(jnp.int32, (plen, DH), 0)
        bias[...] = jnp.where(place < info_ref[0], 0.0, NEG)
        values[...] = kv_ref[:, DH:].T

    causal = jnp.where(visible(start_ref, info_ref[1], pl.program_id(0), 1), 0.0, NEG)
    bias_all = jnp.concatenate([bias[...], causal], 0)
    bias_all = jnp.concatenate([bias_all] * 2, 1)
    keys = kv_ref[:, :DH]

    def scores(i):
        q = jnp.concatenate([q_ref[:, h * DH : (h + 1) * DH] for h in (2 * i, 2 * i + 1)], 0)
        return lax.dot_general(keys, q, NT, preferred_element_type=F32)

    following = scores(0)
    for i in range(HALF // 2):
        s = following * coef + bias_all
        if i + 1 < HALF // 2:
            following = scores(i + 1)
        lanes = slice(2 * i * SLOTS, 2 * (i + 1) * SLOTS)
        top = jnp.max(s, 0, keepdims=True)
        if last:
            before = prev_stat_ref[0:1, lanes]
            top = jnp.maximum(top, before)
        p = jnp.exp2(s - top)
        total = jnp.sum(p, 0, keepdims=True)
        o = jnp.dot(values[...], p.astype(BF16), preferred_element_type=F32)
        if last:
            alpha = jnp.exp2(before - top)
            total = total + prev_stat_ref[1:2, lanes] * alpha
            o = (o + prev_out_ref[:, lanes] * alpha) / total
            for j in range(2):
                h = 2 * i + j
                cols = slice(h * DH, (h + 1) * DH)
                part = o[:, j * SLOTS : (j + 1) * SLOTS]
                d = jnp.sum(part * g_ref[:, cols].astype(F32).T, 0, keepdims=True)
                stat_ref[2:3, h * SLOTS : (h + 1) * SLOTS] = d
                out_ref[:, cols] = part.T.astype(BF16)
        else:
            out_ref[:, lanes] = o
        stat_ref[0:1, lanes] = top
        stat_ref[1:2, lanes] = total


def second_pass(coef, scale, last, info_ref, start_ref, q_ref, g_ref, kv_ref, *refs):
    stat_refs, refs = refs[:NY], refs[NY:]
    if last:
        span_ref, out_ref, prev_ref, back_ref, kvgrad_ref, acc, bias = refs
    else:
        back_ref, kvgrad_ref, acc, bias = refs
    step = pl.program_id(0)
    plen = kv_ref.shape[0] - DH
    tops = [ref[0:1] for ref in stat_refs]
    top = functools.reduce(jnp.maximum, tops)
    share = [ref[1:2] * jnp.exp2(t - top) for ref, t in zip(stat_refs, tops)]
    inv = 1.0 / sum(share)
    delta = sum(w * ref[2:3] for w, ref in zip(share, stat_refs)) * inv
    row = lax.broadcasted_iota(jnp.int32, (8, ROWS), 0)
    weight = share[0] * inv
    columns = jnp.where(row == 0, top, jnp.where(row == 1, inv, jnp.where(row == 2, delta, weight)))
    columns = jnp.concatenate([columns] * 16, 0).T

    @pl.when(step == 0)
    def _():
        acc[...] = jnp.zeros_like(acc)
        place = lax.broadcasted_iota(jnp.int32, (8, plen), 1)
        bias[...] = jnp.where(place < info_ref[0], 0.0, NEG)

    c_top, c_inv, c_delta = columns[:, 0:1], columns[:, 1:2], columns[:, 2:3]
    q = stack_heads(q_ref)
    g = stack_heads(g_ref)
    qt = q.T
    gt = g.T
    seen = visible(start_ref, info_ref[1], step, 0)
    causal = jnp.concatenate([jnp.where(seen, 0.0, NEG)] * HALF, 0)
    chunk = 256
    cuts = [slice(i, i + chunk) for i in range(0, plen, chunk)] + [slice(plen, plen + DH)]

    def products(keys):
        s = lax.dot_general(q, kv_ref[keys, :DH], NT, preferred_element_type=F32)
        return s, lax.dot_general(g, kv_ref[keys, DH:], NT, preferred_element_type=F32)

    def weights(keys, s, dp):
        hidden = bias[0:1, keys] if keys.start < plen else causal
        p = jnp.exp2(s * coef - c_top + hidden) * c_inv
        return p.astype(BF16), (p * (dp - c_delta) * scale).astype(BF16)

    def gradients(keys, p, ds):
        acc[:DH, keys] += jnp.dot(qt, ds, preferred_element_type=F32)
        acc[DH:, keys] += jnp.dot(gt, p, preferred_element_type=F32)
        return jnp.dot(ds, kv_ref[keys, :DH], preferred_element_type=F32)

    dq = jnp.zeros((ROWS, DH), F32)
    following = products(cuts[0])
    for i, keys in enumerate(cuts):
        current = following
        if i + 1 < len(cuts):
            following = products(cuts[i + 1])
        if i:
            dq = dq + gradients(cuts[i - 1], *ready)
        ready = weights(keys, *current)
    dq = dq + gradients(cuts[-1], *ready)
    parts = [slice(h * SLOTS, (h + 1) * SLOTS) for h in range(HALF)]
    if last:
        att = [out_ref[:, r].astype(F32) * columns[r, 3:4] for r in parts]
        grad = [dq[r] + prev_ref[:, r] for r in parts]
        back = jnp.concatenate(att + grad, 1).astype(BF16)

        @pl.when(step == 0)
        def _():
            back_ref[...] = jnp.zeros_like(back_ref)

        def place(r, _):
            slots = pl.ds(pl.multiple_of(r * SLOTS, SLOTS), SLOTS)
            onehot = one_hot(start_ref, r, step)
            back_ref[slots] += jnp.dot(onehot, back, preferred_element_type=F32).astype(BF16)
            return 0

        lax.fori_loop(span_ref[2 * step], span_ref[2 * step + 1], place, 0)
    else:
        for r in parts:
            back_ref[:, r] = dq[r]

    @pl.when(step == pl.num_programs(0) - 1)
    def _():
        kvgrad_ref[...] = acc[...].T.astype(kvgrad_ref.dtype)


def weight_kernel(cuts, place_ref, own_ref, got_ref, prompt_ref, resp_ref, *refs):
    keeps, gives = refs[:NX], refs[NX : 2 * NX]
    prompt_grad_ref, buf, whole, sems = refs[2 * NX :]
    plen = prompt_ref.shape[0]
    wide = prompt_ref.shape[1] // NX
    part = wide // 4
    copies = [
        pltpu.make_async_copy(prompt_ref.at[lo:hi], buf.at[lo:hi], sems.at[n])
        for n, (lo, hi) in enumerate(cuts)
    ]
    copies.append(pltpu.make_async_copy(resp_ref, buf.at[plen:], sems.at[len(cuts)]))
    for copy in copies:
        copy.start()
    x, core = place_ref[0], place_ref[1]
    grad = (own_ref[...] + got_ref[...].astype(F32)).astype(BF16)
    prompt_grad_ref[...] = grad[:plen]
    grad = grad.T
    spans = list(cuts[:-1]) + [(cuts[-1][0], buf.shape[0])]
    for n, (lo, hi) in enumerate(spans):
        copies[n].wait()
        if n + 1 == len(spans):
            copies[n + 1].wait()
        for k in range(NX):
            cols = pl.ds(pl.multiple_of(lax.rem(x + k, NX) * wide, DH), wide)
            t = jnp.dot(grad[:, lo:hi], buf[lo:hi, cols], preferred_element_type=F32).T
            if n:
                t = t + whole[k]
            whole[k] = t
            if n + 1 == len(spans):
                for z in range(2):
                    base = z * 2 * part
                    mine = pl.ds(pl.multiple_of(base + core * part, part), part)
                    theirs = pl.ds(pl.multiple_of(base + (1 - core) * part, part), part)
                    keeps[k][z] = whole[k, mine]
                    gives[k][z] = whole[k, theirs].astype(BF16)


def finish_kernel(back_ref, attended_ref, query_grad_ref):
    width = back_ref.shape[2] // 2
    for side in range(2):
        total = sum(back_ref[2 * k + side].astype(F32) for k in range(NY)).astype(BF16)
        there = slice(side * width, (side + 1) * width)
        attended_ref[:, there] = total[:, :width]
        query_grad_ref[:, there] = total[:, width:]


def per_device(
    prompt_hidden, resp_hidden, queries, grad_out, kv_weight, prompt_lengths, response_lengths
):
    rank = lax.axis_index(SEQ)
    x = lax.axis_index("x")
    place = jnp.stack([x, lax.axis_index("c")]).astype(jnp.int32)
    slots = resp_hidden.shape[1]
    plen = prompt_hidden.shape[1]
    model = prompt_hidden.shape[2]
    width = queries.shape[2]
    half = width // 2
    scale = DH ** (-0.5)
    coef = scale * LOG2E
    prompt_rows = prompt_hidden[0]
    resp_rows = resp_hidden[0]
    keys = plen + slots
    shard = kv_weight.shape[0]
    smem = pl.BlockSpec(memory_space=pltpu.SMEM)
    vmem = pl.BlockSpec(memory_space=pltpu.VMEM)

    lengths = response_lengths[0]
    live_all = slots * N_SEQ * 5 // 8
    ends = jnp.cumsum(lengths)
    packed = jnp.arange(live_all)
    past = packed[:, None] >= ends[None, :]
    source = packed + jnp.sum(jnp.where(past, slots - lengths[None, :], 0), 1)
    starts = jnp.concatenate([jnp.zeros((1,), jnp.int32), ends.astype(jnp.int32)])
    lows = jnp.arange(live_all // SLOTS)[:, None] * SLOTS
    first = jnp.sum(ends[None, :] <= lows, 1)
    behind = jnp.sum((ends - lengths)[None, :] < lows + SLOTS, 1)
    spans = jnp.stack([first, behind], 1).astype(jnp.int32).reshape(-1)

    def info(owner):
        return jnp.stack([prompt_lengths[0] - plen * owner, owner]).astype(jnp.int32)

    mine, others = info(rank), info(rank ^ 1)

    block = pl.pallas_call(
        copies_kernel,
        in_specs=[vmem],
        out_specs=vmem,
        out_shape=jax.ShapeDtypeStruct((16,) + kv_weight.shape, BF16),
        compiler_params=params(16),
        name="weight_copies",
    )(kv_weight)
    block = lax.all_to_all(block, PLANE, 0, 0, tiled=True).reshape(2, 8 * shard, 2 * DH)

    qg = pl.pallas_call(
        halves_kernel,
        in_specs=[vmem] * 2,
        out_specs=pl.BlockSpec(memory_space=pl.ANY),
        out_shape=jax.ShapeDtypeStruct((N_SEQ, slots, 2 * half), BF16),
        scratch_shapes=[pltpu.VMEM((2, slots, 2 * half), BF16), pltpu.SemaphoreType.DMA((NY,))],
        compiler_params=params(16),
        cost_estimate=pl.CostEstimate(flops=0, bytes_accessed=8 << 20, transcendentals=0),
        name="query_halves",
    )(queries[0], grad_out[0])
    small = (place, source, starts, spans, mine, others)
    qg, block, small = lax.optimization_barrier((qg, block, small))
    place, source, starts, spans, mine, others = small
    nears = [block] + [lax.ppermute(block, "x", shift(k)) for k in range(1, NX)]
    fars = [lax.ppermute(block, "c", SWAP)]
    qg_all = lax.all_to_all(qg, SEQ, 0, 0, tiled=True).reshape(N_SEQ * slots, 2 * half)

    def project(steps, prev, last):
        count = len(steps)
        return pl.pallas_call(
            functools.partial(project_kernel, steps, prev is None, last),
            in_specs=[smem] + [vmem] * (2 + 2 * count + (prev is not None)),
            out_specs=vmem,
            out_shape=jax.ShapeDtypeStruct((keys, 2 * DH), BF16 if last else F32),
            scratch_shapes=[pltpu.VMEM((count * model // NX, 2 * DH), BF16)],
            compiler_params=params(20),
            cost_estimate=pl.CostEstimate(
                flops=2 * keys * model * DH * count // 2,
                bytes_accessed=keys * model * count // 2,
                transcendentals=0,
            ),
            name="project_last" if last else "project",
        )(
            place, prompt_rows, resp_rows, *[nears[k] for k in steps], *[fars[k] for k in steps],
            *(() if prev is None else (prev,)),
        )

    kv = project((0,), None, False)
    nears[3], kv = lax.optimization_barrier((nears[3], kv))
    fars = fars + [lax.ppermute(piece, "c", SWAP) for piece in nears[1:]]
    kv = project((3,), kv, False)
    kv = project((1, 2), kv, True)
    kv_other = lax.ppermute(kv, "zl", SWAP)

    steps = live_all // SLOTS
    rows = live_all * HALF
    whole = pl.BlockSpec((keys, 2 * DH), lambda i: (0, 0))
    slot_block = pl.BlockSpec((SLOTS, half), lambda i: (i, 0))
    g_block = pl.BlockSpec((SLOTS, half), lambda i: (i, 1))
    lane_block = pl.BlockSpec((DH, ROWS), lambda i: (0, i))
    stat_block = pl.BlockSpec((3, ROWS), lambda i: (0, i))

    every = pl.BlockSpec((N_SEQ * slots, 2 * half), lambda i: (0, 0))

    def forward(owner, kv, more):
        last = bool(more)
        return pl.pallas_call(
            functools.partial(first_pass, coef, last),
            grid=(steps,),
            in_specs=[smem, smem, slot_block, whole]
            + [g_block, lane_block, stat_block] * last,
            out_specs=[slot_block if last else lane_block, stat_block],
            out_shape=[
                jax.ShapeDtypeStruct((live_all, half), BF16)
                if last
                else jax.ShapeDtypeStruct((DH, rows), F32),
                jax.ShapeDtypeStruct((3, rows), F32),
            ],
            scratch_shapes=[pltpu.VMEM((plen, DH), F32), pltpu.VMEM((DH, keys), BF16)],
            compiler_params=params(20),
            cost_estimate=pl.CostEstimate(
                flops=4 * rows * keys * DH, bytes_accessed=4 << 20, transcendentals=rows * keys
            ),
            name="attend_more" if last else "attend_own",
        )(owner, starts, qg, kv, *more)

    pick = (source[:, None] == jnp.arange(N_SEQ * slots)[None, :]).astype(BF16)
    qg = jnp.dot(pick, qg_all, preferred_element_type=F32).astype(BF16)
    state = forward(mine, kv, ())
    out, stat = forward(others, kv_other, (qg, *state))
    stats = [stat] + [lax.ppermute(stat, "y", shift(k)) for k in range(1, NY)]

    def backward(owner, kv, more):
        last = bool(more)
        return pl.pallas_call(
            functools.partial(second_pass, coef, scale, last),
            grid=(steps,),
            in_specs=[
                smem, smem, slot_block, g_block, whole,
            ] + [stat_block] * NY + [smem, slot_block, slot_block] * last,
            out_specs=[
                every if last else slot_block,
                whole,
            ],
            out_shape=[
                jax.ShapeDtypeStruct((N_SEQ * slots, 2 * half), BF16)
                if last
                else jax.ShapeDtypeStruct((live_all, half), F32),
                jax.ShapeDtypeStruct((keys, 2 * DH), F32 if last else BF16),
            ],
            scratch_shapes=[pltpu.VMEM((2 * DH, keys), F32), pltpu.VMEM((8, plen), F32)],
            compiler_params=params(20),
            cost_estimate=pl.CostEstimate(
                flops=10 * rows * keys * DH, bytes_accessed=8 << 20, transcendentals=rows * keys
            ),
            name="grads_own" if last else "grads_other",
        )(owner, starts, qg, qg, kv, *stats, *more)

    qgrad_part, kvgrad_other = backward(others, kv_other, ())
    kvgrad_got = lax.ppermute(kvgrad_other, "zl", SWAP)
    back, kvgrad_own = backward(mine, kv, (spans, out, qgrad_part))

    back, kvgrad_own = lax.optimization_barrier((back, kvgrad_own))
    back = lax.all_to_all(back.reshape(N_SEQ, slots, 2 * half), SEQ, 0, 0, tiled=True)

    cuts = ((0, plen // 2), (plen // 2, plen))
    piece = (2, 8 * shard, 2 * DH)
    *pieces, prompt_grad = pl.pallas_call(
        functools.partial(weight_kernel, cuts),
        in_specs=[smem] + [vmem] * 2 + [pl.BlockSpec(memory_space=pltpu.HBM)] * 2,
        out_specs=[vmem] * (2 * NX + 1),
        out_shape=[jax.ShapeDtypeStruct(piece, F32)] * NX
        + [jax.ShapeDtypeStruct(piece, BF16)] * NX
        + [jax.ShapeDtypeStruct((plen, 2 * DH), BF16)],
        scratch_shapes=[
            pltpu.VMEM((keys, model), BF16),
            pltpu.VMEM((NX, model // NX, 2 * DH), F32),
            pltpu.SemaphoreType.DMA((len(cuts) + 1,)),
        ],
        compiler_params=params(50),
        cost_estimate=pl.CostEstimate(
            flops=4 * keys * model * DH, bytes_accessed=2 * keys * model, transcendentals=0
        ),
        name="weight_grad",
    )(place, kvgrad_own, kvgrad_got, prompt_rows, resp_rows)
    keeps, gives = pieces[:NX], pieces[NX:]
    got = [lax.ppermute(give, "c", SWAP) for give in gives]
    line = keeps[0] + got[0].astype(F32)
    for k in range(1, NX):
        piece = (keeps[k] + got[k].astype(F32)).astype(BF16)
        line = line + lax.ppermute(piece, "x", shift(-k)).astype(F32)
    line = line.astype(BF16).reshape(16, shard, 2 * DH)
    line, back = lax.optimization_barrier((line, back))
    shares = lax.all_to_all(line, PLANE, 0, 0, tiled=True)
    weight_grad = jnp.sum(shares.astype(F32), 0)

    attended, query_grad = pl.pallas_call(
        finish_kernel,
        in_specs=[vmem],
        out_specs=[vmem] * 2,
        out_shape=[jax.ShapeDtypeStruct((slots, width), BF16)] * 2,
        compiler_params=params(16),
        name="finish",
    )(back)
    return attended[None], query_grad[None], prompt_grad[None], weight_grad


def solution(mesh):
    fine = Mesh(mesh.devices.reshape(4, 2, 2, 4, 2), AXES)
    return jax.shard_map(
        per_device,
        mesh=fine,
        in_specs=(
            P(GRP, SEQ, None),
            P(GRP, SEQ, None),
            P(GRP, SEQ, None),
            P(GRP, SEQ, None),
            P(AXES, None),
            P(GRP),
            P(GRP, None),
        ),
        out_specs=(
            P(GRP, SEQ, None),
            P(GRP, SEQ, None),
            P(GRP, SEQ, None),
            P(AXES, None),
        ),
        check_vma=False,
    )
```

```python
import functools

import jax
import jax.numpy as jnp
from jax import lax
from jax.experimental import pallas as pl
from jax.experimental.pallas import tpu as pltpu
from jax.sharding import Mesh
from jax.sharding import PartitionSpec as P

AXES = ("x", "zh", "c", "y", "zl")
GRP = ("x", "zh", "c")
SEQ = ("y", "zl")
PLANE = ("zh", "y", "zl")
N_SEQ = 8
NX = 4
NY = 4
HEADS = 8
HALF = 4
DH = 128
SLOTS = 128
ROWS = HALF * SLOTS
NEG = -1e30
LOG2E = 1.4426950408889634
NT = (((1,), (1,)), ((), ()))
TN = (((0,), (0,)), ((), ()))
F32 = jnp.float32
BF16 = jnp.bfloat16
SWAP = [(0, 1), (1, 0)]


def params(mib):
    return pltpu.CompilerParams(vmem_limit_bytes=mib << 20)


def shift(k):
    return [((i + k) % 4, i) for i in range(4)]


def stack_heads(ref):
    return jnp.concatenate([ref[:, h * DH : (h + 1) * DH] for h in range(HALF)], 0)


def copies_kernel(block_ref, out_ref):
    for i in range(out_ref.shape[0]):
        out_ref[i] = block_ref[...]


def halves_kernel(q_ref, g_ref, out_ref, buf, sems):
    half = q_ref.shape[1] // 2
    for side in range(2):
        cols = slice(side * half, (side + 1) * half)
        buf[side, :, :half] = q_ref[:, cols]
        buf[side, :, half:] = g_ref[:, cols]
    copies = [
        pltpu.make_async_copy(buf, out_ref.at[2 * k : 2 * k + 2], sems.at[k]) for k in range(NY)
    ]
    for copy in copies:
        copy.start()
    for copy in copies:
        copy.wait()


def project_kernel(steps, first, last, place_ref, prompt_ref, resp_ref, *refs):
    refs = list(refs)
    nears = [refs.pop(0) for _ in steps]
    fars = [refs.pop(0) for _ in steps]
    prev_ref = None if first else refs.pop(0)
    kv_ref, weight = refs
    plen = prompt_ref.shape[0]
    wide = prompt_ref.shape[1] // NX
    half = wide // 2
    part = wide // 4
    x, core = place_ref[0], place_ref[1]
    tops, ends = [], []
    for n, k in enumerate(steps):
        for z in range(2):
            base = n * wide + z * half
            weight[pl.ds(pl.multiple_of(base + core * part, part), part)] = nears[n][z]
            weight[pl.ds(pl.multiple_of(base + (1 - core) * part, part), part)] = fars[n][z]
        cols = pl.ds(pl.multiple_of(lax.rem(x + k, NX) * wide, DH), wide)
        w = weight[n * wide : (n + 1) * wide]
        tops.append(jnp.dot(prompt_ref[:, cols], w, preferred_element_type=F32))
        ends.append(jnp.dot(resp_ref[:, cols], w, preferred_element_type=F32))
    top, end = sum(tops[1:], tops[0]), sum(ends[1:], ends[0])
    if not first:
        top, end = top + prev_ref[:plen], end + prev_ref[plen:]
    kv_ref[:plen] = top.astype(kv_ref.dtype)
    kv_ref[plen:] = end.astype(kv_ref.dtype)


def one_hot(start_ref, r, block):
    row = lax.broadcasted_iota(jnp.int32, (SLOTS, SLOTS), 1) + block * SLOTS
    slot = lax.broadcasted_iota(jnp.int32, (SLOTS, SLOTS), 0) + start_ref[r]
    return jnp.where((row == slot) & (row < start_ref[r + 1]), 1.0, 0.0).astype(BF16)


def first_pass(coef, last, bound_ref, *refs):
    if last:
        q_ref, kv_ref, g_ref, prev_out_ref, prev_stat_ref, out_ref, stat_ref, bias, values = refs
    else:
        q_ref, kv_ref, out_ref, stat_ref, bias, values = refs
    plen = kv_ref.shape[0] - DH

    @pl.when(pl.program_id(0) == 0)
    def _():
        place = lax.broadcasted_iota(jnp.int32, (plen, DH), 0)
        bias[...] = jnp.where(place < bound_ref[8:9], 0.0, NEG)
        values[...] = kv_ref[:, DH:].T

    slot = lax.broadcasted_iota(jnp.int32, (DH, SLOTS), 0)
    causal = jnp.where(slot <= bound_ref[0:1], 0.0, NEG)
    bias_all = jnp.concatenate([bias[...], causal], 0)
    bias_all = jnp.concatenate([bias_all] * 2, 1)
    keys = kv_ref[:, :DH]

    def scores(i):
        q = jnp.concatenate([q_ref[:, h * DH : (h + 1) * DH] for h in (2 * i, 2 * i + 1)], 0)
        return lax.dot_general(keys, q, NT, preferred_element_type=F32)

    following = scores(0)
    for i in range(HALF // 2):
        s = following * coef + bias_all
        if i + 1 < HALF // 2:
            following = scores(i + 1)
        lanes = slice(2 * i * SLOTS, 2 * (i + 1) * SLOTS)
        top = jnp.max(s, 0, keepdims=True)
        if last:
            before = prev_stat_ref[0:1, lanes]
            top = jnp.maximum(top, before)
        p = jnp.exp2(s - top)
        total = jnp.sum(p, 0, keepdims=True)
        o = jnp.dot(values[...], p.astype(BF16), preferred_element_type=F32)
        if last:
            alpha = jnp.exp2(before - top)
            total = total + prev_stat_ref[1:2, lanes] * alpha
            o = (o + prev_out_ref[:, lanes] * alpha) / total
            for j in range(2):
                h = 2 * i + j
                cols = slice(h * DH, (h + 1) * DH)
                part = o[:, j * SLOTS : (j + 1) * SLOTS]
                d = jnp.sum(part * g_ref[:, cols].astype(F32).T, 0, keepdims=True)
                stat_ref[2:3, h * SLOTS : (h + 1) * SLOTS] = d
                out_ref[:, cols] = part.T.astype(BF16)
        else:
            out_ref[:, lanes] = o
        stat_ref[0:1, lanes] = top
        stat_ref[1:2, lanes] = total


def second_pass(coef, scale, last, bound_ref, q_ref, g_ref, kv_ref, *refs):
    stat_refs, refs = refs[:NY], refs[NY:]
    if last:
        layout_ref, out_ref, prev_ref, back_hbm, kvgrad_hbm, acc, bias, back_ref, total_ref, sems = refs
    else:
        back_ref, kvgrad_ref, acc, bias = refs
    step = pl.program_id(0)
    plen = kv_ref.shape[0] - DH
    tops = [ref[0:1] for ref in stat_refs]
    top = functools.reduce(jnp.maximum, tops)
    share = [ref[1:2] * jnp.exp2(t - top) for ref, t in zip(stat_refs, tops)]
    inv = 1.0 / sum(share)
    delta = sum(w * ref[2:3] for w, ref in zip(share, stat_refs)) * inv
    row = lax.broadcasted_iota(jnp.int32, (8, ROWS), 0)
    weight = share[0] * inv
    columns = jnp.where(row == 0, top, jnp.where(row == 1, inv, jnp.where(row == 2, delta, weight)))
    columns = jnp.concatenate([columns] * 16, 0).T

    @pl.when(step == 0)
    def _():
        acc[...] = jnp.zeros_like(acc)
        place = lax.broadcasted_iota(jnp.int32, (8, plen), 1)
        bias[...] = jnp.where(place < bound_ref[8:16, 0:1], 0.0, NEG)

    c_top, c_inv, c_delta = columns[:, 0:1], columns[:, 1:2], columns[:, 2:3]
    q = stack_heads(q_ref)
    g = stack_heads(g_ref)
    qt = q.T
    gt = g.T
    slot = lax.broadcasted_iota(jnp.int32, (DH, SLOTS), 0)
    hidden_slots = jnp.where(slot <= bound_ref[0:1], 0.0, NEG).T
    causal = jnp.concatenate([hidden_slots] * HALF, 0)
    chunk = 256
    cuts = [slice(i, i + chunk) for i in range(0, plen, chunk)] + [slice(plen, plen + DH)]

    def products(keys):
        s = lax.dot_general(q, kv_ref[keys, :DH], NT, preferred_element_type=F32)
        return s, lax.dot_general(g, kv_ref[keys, DH:], NT, preferred_element_type=F32)

    def weights(keys, s, dp):
        hidden = bias[0:1, keys] if keys.start < plen else causal
        p = jnp.exp2(s * coef - c_top + hidden) * c_inv
        return p.astype(BF16), (p * (dp - c_delta) * scale).astype(BF16)

    def gradients(keys, p, ds):
        acc[:DH, keys] += jnp.dot(qt, ds, preferred_element_type=F32)
        acc[DH:, keys] += jnp.dot(gt, p, preferred_element_type=F32)
        return jnp.dot(ds, kv_ref[keys, :DH], preferred_element_type=F32)

    dq = jnp.zeros((ROWS, DH), F32)
    following = products(cuts[0])
    for i, keys in enumerate(cuts):
        current = following
        if i + 1 < len(cuts):
            following = products(cuts[i + 1])
        if i:
            dq = dq + gradients(cuts[i - 1], *ready)
        ready = weights(keys, *current)
    dq = dq + gradients(cuts[-1], *ready)
    parts = [slice(h * SLOTS, (h + 1) * SLOTS) for h in range(HALF)]
    if last:
        att = [out_ref[:, r].astype(F32) * columns[r, 3:4] for r in parts]
        grad = [dq[r] + prev_ref[:, r] for r in parts]
        back = jnp.concatenate(att + grad, 1).astype(BF16)

        @pl.when(step == 0)
        def _():
            back_ref[...] = jnp.zeros_like(back_ref)

        def leave(r):
            slots = pl.ds(pl.multiple_of(r * SLOTS, SLOTS), SLOTS)
            return pltpu.make_async_copy(back_ref.at[slots], back_hbm.at[slots], sems.at[r])

        def place(r, _):
            slots = pl.ds(pl.multiple_of(r * SLOTS, SLOTS), SLOTS)
            onehot = one_hot(layout_ref, r, step)
            back_ref[slots] += jnp.dot(onehot, back, preferred_element_type=F32).astype(BF16)

            @pl.when(layout_ref[r + 1] <= (step + 1) * SLOTS)
            def _():
                leave(r).start()

            return 0

        base = N_SEQ + 1 + 2 * step
        lax.fori_loop(layout_ref[base], layout_ref[base + 1], place, 0)
    else:
        for r in parts:
            back_ref[:, r] = dq[r]

    @pl.when(step == pl.num_programs(0) - 1)
    def _():
        if last:
            total_ref[...] = acc[...].T
            copy = pltpu.make_async_copy(total_ref, kvgrad_hbm, sems.at[N_SEQ])
            copy.start()
            for r in range(N_SEQ):
                leave(r).wait()
            copy.wait()
        else:
            kvgrad_ref[...] = acc[...].T.astype(BF16)


def weight_kernel(cuts, place_ref, own_ref, got_ref, prompt_ref, resp_ref, *refs):
    keeps, gives = refs[:NX], refs[NX : 2 * NX]
    prompt_grad_ref, buf, whole, sems = refs[2 * NX :]
    plen = prompt_ref.shape[0]
    wide = prompt_ref.shape[1] // NX
    part = wide // 4
    copies = [
        pltpu.make_async_copy(prompt_ref.at[lo:hi], buf.at[lo:hi], sems.at[n])
        for n, (lo, hi) in enumerate(cuts)
    ]
    copies.append(pltpu.make_async_copy(resp_ref, buf.at[plen:], sems.at[len(cuts)]))
    for copy in copies:
        copy.start()
    x, core = place_ref[0], place_ref[1]
    grad = (own_ref[...] + got_ref[...].astype(F32)).astype(BF16)
    prompt_grad_ref[...] = grad[:plen]
    grad = grad.T
    spans = list(cuts[:-1]) + [(cuts[-1][0], buf.shape[0])]
    swapped = core == 1
    for n, (lo, hi) in enumerate(spans):
        copies[n].wait()
        if n + 1 == len(spans):
            copies[n + 1].wait()
        for k in range(NX):
            cols = pl.ds(pl.multiple_of(lax.rem(x + k, NX) * wide, DH), wide)
            t = jnp.dot(grad[:, lo:hi], buf[lo:hi, cols], preferred_element_type=F32)
            if n:
                t = t + whole[k]
            if n + 1 < len(spans):
                whole[k] = t
                continue
            t = t.T
            for z in range(2):
                low = t[2 * z * part : (2 * z + 1) * part]
                high = t[(2 * z + 1) * part : (2 * z + 2) * part]
                keeps[k][z] = jnp.where(swapped, high, low)
                gives[k][z] = jnp.where(swapped, low, high).astype(BF16)


def finish_kernel(back_ref, attended_ref, query_grad_ref):
    width = back_ref.shape[2] // 2
    for side in range(2):
        total = sum(back_ref[2 * k + side].astype(F32) for k in range(NY)).astype(BF16)
        there = slice(side * width, (side + 1) * width)
        attended_ref[:, there] = total[:, :width]
        query_grad_ref[:, there] = total[:, width:]


def per_device(
    prompt_hidden, resp_hidden, queries, grad_out, kv_weight, prompt_lengths, response_lengths
):
    rank = lax.axis_index(SEQ)
    x = lax.axis_index("x")
    place = jnp.stack([x, lax.axis_index("c")]).astype(jnp.int32)
    slots = resp_hidden.shape[1]
    plen = prompt_hidden.shape[1]
    model = prompt_hidden.shape[2]
    width = queries.shape[2]
    half = width // 2
    scale = DH ** (-0.5)
    coef = scale * LOG2E
    prompt_rows = prompt_hidden[0]
    resp_rows = resp_hidden[0]
    keys = plen + slots
    shard = kv_weight.shape[0]
    smem = pl.BlockSpec(memory_space=pltpu.SMEM)
    vmem = pl.BlockSpec(memory_space=pltpu.VMEM)
    hbm = pl.BlockSpec(memory_space=pltpu.HBM)

    lengths = response_lengths[0]
    live_all = slots * N_SEQ * 5 // 8
    ends = jnp.cumsum(lengths)
    packed = jnp.arange(live_all)
    past = packed[:, None] >= ends[None, :]
    source = packed + jnp.sum(jnp.where(past, slots - lengths[None, :], 0), 1)
    starts = jnp.concatenate([jnp.zeros((1,), jnp.int32), ends.astype(jnp.int32)])
    lows = jnp.arange(live_all // SLOTS)[:, None] * SLOTS
    first = jnp.sum(ends[None, :] <= lows, 1)
    behind = jnp.sum((ends - lengths)[None, :] < lows + SLOTS, 1)
    spans = jnp.stack([first, behind], 1).astype(jnp.int32).reshape(-1)
    layout = jnp.concatenate([starts, spans])

    def bounds(owner):
        offset = source - owner * slots
        limit = jnp.where((offset >= 0) & (offset < slots), offset, -1)
        live = jnp.broadcast_to(prompt_lengths[0] - plen * owner, (8, live_all))
        return jnp.concatenate([jnp.broadcast_to(limit[None, :], (8, live_all)), live], 0).astype(jnp.int32)

    mine, others = bounds(rank), bounds(rank ^ 1)

    block = pl.pallas_call(
        copies_kernel,
        in_specs=[vmem],
        out_specs=vmem,
        out_shape=jax.ShapeDtypeStruct((16,) + kv_weight.shape, BF16),
        compiler_params=params(16),
        name="weight_copies",
    )(kv_weight)
    block = lax.all_to_all(block, PLANE, 0, 0, tiled=True).reshape(2, 8 * shard, 2 * DH)

    qg = pl.pallas_call(
        halves_kernel,
        in_specs=[vmem] * 2,
        out_specs=pl.BlockSpec(memory_space=pl.ANY),
        out_shape=jax.ShapeDtypeStruct((N_SEQ, slots, 2 * half), BF16),
        scratch_shapes=[pltpu.VMEM((2, slots, 2 * half), BF16), pltpu.SemaphoreType.DMA((NY,))],
        compiler_params=params(16),
        cost_estimate=pl.CostEstimate(flops=0, bytes_accessed=8 << 20, transcendentals=0),
        name="query_halves",
    )(queries[0], grad_out[0])
    small = (place, source, layout, mine, others)
    qg, block, small = lax.optimization_barrier((qg, block, small))
    place, source, layout, mine, others = small
    nears = [block] + [lax.ppermute(block, "x", shift(k)) for k in range(1, NX)]
    fars = [lax.ppermute(block, "c", SWAP)]
    qg_all = lax.all_to_all(qg, SEQ, 0, 0, tiled=True).reshape(N_SEQ * slots, 2 * half)

    def project(steps, prev, last):
        count = len(steps)
        return pl.pallas_call(
            functools.partial(project_kernel, steps, prev is None, last),
            in_specs=[smem] + [vmem] * (2 + 2 * count + (prev is not None)),
            out_specs=vmem,
            out_shape=jax.ShapeDtypeStruct((keys, 2 * DH), BF16 if last else F32),
            scratch_shapes=[pltpu.VMEM((count * model // NX, 2 * DH), BF16)],
            compiler_params=params(20),
            cost_estimate=pl.CostEstimate(
                flops=2 * keys * model * DH * count // 2,
                bytes_accessed=keys * model * count // 2,
                transcendentals=0,
            ),
            name="project_last" if last else "project",
        )(
            place, prompt_rows, resp_rows, *[nears[k] for k in steps], *[fars[k] for k in steps],
            *(() if prev is None else (prev,)),
        )

    kv = project((0,), None, False)
    nears[3], kv = lax.optimization_barrier((nears[3], kv))
    fars = fars + [lax.ppermute(piece, "c", SWAP) for piece in nears[1:]]
    kv = project((3,), kv, False)
    kv = project((1, 2), kv, True)
    kv_other = lax.ppermute(kv, "zl", SWAP)

    steps = live_all // SLOTS
    rows = live_all * HALF
    whole = pl.BlockSpec((keys, 2 * DH), lambda i: (0, 0))
    slot_block = pl.BlockSpec((SLOTS, half), lambda i: (i, 0))
    g_block = pl.BlockSpec((SLOTS, half), lambda i: (i, 1))
    lane_block = pl.BlockSpec((DH, ROWS), lambda i: (0, i))
    stat_block = pl.BlockSpec((3, ROWS), lambda i: (0, i))


    def forward(owner, kv, more):
        last = bool(more)
        return pl.pallas_call(
            functools.partial(first_pass, coef, last),
            grid=(steps,),
            in_specs=[pl.BlockSpec((16, SLOTS), lambda i: (0, i)), slot_block, whole]
            + [g_block, lane_block, stat_block] * last,
            out_specs=[slot_block if last else lane_block, stat_block],
            out_shape=[
                jax.ShapeDtypeStruct((live_all, half), BF16)
                if last
                else jax.ShapeDtypeStruct((DH, rows), F32),
                jax.ShapeDtypeStruct((3, rows), F32),
            ],
            scratch_shapes=[pltpu.VMEM((plen, DH), F32), pltpu.VMEM((DH, keys), BF16)],
            compiler_params=params(20),
            cost_estimate=pl.CostEstimate(
                flops=4 * rows * keys * DH, bytes_accessed=4 << 20, transcendentals=rows * keys
            ),
            name="attend_more" if last else "attend_own",
        )(owner, qg, kv, *more)

    pick = (source[:, None] == jnp.arange(N_SEQ * slots)[None, :]).astype(BF16)
    qg = jnp.dot(pick, qg_all, preferred_element_type=F32).astype(BF16)
    state = forward(mine, kv, ())
    out, stat = forward(others, kv_other, (qg, *state))
    stats = [stat] + [lax.ppermute(stat, "y", shift(k)) for k in range(1, NY)]

    def backward(owner, kv, more):
        last = bool(more)
        return pl.pallas_call(
            functools.partial(second_pass, coef, scale, last),
            grid=(steps,),
            in_specs=[
                pl.BlockSpec((16, SLOTS), lambda i: (0, i)), slot_block, g_block, whole,
            ] + [stat_block] * NY + [smem, slot_block, slot_block] * last,
            out_specs=[hbm, hbm] if last else [slot_block, whole],
            out_shape=[
                pltpu.HBM((N_SEQ * slots, 2 * half), BF16),
                pltpu.HBM((keys, 2 * DH), F32),
            ]
            if last
            else [
                jax.ShapeDtypeStruct((live_all, half), F32),
                jax.ShapeDtypeStruct((keys, 2 * DH), BF16),
            ],
            scratch_shapes=[pltpu.VMEM((2 * DH, keys), F32), pltpu.VMEM((8, plen), F32)]
            + [
                pltpu.VMEM((N_SEQ * slots, 2 * half), BF16),
                pltpu.VMEM((keys, 2 * DH), F32),
                pltpu.SemaphoreType.DMA((N_SEQ + 1,)),
            ]
            * last,
            compiler_params=params(20),
            cost_estimate=pl.CostEstimate(
                flops=10 * rows * keys * DH, bytes_accessed=8 << 20, transcendentals=rows * keys
            ),
            name="grads_own" if last else "grads_other",
        )(owner, qg, qg, kv, *stats, *more)

    qgrad_part, kvgrad_other = backward(others, kv_other, ())
    kvgrad_got = lax.ppermute(kvgrad_other, "zl", SWAP)
    back, kvgrad_own = backward(mine, kv, (layout, out, qgrad_part))

    back, kvgrad_own = lax.optimization_barrier((back, kvgrad_own))
    back = lax.all_to_all(back.reshape(N_SEQ, slots, 2 * half), SEQ, 0, 0, tiled=True)

    cuts = ((0, plen // 2), (plen // 2, plen))
    piece = (2, 8 * shard, 2 * DH)
    *pieces, prompt_grad = pl.pallas_call(
        functools.partial(weight_kernel, cuts),
        in_specs=[smem] + [vmem] * 2 + [pl.BlockSpec(memory_space=pltpu.HBM)] * 2,
        out_specs=[vmem] * (2 * NX + 1),
        out_shape=[jax.ShapeDtypeStruct(piece, F32)] * NX
        + [jax.ShapeDtypeStruct(piece, BF16)] * NX
        + [jax.ShapeDtypeStruct((plen, 2 * DH), BF16)],
        scratch_shapes=[
            pltpu.VMEM((keys, model), BF16),
            pltpu.VMEM((NX, 2 * DH, model // NX), F32),
            pltpu.SemaphoreType.DMA((len(cuts) + 1,)),
        ],
        compiler_params=params(50),
        cost_estimate=pl.CostEstimate(
            flops=4 * keys * model * DH, bytes_accessed=2 * keys * model, transcendentals=0
        ),
        name="weight_grad",
    )(place, kvgrad_own, kvgrad_got, prompt_rows, resp_rows)
    keeps, gives = pieces[:NX], pieces[NX:]
    got = [lax.ppermute(give, "c", SWAP) for give in gives]
    line = keeps[0] + got[0].astype(F32)
    for k in range(1, NX):
        piece = (keeps[k] + got[k].astype(F32)).astype(BF16)
        line = line + lax.ppermute(piece, "x", shift(-k)).astype(F32)
    line = line.astype(BF16).reshape(16, shard, 2 * DH)
    line, back = lax.optimization_barrier((line, back))
    shares = lax.all_to_all(line, PLANE, 0, 0, tiled=True)
    weight_grad = jnp.sum(shares.astype(F32), 0)

    attended, query_grad = pl.pallas_call(
        finish_kernel,
        in_specs=[vmem],
        out_specs=[vmem] * 2,
        out_shape=[jax.ShapeDtypeStruct((slots, width), BF16)] * 2,
        compiler_params=params(16),
        name="finish",
    )(back)
    return attended[None], query_grad[None], prompt_grad[None], weight_grad


def solution(mesh):
    fine = Mesh(mesh.devices.reshape(4, 2, 2, 4, 2), AXES)
    return jax.shard_map(
        per_device,
        mesh=fine,
        in_specs=(
            P(GRP, SEQ, None),
            P(GRP, SEQ, None),
            P(GRP, SEQ, None),
            P(GRP, SEQ, None),
            P(AXES, None),
            P(GRP),
            P(GRP, None),
        ),
        out_specs=(
            P(GRP, SEQ, None),
            P(GRP, SEQ, None),
            P(GRP, SEQ, None),
            P(AXES, None),
        ),
        check_vma=False,
    )
```

```python
import functools

import jax
import jax.numpy as jnp
from jax import lax
from jax.experimental import pallas as pl
from jax.experimental.pallas import tpu as pltpu
from jax.sharding import Mesh
from jax.sharding import PartitionSpec as P

AXES = ("x", "zh", "c", "y", "zl")
GRP = ("x", "zh", "c")
SEQ = ("y", "zl")
PLANE = ("zh", "y", "zl")
N_SEQ = 8
NX = 4
NY = 4
HEADS = 8
HALF = 4
DH = 128
SLOTS = 128
ROWS = HALF * SLOTS
NEG = -1e30
LOG2E = 1.4426950408889634
NT = (((1,), (1,)), ((), ()))
TN = (((0,), (0,)), ((), ()))
F32 = jnp.float32
BF16 = jnp.bfloat16
SWAP = [(0, 1), (1, 0)]


def params(mib):
    return pltpu.CompilerParams(vmem_limit_bytes=mib << 20)


def shift(k):
    return [((i + k) % 4, i) for i in range(4)]


def stack_heads(ref):
    return jnp.concatenate([ref[:, h * DH : (h + 1) * DH] for h in range(HALF)], 0)


def copies_kernel(block_ref, out_ref):
    for i in range(out_ref.shape[0]):
        out_ref[i] = block_ref[...]


def halves_kernel(q_ref, g_ref, out_ref, buf, sems):
    half = q_ref.shape[1] // 2
    for side in range(2):
        cols = slice(side * half, (side + 1) * half)
        buf[side, :, :half] = q_ref[:, cols]
        buf[side, :, half:] = g_ref[:, cols]
    copies = [
        pltpu.make_async_copy(buf, out_ref.at[2 * k : 2 * k + 2], sems.at[k]) for k in range(NY)
    ]
    for copy in copies:
        copy.start()
    for copy in copies:
        copy.wait()


def project_kernel(steps, first, last, prompt_ref, resp_ref, *refs):
    refs = list(refs)
    nears = [refs.pop(0) for _ in steps]
    fars = [refs.pop(0) for _ in steps]
    prev_ref = None if first else refs.pop(0)
    kv_ref, weight = refs
    plen = prompt_ref.shape[0]
    wide = prompt_ref.shape[1] // NX
    half = wide // 2
    part = wide // 4
    x, core = lax.axis_index("x"), lax.axis_index("c")
    tops, ends = [], []
    for n, k in enumerate(steps):
        for z in range(2):
            base = n * wide + z * half
            weight[pl.ds(pl.multiple_of(base + core * part, part), part)] = nears[n][z]
            weight[pl.ds(pl.multiple_of(base + (1 - core) * part, part), part)] = fars[n][z]
        cols = pl.ds(pl.multiple_of(lax.rem(x + k, NX) * wide, DH), wide)
        w = weight[n * wide : (n + 1) * wide]
        tops.append(jnp.dot(prompt_ref[:, cols], w, preferred_element_type=F32))
        ends.append(jnp.dot(resp_ref[:, cols], w, preferred_element_type=F32))
    top, end = sum(tops[1:], tops[0]), sum(ends[1:], ends[0])
    if not first:
        top, end = top + prev_ref[:plen], end + prev_ref[plen:]
    kv_ref[:plen] = top.astype(kv_ref.dtype)
    kv_ref[plen:] = end.astype(kv_ref.dtype)


def one_hot(start_ref, r, block):
    row = lax.broadcasted_iota(jnp.int32, (SLOTS, SLOTS), 1) + block * SLOTS
    slot = lax.broadcasted_iota(jnp.int32, (SLOTS, SLOTS), 0) + start_ref[r]
    return jnp.where((row == slot) & (row < start_ref[r + 1]), 1.0, 0.0).astype(BF16)


def first_pass(coef, last, bound_ref, *refs):
    if last:
        q_ref, kv_ref, g_ref, prev_out_ref, prev_stat_ref, out_ref, stat_ref, bias, values = refs
    else:
        q_ref, kv_ref, out_ref, stat_ref, bias, values = refs
    plen = kv_ref.shape[0] - DH

    @pl.when(pl.program_id(0) == 0)
    def _():
        place = lax.broadcasted_iota(jnp.int32, (plen, DH), 0)
        bias[...] = jnp.where(place < bound_ref[8:9], 0.0, NEG)
        values[...] = kv_ref[:, DH:].T

    slot = lax.broadcasted_iota(jnp.int32, (DH, SLOTS), 0)
    causal = jnp.where(slot <= bound_ref[0:1], 0.0, NEG)
    bias_all = jnp.concatenate([bias[...], causal], 0)
    bias_all = jnp.concatenate([bias_all] * 2, 1)
    keys = kv_ref[:, :DH]

    def scores(i):
        q = jnp.concatenate([q_ref[:, h * DH : (h + 1) * DH] for h in (2 * i, 2 * i + 1)], 0)
        return lax.dot_general(keys, q, NT, preferred_element_type=F32)

    following = scores(0)
    for i in range(HALF // 2):
        s = following * coef + bias_all
        if i + 1 < HALF // 2:
            following = scores(i + 1)
        lanes = slice(2 * i * SLOTS, 2 * (i + 1) * SLOTS)
        top = jnp.max(s, 0, keepdims=True)
        if last:
            before = prev_stat_ref[0:1, lanes]
            top = jnp.maximum(top, before)
        p = jnp.exp2(s - top)
        total = jnp.sum(p, 0, keepdims=True)
        o = jnp.dot(values[...], p.astype(BF16), preferred_element_type=F32)
        if last:
            alpha = jnp.exp2(before - top)
            total = total + prev_stat_ref[1:2, lanes] * alpha
            o = (o + prev_out_ref[:, lanes] * alpha) / total
            for j in range(2):
                h = 2 * i + j
                cols = slice(h * DH, (h + 1) * DH)
                part = o[:, j * SLOTS : (j + 1) * SLOTS]
                d = jnp.sum(part * g_ref[:, cols].astype(F32).T, 0, keepdims=True)
                stat_ref[2:3, h * SLOTS : (h + 1) * SLOTS] = d
                out_ref[:, cols] = part.T.astype(BF16)
        else:
            out_ref[:, lanes] = o
        stat_ref[0:1, lanes] = top
        stat_ref[1:2, lanes] = total


def second_pass(coef, scale, last, bound_ref, q_ref, g_ref, kv_ref, *refs):
    stat_refs, refs = refs[:NY], refs[NY:]
    if last:
        layout_hbm, out_ref, prev_ref, back_hbm, kvgrad_hbm = refs[:5]
        acc, bias, back_ref, total_ref, layout_ref, sems = refs[5:]
        bring = pltpu.make_async_copy(layout_hbm, layout_ref, sems.at[N_SEQ + 1])
    else:
        back_ref, kvgrad_ref, acc, bias = refs
    step = pl.program_id(0)
    plen = kv_ref.shape[0] - DH
    tops = [ref[0:1] for ref in stat_refs]
    top = functools.reduce(jnp.maximum, tops)
    share = [ref[1:2] * jnp.exp2(t - top) for ref, t in zip(stat_refs, tops)]
    inv = 1.0 / sum(share)
    delta = sum(w * ref[2:3] for w, ref in zip(share, stat_refs)) * inv
    row = lax.broadcasted_iota(jnp.int32, (8, ROWS), 0)
    weight = share[0] * inv
    columns = jnp.where(row == 0, top, jnp.where(row == 1, inv, jnp.where(row == 2, delta, weight)))
    columns = jnp.concatenate([columns] * 16, 0).T

    @pl.when(step == 0)
    def _():
        if last:
            bring.start()
        acc[...] = jnp.zeros_like(acc)
        place = lax.broadcasted_iota(jnp.int32, (8, plen), 1)
        bias[...] = jnp.where(place < bound_ref[8:16, 0:1], 0.0, NEG)

    c_top, c_inv, c_delta = columns[:, 0:1], columns[:, 1:2], columns[:, 2:3]
    q = stack_heads(q_ref)
    g = stack_heads(g_ref)
    qt = q.T
    gt = g.T
    slot = lax.broadcasted_iota(jnp.int32, (DH, SLOTS), 0)
    hidden_slots = jnp.where(slot <= bound_ref[0:1], 0.0, NEG).T
    causal = jnp.concatenate([hidden_slots] * HALF, 0)
    chunk = 256
    cuts = [slice(i, i + chunk) for i in range(0, plen, chunk)] + [slice(plen, plen + DH)]

    def products(keys):
        s = lax.dot_general(q, kv_ref[keys, :DH], NT, preferred_element_type=F32)
        return s, lax.dot_general(g, kv_ref[keys, DH:], NT, preferred_element_type=F32)

    def weights(keys, s, dp):
        hidden = bias[0:1, keys] if keys.start < plen else causal
        p = jnp.exp2(s * coef - c_top + hidden) * c_inv
        return p.astype(BF16), (p * (dp - c_delta) * scale).astype(BF16)

    def gradients(keys, p, ds):
        acc[:DH, keys] += jnp.dot(qt, ds, preferred_element_type=F32)
        acc[DH:, keys] += jnp.dot(gt, p, preferred_element_type=F32)
        return jnp.dot(ds, kv_ref[keys, :DH], preferred_element_type=F32)

    dq = jnp.zeros((ROWS, DH), F32)
    following = products(cuts[0])
    for i, keys in enumerate(cuts):
        current = following
        if i + 1 < len(cuts):
            following = products(cuts[i + 1])
        if i:
            dq = dq + gradients(cuts[i - 1], *ready)
        ready = weights(keys, *current)
    dq = dq + gradients(cuts[-1], *ready)
    parts = [slice(h * SLOTS, (h + 1) * SLOTS) for h in range(HALF)]
    if last:
        att = [out_ref[:, r].astype(F32) * columns[r, 3:4] for r in parts]
        grad = [dq[r] + prev_ref[:, r] for r in parts]
        back = jnp.concatenate(att + grad, 1).astype(BF16)

        @pl.when(step == 0)
        def _():
            bring.wait()
            back_ref[...] = jnp.zeros_like(back_ref)

        def leave(r):
            slots = pl.ds(pl.multiple_of(r * SLOTS, SLOTS), SLOTS)
            return pltpu.make_async_copy(back_ref.at[slots], back_hbm.at[slots], sems.at[r])

        def place(r, _):
            slots = pl.ds(pl.multiple_of(r * SLOTS, SLOTS), SLOTS)
            onehot = one_hot(layout_ref, r, step)
            back_ref[slots] += jnp.dot(onehot, back, preferred_element_type=F32).astype(BF16)

            @pl.when(layout_ref[r + 1] <= (step + 1) * SLOTS)
            def _():
                leave(r).start()

            return 0

        base = N_SEQ + 1 + 2 * step
        lax.fori_loop(layout_ref[base], layout_ref[base + 1], place, 0)
    else:
        for r in parts:
            back_ref[:, r] = dq[r]

    @pl.when(step == pl.num_programs(0) - 1)
    def _():
        if last:
            total_ref[...] = acc[...].T
            copy = pltpu.make_async_copy(total_ref, kvgrad_hbm, sems.at[N_SEQ])
            copy.start()
            for r in range(N_SEQ):
                leave(r).wait()
            copy.wait()
        else:
            kvgrad_ref[...] = acc[...].T.astype(BF16)


def weight_kernel(cuts, own_ref, got_ref, prompt_ref, resp_ref, *refs):
    keeps, gives = refs[:NX], refs[NX : 2 * NX]
    prompt_grad_ref, buf, whole, sems = refs[2 * NX :]
    plen = prompt_ref.shape[0]
    wide = prompt_ref.shape[1] // NX
    part = wide // 4
    copies = [
        pltpu.make_async_copy(prompt_ref.at[lo:hi], buf.at[lo:hi], sems.at[n])
        for n, (lo, hi) in enumerate(cuts)
    ]
    copies.append(pltpu.make_async_copy(resp_ref, buf.at[plen:], sems.at[len(cuts)]))
    for copy in copies:
        copy.start()
    x, core = lax.axis_index("x"), lax.axis_index("c")
    grad = (own_ref[...] + got_ref[...].astype(F32)).astype(BF16)
    prompt_grad_ref[...] = grad[:plen]
    grad = grad.T
    spans = list(cuts[:-1]) + [(cuts[-1][0], buf.shape[0])]
    swapped = core == 1
    for n, (lo, hi) in enumerate(spans):
        copies[n].wait()
        if n + 1 == len(spans):
            copies[n + 1].wait()
        for k in range(NX):
            cols = pl.ds(pl.multiple_of(lax.rem(x + k, NX) * wide, DH), wide)
            t = jnp.dot(grad[:, lo:hi], buf[lo:hi, cols], preferred_element_type=F32)
            if n:
                t = t + whole[k]
            if n + 1 < len(spans):
                whole[k] = t
                continue
            t = t.T
            for z in range(2):
                low = t[2 * z * part : (2 * z + 1) * part]
                high = t[(2 * z + 1) * part : (2 * z + 2) * part]
                keeps[k][z] = jnp.where(swapped, high, low)
                gives[k][z] = jnp.where(swapped, low, high).astype(BF16)


def finish_kernel(back_ref, attended_ref, query_grad_ref):
    width = back_ref.shape[2] // 2
    for side in range(2):
        total = sum(back_ref[2 * k + side].astype(F32) for k in range(NY)).astype(BF16)
        there = slice(side * width, (side + 1) * width)
        attended_ref[:, there] = total[:, :width]
        query_grad_ref[:, there] = total[:, width:]


def per_device(
    prompt_hidden, resp_hidden, queries, grad_out, kv_weight, prompt_lengths, response_lengths
):
    rank = lax.axis_index(SEQ)
    x = lax.axis_index("x")
    slots = resp_hidden.shape[1]
    plen = prompt_hidden.shape[1]
    model = prompt_hidden.shape[2]
    width = queries.shape[2]
    half = width // 2
    scale = DH ** (-0.5)
    coef = scale * LOG2E
    prompt_rows = prompt_hidden[0]
    resp_rows = resp_hidden[0]
    keys = plen + slots
    shard = kv_weight.shape[0]
    vmem = pl.BlockSpec(memory_space=pltpu.VMEM)
    hbm = pl.BlockSpec(memory_space=pltpu.HBM)

    lengths = response_lengths[0]
    live_all = slots * N_SEQ * 5 // 8
    ends = jnp.cumsum(lengths)
    packed = jnp.arange(live_all)
    past = packed[:, None] >= ends[None, :]
    source = packed + jnp.sum(jnp.where(past, slots - lengths[None, :], 0), 1)
    starts = jnp.concatenate([jnp.zeros((1,), jnp.int32), ends.astype(jnp.int32)])
    lows = jnp.arange(live_all // SLOTS)[:, None] * SLOTS
    first = jnp.sum(ends[None, :] <= lows, 1)
    behind = jnp.sum((ends - lengths)[None, :] < lows + SLOTS, 1)
    spans = jnp.stack([first, behind], 1).astype(jnp.int32).reshape(-1)
    layout = jnp.concatenate([starts, spans])
    layout = jnp.pad(layout, (0, 3 * N_SEQ - layout.shape[0]))

    def bounds(owner):
        offset = source - owner * slots
        limit = jnp.where((offset >= 0) & (offset < slots), offset, -1)
        live = jnp.broadcast_to(prompt_lengths[0] - plen * owner, (8, live_all))
        return jnp.concatenate([jnp.broadcast_to(limit[None, :], (8, live_all)), live], 0).astype(jnp.int32)

    mine, others = bounds(rank), bounds(rank ^ 1)

    block = pl.pallas_call(
        copies_kernel,
        in_specs=[vmem],
        out_specs=vmem,
        out_shape=jax.ShapeDtypeStruct((16,) + kv_weight.shape, BF16),
        compiler_params=params(16),
        name="weight_copies",
    )(kv_weight)
    block = lax.all_to_all(block, PLANE, 0, 0, tiled=True).reshape(2, 8 * shard, 2 * DH)

    qg = pl.pallas_call(
        halves_kernel,
        in_specs=[vmem] * 2,
        out_specs=pl.BlockSpec(memory_space=pl.ANY),
        out_shape=jax.ShapeDtypeStruct((N_SEQ, slots, 2 * half), BF16),
        scratch_shapes=[pltpu.VMEM((2, slots, 2 * half), BF16), pltpu.SemaphoreType.DMA((NY,))],
        compiler_params=params(16),
        cost_estimate=pl.CostEstimate(flops=0, bytes_accessed=8 << 20, transcendentals=0),
        name="query_halves",
    )(queries[0], grad_out[0])
    small = (source, layout, mine, others)
    qg, block, small = lax.optimization_barrier((qg, block, small))
    source, layout, mine, others = small
    nears = [block] + [lax.ppermute(block, "x", shift(k)) for k in range(1, NX)]
    fars = [lax.ppermute(block, "c", SWAP)]
    qg_all = lax.all_to_all(qg, SEQ, 0, 0, tiled=True).reshape(N_SEQ * slots, 2 * half)

    def project(steps, prev, last):
        count = len(steps)
        return pl.pallas_call(
            functools.partial(project_kernel, steps, prev is None, last),
            in_specs=[vmem] * (2 + 2 * count + (prev is not None)),
            out_specs=vmem,
            out_shape=jax.ShapeDtypeStruct((keys, 2 * DH), BF16 if last else F32),
            scratch_shapes=[pltpu.VMEM((count * model // NX, 2 * DH), BF16)],
            compiler_params=params(20),
            cost_estimate=pl.CostEstimate(
                flops=2 * keys * model * DH * count // 2,
                bytes_accessed=keys * model * count // 2,
                transcendentals=0,
            ),
            name="project_last" if last else "project",
        )(
            prompt_rows, resp_rows, *[nears[k] for k in steps], *[fars[k] for k in steps],
            *(() if prev is None else (prev,)),
        )

    kv = project((0,), None, False)
    nears[3], kv = lax.optimization_barrier((nears[3], kv))
    fars = fars + [lax.ppermute(piece, "c", SWAP) for piece in nears[1:]]
    kv = project((3,), kv, False)
    kv = project((1, 2), kv, True)
    kv_other = lax.ppermute(kv, "zl", SWAP)

    steps = live_all // SLOTS
    rows = live_all * HALF
    whole = pl.BlockSpec((keys, 2 * DH), lambda i: (0, 0))
    slot_block = pl.BlockSpec((SLOTS, half), lambda i: (i, 0))
    g_block = pl.BlockSpec((SLOTS, half), lambda i: (i, 1))
    lane_block = pl.BlockSpec((DH, ROWS), lambda i: (0, i))
    stat_block = pl.BlockSpec((3, ROWS), lambda i: (0, i))


    def forward(owner, kv, more):
        last = bool(more)
        return pl.pallas_call(
            functools.partial(first_pass, coef, last),
            grid=(steps,),
            in_specs=[pl.BlockSpec((16, SLOTS), lambda i: (0, i)), slot_block, whole]
            + [g_block, lane_block, stat_block] * last,
            out_specs=[slot_block if last else lane_block, stat_block],
            out_shape=[
                jax.ShapeDtypeStruct((live_all, half), BF16)
                if last
                else jax.ShapeDtypeStruct((DH, rows), F32),
                jax.ShapeDtypeStruct((3, rows), F32),
            ],
            scratch_shapes=[pltpu.VMEM((plen, DH), F32), pltpu.VMEM((DH, keys), BF16)],
            compiler_params=params(20),
            cost_estimate=pl.CostEstimate(
                flops=4 * rows * keys * DH, bytes_accessed=4 << 20, transcendentals=rows * keys
            ),
            name="attend_more" if last else "attend_own",
        )(owner, qg, kv, *more)

    pick = (source[:, None] == jnp.arange(N_SEQ * slots)[None, :]).astype(BF16)
    qg = jnp.dot(pick, qg_all, preferred_element_type=F32).astype(BF16)
    state = forward(mine, kv, ())
    out, stat = forward(others, kv_other, (qg, *state))
    stats = [stat] + [lax.ppermute(stat, "y", shift(k)) for k in range(1, NY)]

    def backward(owner, kv, more):
        last = bool(more)
        return pl.pallas_call(
            functools.partial(second_pass, coef, scale, last),
            grid=(steps,),
            in_specs=[
                pl.BlockSpec((16, SLOTS), lambda i: (0, i)), slot_block, g_block, whole,
            ] + [stat_block] * NY + [hbm, slot_block, slot_block] * last,
            out_specs=[hbm, hbm] if last else [slot_block, whole],
            out_shape=[
                pltpu.HBM((N_SEQ * slots, 2 * half), BF16),
                pltpu.HBM((keys, 2 * DH), F32),
            ]
            if last
            else [
                jax.ShapeDtypeStruct((live_all, half), F32),
                jax.ShapeDtypeStruct((keys, 2 * DH), BF16),
            ],
            scratch_shapes=[pltpu.VMEM((2 * DH, keys), F32), pltpu.VMEM((8, plen), F32)]
            + [
                pltpu.VMEM((N_SEQ * slots, 2 * half), BF16),
                pltpu.VMEM((keys, 2 * DH), F32),
                pltpu.SMEM((3 * N_SEQ,), jnp.int32),
                pltpu.SemaphoreType.DMA((N_SEQ + 2,)),
            ]
            * last,
            compiler_params=params(20),
            cost_estimate=pl.CostEstimate(
                flops=10 * rows * keys * DH, bytes_accessed=8 << 20, transcendentals=rows * keys
            ),
            name="grads_own" if last else "grads_other",
        )(owner, qg, qg, kv, *stats, *more)

    qgrad_part, kvgrad_other = backward(others, kv_other, ())
    kvgrad_got = lax.ppermute(kvgrad_other, "zl", SWAP)
    back, kvgrad_own = backward(mine, kv, (layout, out, qgrad_part))

    back, kvgrad_own = lax.optimization_barrier((back, kvgrad_own))
    back = lax.all_to_all(back.reshape(N_SEQ, slots, 2 * half), SEQ, 0, 0, tiled=True)

    cuts = ((0, plen // 2), (plen // 2, plen))
    piece = (2, 8 * shard, 2 * DH)
    *pieces, prompt_grad = pl.pallas_call(
        functools.partial(weight_kernel, cuts),
        in_specs=[vmem] * 2 + [pl.BlockSpec(memory_space=pltpu.HBM)] * 2,
        out_specs=[vmem] * (2 * NX + 1),
        out_shape=[jax.ShapeDtypeStruct(piece, F32)] * NX
        + [jax.ShapeDtypeStruct(piece, BF16)] * NX
        + [jax.ShapeDtypeStruct((plen, 2 * DH), BF16)],
        scratch_shapes=[
            pltpu.VMEM((keys, model), BF16),
            pltpu.VMEM((NX, 2 * DH, model // NX), F32),
            pltpu.SemaphoreType.DMA((len(cuts) + 1,)),
        ],
        compiler_params=params(50),
        cost_estimate=pl.CostEstimate(
            flops=4 * keys * model * DH, bytes_accessed=2 * keys * model, transcendentals=0
        ),
        name="weight_grad",
    )(kvgrad_own, kvgrad_got, prompt_rows, resp_rows)
    keeps, gives = pieces[:NX], pieces[NX:]
    got = [lax.ppermute(give, "c", SWAP) for give in gives]
    line = keeps[0] + got[0].astype(F32)
    for k in range(1, NX):
        piece = (keeps[k] + got[k].astype(F32)).astype(BF16)
        line = line + lax.ppermute(piece, "x", shift(-k)).astype(F32)
    line = line.astype(BF16).reshape(16, shard, 2 * DH)
    line, back = lax.optimization_barrier((line, back))
    shares = lax.all_to_all(line, PLANE, 0, 0, tiled=True)
    weight_grad = jnp.sum(shares.astype(F32), 0)

    attended, query_grad = pl.pallas_call(
        finish_kernel,
        in_specs=[vmem],
        out_specs=[vmem] * 2,
        out_shape=[jax.ShapeDtypeStruct((slots, width), BF16)] * 2,
        compiler_params=params(16),
        name="finish",
    )(back)
    return attended[None], query_grad[None], prompt_grad[None], weight_grad


def solution(mesh):
    fine = Mesh(mesh.devices.reshape(4, 2, 2, 4, 2), AXES)
    return jax.shard_map(
        per_device,
        mesh=fine,
        in_specs=(
            P(GRP, SEQ, None),
            P(GRP, SEQ, None),
            P(GRP, SEQ, None),
            P(GRP, SEQ, None),
            P(AXES, None),
            P(GRP),
            P(GRP, None),
        ),
        out_specs=(
            P(GRP, SEQ, None),
            P(GRP, SEQ, None),
            P(GRP, SEQ, None),
            P(AXES, None),
        ),
        check_vma=False,
    )
```

```python
import functools

import jax
import jax.numpy as jnp
from jax import lax
from jax.experimental import pallas as pl
from jax.experimental.pallas import tpu as pltpu
from jax.sharding import Mesh
from jax.sharding import PartitionSpec as P

AXES = ("x", "zh", "c", "y", "zl")
GRP = ("x", "zh", "c")
SEQ = ("y", "zl")
PLANE = ("zh", "y", "zl")
N_SEQ = 8
NX = 4
NY = 4
HEADS = 8
HALF = 4
DH = 128
SLOTS = 128
ROWS = HALF * SLOTS
NEG = -1e30
LOG2E = 1.4426950408889634
NT = (((1,), (1,)), ((), ()))
TN = (((0,), (0,)), ((), ()))
F32 = jnp.float32
BF16 = jnp.bfloat16
SWAP = [(0, 1), (1, 0)]


def params(mib):
    return pltpu.CompilerParams(vmem_limit_bytes=mib << 20)


def shift(k):
    return [((i + k) % 4, i) for i in range(4)]


def stack_heads(ref):
    return jnp.concatenate([ref[:, h * DH : (h + 1) * DH] for h in range(HALF)], 0)


def copies_kernel(block_ref, out_ref):
    for i in range(out_ref.shape[0]):
        out_ref[i] = block_ref[...]


def halves_kernel(q_ref, g_ref, out_ref, buf, sems):
    half = q_ref.shape[1] // 2
    for side in range(2):
        cols = slice(side * half, (side + 1) * half)
        buf[side, :, :half] = q_ref[:, cols]
        buf[side, :, half:] = g_ref[:, cols]
    copies = [
        pltpu.make_async_copy(buf, out_ref.at[2 * k : 2 * k + 2], sems.at[k]) for k in range(NY)
    ]
    for copy in copies:
        copy.start()
    for copy in copies:
        copy.wait()


def project_kernel(steps, first, last, prompt_ref, resp_ref, *refs):
    refs = list(refs)
    nears = [refs.pop(0) for _ in steps]
    fars = [refs.pop(0) for _ in steps]
    prev_ref = None if first else refs.pop(0)
    kv_ref, weight = refs
    plen = prompt_ref.shape[0]
    wide = prompt_ref.shape[1] // NX
    half = wide // 2
    part = wide // 4
    x, core = lax.axis_index("x"), lax.axis_index("c")
    tops, ends = [], []
    for n, k in enumerate(steps):
        for z in range(2):
            base = n * wide + z * half
            weight[pl.ds(pl.multiple_of(base + core * part, part), part)] = nears[n][z]
            weight[pl.ds(pl.multiple_of(base + (1 - core) * part, part), part)] = fars[n][z]
        cols = pl.ds(pl.multiple_of(lax.rem(x + k, NX) * wide, DH), wide)
        w = weight[n * wide : (n + 1) * wide]
        tops.append(jnp.dot(prompt_ref[:, cols], w, preferred_element_type=F32))
        ends.append(jnp.dot(resp_ref[:, cols], w, preferred_element_type=F32))
    top, end = sum(tops[1:], tops[0]), sum(ends[1:], ends[0])
    if not first:
        top, end = top + prev_ref[:plen], end + prev_ref[plen:]
    kv_ref[:plen] = top.astype(kv_ref.dtype)
    kv_ref[plen:] = end.astype(kv_ref.dtype)


def one_hot(start_ref, r, block):
    row = lax.broadcasted_iota(jnp.int32, (SLOTS, SLOTS), 1) + block * SLOTS
    slot = lax.broadcasted_iota(jnp.int32, (SLOTS, SLOTS), 0) + start_ref[r]
    return jnp.where((row == slot) & (row < start_ref[r + 1]), 1.0, 0.0).astype(BF16)


def first_pass(coef, last, bound_ref, *refs):
    if last:
        q_ref, kv_ref, g_ref, prev_out_ref, prev_stat_ref, out_ref, stat_ref, bias, values = refs
    else:
        q_ref, kv_ref, out_ref, stat_ref, bias, values = refs
    plen = kv_ref.shape[0] - DH

    @pl.when(pl.program_id(0) == 0)
    def _():
        place = lax.broadcasted_iota(jnp.int32, (plen, DH), 0)
        bias[...] = jnp.where(place < bound_ref[8:9], 0.0, NEG)
        values[...] = kv_ref[:, DH:].T

    slot = lax.broadcasted_iota(jnp.int32, (DH, SLOTS), 0)
    causal = jnp.where(slot <= bound_ref[0:1], 0.0, NEG)
    bias_all = jnp.concatenate([bias[...], causal], 0)
    bias_all = jnp.concatenate([bias_all] * 2, 1)
    keys = kv_ref[:, :DH]

    def scores(i):
        q = jnp.concatenate([q_ref[:, h * DH : (h + 1) * DH] for h in (2 * i, 2 * i + 1)], 0)
        return lax.dot_general(keys, q, NT, preferred_element_type=F32)

    following = scores(0)
    for i in range(HALF // 2):
        s = following * coef + bias_all
        if i + 1 < HALF // 2:
            following = scores(i + 1)
        lanes = slice(2 * i * SLOTS, 2 * (i + 1) * SLOTS)
        top = jnp.max(s, 0, keepdims=True)
        if last:
            before = prev_stat_ref[0:1, lanes]
            top = jnp.maximum(top, before)
        p = jnp.exp2(s - top)
        total = jnp.sum(p, 0, keepdims=True)
        o = jnp.dot(values[...], p.astype(BF16), preferred_element_type=F32)
        if last:
            alpha = jnp.exp2(before - top)
            total = total + prev_stat_ref[1:2, lanes] * alpha
            o = (o + prev_out_ref[:, lanes] * alpha) / total
            for j in range(2):
                h = 2 * i + j
                cols = slice(h * DH, (h + 1) * DH)
                part = o[:, j * SLOTS : (j + 1) * SLOTS]
                d = jnp.sum(part * g_ref[:, cols].astype(F32).T, 0, keepdims=True)
                stat_ref[2:3, h * SLOTS : (h + 1) * SLOTS] = d
                out_ref[:, cols] = part.T.astype(BF16)
        else:
            out_ref[:, lanes] = o
        stat_ref[0:1, lanes] = top
        stat_ref[1:2, lanes] = total


def second_pass(coef, scale, last, bound_ref, q_ref, g_ref, kv_ref, *refs):
    stat_refs, refs = refs[:NY], refs[NY:]
    if last:
        layout_hbm, out_ref, prev_ref, back_hbm, kvgrad_hbm = refs[:5]
        acc, bias, back_ref, layout_ref, sems = refs[5:]
        bring = pltpu.make_async_copy(layout_hbm, layout_ref, sems.at[N_SEQ + 1])
    else:
        back_ref, kvgrad_ref, acc, bias = refs
    step = pl.program_id(0)
    plen = kv_ref.shape[0] - DH
    tops = [ref[0:1] for ref in stat_refs]
    top = functools.reduce(jnp.maximum, tops)
    share = [ref[1:2] * jnp.exp2(t - top) for ref, t in zip(stat_refs, tops)]
    inv = 1.0 / sum(share)
    delta = sum(w * ref[2:3] for w, ref in zip(share, stat_refs)) * inv
    row = lax.broadcasted_iota(jnp.int32, (8, ROWS), 0)
    weight = share[0] * inv
    columns = jnp.where(row == 0, top, jnp.where(row == 1, inv, jnp.where(row == 2, delta, weight)))
    columns = jnp.concatenate([columns] * 16, 0).T

    @pl.when(step == 0)
    def _():
        if last:
            bring.start()
        acc[...] = jnp.zeros_like(acc)
        place = lax.broadcasted_iota(jnp.int32, (8, plen), 1)
        bias[...] = jnp.where(place < bound_ref[8:16, 0:1], 0.0, NEG)

    c_top, c_inv, c_delta = columns[:, 0:1], columns[:, 1:2], columns[:, 2:3]
    q = stack_heads(q_ref)
    g = stack_heads(g_ref)
    qt = q.T
    gt = g.T
    slot = lax.broadcasted_iota(jnp.int32, (DH, SLOTS), 0)
    hidden_slots = jnp.where(slot <= bound_ref[0:1], 0.0, NEG).T
    causal = jnp.concatenate([hidden_slots] * HALF, 0)
    chunk = 256
    cuts = [slice(i, i + chunk) for i in range(0, plen, chunk)] + [slice(plen, plen + DH)]

    def products(keys):
        s = lax.dot_general(q, kv_ref[keys, :DH], NT, preferred_element_type=F32)
        return s, lax.dot_general(g, kv_ref[keys, DH:], NT, preferred_element_type=F32)

    def weights(keys, s, dp):
        hidden = bias[0:1, keys] if keys.start < plen else causal
        p = jnp.exp2(s * coef - c_top + hidden) * c_inv
        return p.astype(BF16), (p * (dp - c_delta) * scale).astype(BF16)

    def gradients(keys, p, ds):
        acc[:DH, keys] += jnp.dot(qt, ds, preferred_element_type=F32)
        acc[DH:, keys] += jnp.dot(gt, p, preferred_element_type=F32)
        return jnp.dot(ds, kv_ref[keys, :DH], preferred_element_type=F32)

    dq = jnp.zeros((ROWS, DH), F32)
    following = products(cuts[0])
    for i, keys in enumerate(cuts):
        current = following
        if i + 1 < len(cuts):
            following = products(cuts[i + 1])
        if i:
            dq = dq + gradients(cuts[i - 1], *ready)
        ready = weights(keys, *current)
    dq = dq + gradients(cuts[-1], *ready)
    parts = [slice(h * SLOTS, (h + 1) * SLOTS) for h in range(HALF)]
    if last:
        att = [out_ref[:, r].astype(F32) * columns[r, 3:4] for r in parts]
        grad = [dq[r] + prev_ref[:, r] for r in parts]
        back = jnp.concatenate(att + grad, 1).astype(BF16)

        @pl.when(step == 0)
        def _():
            bring.wait()
            back_ref[...] = jnp.zeros_like(back_ref)

        def leave(r):
            slots = pl.ds(pl.multiple_of(r * SLOTS, SLOTS), SLOTS)
            return pltpu.make_async_copy(back_ref.at[slots], back_hbm.at[slots], sems.at[r])

        def place(r, _):
            slots = pl.ds(pl.multiple_of(r * SLOTS, SLOTS), SLOTS)
            onehot = one_hot(layout_ref, r, step)
            back_ref[slots] += jnp.dot(onehot, back, preferred_element_type=F32).astype(BF16)

            @pl.when(layout_ref[r + 1] <= (step + 1) * SLOTS)
            def _():
                leave(r).start()

            return 0

        base = N_SEQ + 1 + 2 * step
        lax.fori_loop(layout_ref[base], layout_ref[base + 1], place, 0)
    else:
        for r in parts:
            back_ref[:, r] = dq[r]

    @pl.when(step == pl.num_programs(0) - 1)
    def _():
        if last:
            copy = pltpu.make_async_copy(acc, kvgrad_hbm, sems.at[N_SEQ])
            copy.start()
            for r in range(N_SEQ):
                leave(r).wait()
            copy.wait()
        else:
            kvgrad_ref[...] = acc[...].astype(BF16)


def weight_kernel(cuts, own_ref, got_ref, prompt_ref, resp_ref, *refs):
    keeps, gives = refs[:NX], refs[NX : 2 * NX]
    prompt_grad_ref, buf, whole, sems = refs[2 * NX :]
    plen = prompt_ref.shape[0]
    wide = prompt_ref.shape[1] // NX
    part = wide // 4
    copies = [
        pltpu.make_async_copy(prompt_ref.at[lo:hi], buf.at[lo:hi], sems.at[n])
        for n, (lo, hi) in enumerate(cuts)
    ]
    copies.append(pltpu.make_async_copy(resp_ref, buf.at[plen:], sems.at[len(cuts)]))
    for copy in copies:
        copy.start()
    x, core = lax.axis_index("x"), lax.axis_index("c")
    grad = (own_ref[...] + got_ref[...].astype(F32)).astype(BF16)
    prompt_grad_ref[...] = grad[:, :plen].T
    spans = list(cuts[:-1]) + [(cuts[-1][0], buf.shape[0])]
    swapped = core == 1
    for n, (lo, hi) in enumerate(spans):
        copies[n].wait()
        if n + 1 == len(spans):
            copies[n + 1].wait()
        for k in range(NX):
            cols = pl.ds(pl.multiple_of(lax.rem(x + k, NX) * wide, DH), wide)
            t = jnp.dot(grad[:, lo:hi], buf[lo:hi, cols], preferred_element_type=F32)
            if n:
                t = t + whole[k]
            if n + 1 < len(spans):
                whole[k] = t
                continue
            t = t.T
            for z in range(2):
                low = t[2 * z * part : (2 * z + 1) * part]
                high = t[(2 * z + 1) * part : (2 * z + 2) * part]
                keeps[k][z] = jnp.where(swapped, high, low)
                gives[k][z] = jnp.where(swapped, low, high).astype(BF16)


def finish_kernel(back_ref, attended_ref, query_grad_ref):
    width = back_ref.shape[2] // 2
    for side in range(2):
        total = sum(back_ref[2 * k + side].astype(F32) for k in range(NY)).astype(BF16)
        there = slice(side * width, (side + 1) * width)
        attended_ref[:, there] = total[:, :width]
        query_grad_ref[:, there] = total[:, width:]


def per_device(
    prompt_hidden, resp_hidden, queries, grad_out, kv_weight, prompt_lengths, response_lengths
):
    rank = lax.axis_index(SEQ)
    x = lax.axis_index("x")
    slots = resp_hidden.shape[1]
    plen = prompt_hidden.shape[1]
    model = prompt_hidden.shape[2]
    width = queries.shape[2]
    half = width // 2
    scale = DH ** (-0.5)
    coef = scale * LOG2E
    prompt_rows = prompt_hidden[0]
    resp_rows = resp_hidden[0]
    keys = plen + slots
    shard = kv_weight.shape[0]
    vmem = pl.BlockSpec(memory_space=pltpu.VMEM)
    hbm = pl.BlockSpec(memory_space=pltpu.HBM)

    lengths = response_lengths[0]
    live_all = slots * N_SEQ * 5 // 8
    ends = jnp.cumsum(lengths)
    packed = jnp.arange(live_all)
    past = packed[:, None] >= ends[None, :]
    source = packed + jnp.sum(jnp.where(past, slots - lengths[None, :], 0), 1)
    starts = jnp.concatenate([jnp.zeros((1,), jnp.int32), ends.astype(jnp.int32)])
    lows = jnp.arange(live_all // SLOTS)[:, None] * SLOTS
    first = jnp.sum(ends[None, :] <= lows, 1)
    behind = jnp.sum((ends - lengths)[None, :] < lows + SLOTS, 1)
    spans = jnp.stack([first, behind], 1).astype(jnp.int32).reshape(-1)
    layout = jnp.concatenate([starts, spans])
    layout = jnp.pad(layout, (0, 3 * N_SEQ - layout.shape[0]))

    def bounds(owner):
        offset = source - owner * slots
        limit = jnp.where((offset >= 0) & (offset < slots), offset, -1)
        live = jnp.broadcast_to(prompt_lengths[0] - plen * owner, (8, live_all))
        return jnp.concatenate([jnp.broadcast_to(limit[None, :], (8, live_all)), live], 0).astype(jnp.int32)

    mine, others = bounds(rank), bounds(rank ^ 1)

    block = pl.pallas_call(
        copies_kernel,
        in_specs=[vmem],
        out_specs=vmem,
        out_shape=jax.ShapeDtypeStruct((16,) + kv_weight.shape, BF16),
        compiler_params=params(16),
        name="weight_copies",
    )(kv_weight)
    block = lax.all_to_all(block, PLANE, 0, 0, tiled=True).reshape(2, 8 * shard, 2 * DH)

    qg = pl.pallas_call(
        halves_kernel,
        in_specs=[vmem] * 2,
        out_specs=pl.BlockSpec(memory_space=pl.ANY),
        out_shape=jax.ShapeDtypeStruct((N_SEQ, slots, 2 * half), BF16),
        scratch_shapes=[pltpu.VMEM((2, slots, 2 * half), BF16), pltpu.SemaphoreType.DMA((NY,))],
        compiler_params=params(16),
        cost_estimate=pl.CostEstimate(flops=0, bytes_accessed=8 << 20, transcendentals=0),
        name="query_halves",
    )(queries[0], grad_out[0])
    small = (source, layout, mine, others)
    qg, block, small = lax.optimization_barrier((qg, block, small))
    source, layout, mine, others = small
    nears = [block] + [lax.ppermute(block, "x", shift(k)) for k in range(1, NX)]
    fars = [lax.ppermute(block, "c", SWAP)]
    qg_all = lax.all_to_all(qg, SEQ, 0, 0, tiled=True).reshape(N_SEQ * slots, 2 * half)

    def project(steps, prev, last):
        count = len(steps)
        return pl.pallas_call(
            functools.partial(project_kernel, steps, prev is None, last),
            in_specs=[vmem] * (2 + 2 * count + (prev is not None)),
            out_specs=vmem,
            out_shape=jax.ShapeDtypeStruct((keys, 2 * DH), BF16 if last else F32),
            scratch_shapes=[pltpu.VMEM((count * model // NX, 2 * DH), BF16)],
            compiler_params=params(20),
            cost_estimate=pl.CostEstimate(
                flops=2 * keys * model * DH * count // 2,
                bytes_accessed=keys * model * count // 2,
                transcendentals=0,
            ),
            name="project_last" if last else "project",
        )(
            prompt_rows, resp_rows, *[nears[k] for k in steps], *[fars[k] for k in steps],
            *(() if prev is None else (prev,)),
        )

    kv = project((0,), None, False)
    nears[3], kv = lax.optimization_barrier((nears[3], kv))
    fars = fars + [lax.ppermute(piece, "c", SWAP) for piece in nears[1:]]
    kv = project((3,), kv, False)
    kv = project((1, 2), kv, True)
    kv_other = lax.ppermute(kv, "zl", SWAP)

    steps = live_all // SLOTS
    rows = live_all * HALF
    whole = pl.BlockSpec((keys, 2 * DH), lambda i: (0, 0))
    slot_block = pl.BlockSpec((SLOTS, half), lambda i: (i, 0))
    g_block = pl.BlockSpec((SLOTS, half), lambda i: (i, 1))
    lane_block = pl.BlockSpec((DH, ROWS), lambda i: (0, i))
    stat_block = pl.BlockSpec((3, ROWS), lambda i: (0, i))


    def forward(owner, kv, more):
        last = bool(more)
        return pl.pallas_call(
            functools.partial(first_pass, coef, last),
            grid=(steps,),
            in_specs=[pl.BlockSpec((16, SLOTS), lambda i: (0, i)), slot_block, whole]
            + [g_block, lane_block, stat_block] * last,
            out_specs=[slot_block if last else lane_block, stat_block],
            out_shape=[
                jax.ShapeDtypeStruct((live_all, half), BF16)
                if last
                else jax.ShapeDtypeStruct((DH, rows), F32),
                jax.ShapeDtypeStruct((3, rows), F32),
            ],
            scratch_shapes=[pltpu.VMEM((plen, DH), F32), pltpu.VMEM((DH, keys), BF16)],
            compiler_params=params(20),
            cost_estimate=pl.CostEstimate(
                flops=4 * rows * keys * DH, bytes_accessed=4 << 20, transcendentals=rows * keys
            ),
            name="attend_more" if last else "attend_own",
        )(owner, qg, kv, *more)

    pick = (source[:, None] == jnp.arange(N_SEQ * slots)[None, :]).astype(BF16)
    qg = jnp.dot(pick, qg_all, preferred_element_type=F32).astype(BF16)
    state = forward(mine, kv, ())
    out, stat = forward(others, kv_other, (qg, *state))
    stats = [stat] + [lax.ppermute(stat, "y", shift(k)) for k in range(1, NY)]

    def backward(owner, kv, more):
        last = bool(more)
        return pl.pallas_call(
            functools.partial(second_pass, coef, scale, last),
            grid=(steps,),
            in_specs=[
                pl.BlockSpec((16, SLOTS), lambda i: (0, i)), slot_block, g_block, whole,
            ] + [stat_block] * NY + [hbm, slot_block, slot_block] * last,
            out_specs=[hbm, hbm]
            if last
            else [slot_block, pl.BlockSpec((2 * DH, keys), lambda i: (0, 0))],
            out_shape=[
                pltpu.HBM((N_SEQ * slots, 2 * half), BF16),
                pltpu.HBM((2 * DH, keys), F32),
            ]
            if last
            else [
                jax.ShapeDtypeStruct((live_all, half), F32),
                jax.ShapeDtypeStruct((2 * DH, keys), BF16),
            ],
            scratch_shapes=[pltpu.VMEM((2 * DH, keys), F32), pltpu.VMEM((8, plen), F32)]
            + [
                pltpu.VMEM((N_SEQ * slots, 2 * half), BF16),
                pltpu.SMEM((3 * N_SEQ,), jnp.int32),
                pltpu.SemaphoreType.DMA((N_SEQ + 2,)),
            ]
            * last,
            compiler_params=params(20),
            cost_estimate=pl.CostEstimate(
                flops=10 * rows * keys * DH, bytes_accessed=8 << 20, transcendentals=rows * keys
            ),
            name="grads_own" if last else "grads_other",
        )(owner, qg, qg, kv, *stats, *more)

    qgrad_part, kvgrad_other = backward(others, kv_other, ())
    kvgrad_got = lax.ppermute(kvgrad_other, "zl", SWAP)
    back, kvgrad_own = backward(mine, kv, (layout, out, qgrad_part))

    back, kvgrad_own = lax.optimization_barrier((back, kvgrad_own))
    back = lax.all_to_all(back.reshape(N_SEQ, slots, 2 * half), SEQ, 0, 0, tiled=True)

    cuts = ((0, plen // 2), (plen // 2, plen))
    piece = (2, 8 * shard, 2 * DH)
    *pieces, prompt_grad = pl.pallas_call(
        functools.partial(weight_kernel, cuts),
        in_specs=[vmem] * 2 + [pl.BlockSpec(memory_space=pltpu.HBM)] * 2,
        out_specs=[vmem] * (2 * NX + 1),
        out_shape=[jax.ShapeDtypeStruct(piece, F32)] * NX
        + [jax.ShapeDtypeStruct(piece, BF16)] * NX
        + [jax.ShapeDtypeStruct((plen, 2 * DH), BF16)],
        scratch_shapes=[
            pltpu.VMEM((keys, model), BF16),
            pltpu.VMEM((NX, 2 * DH, model // NX), F32),
            pltpu.SemaphoreType.DMA((len(cuts) + 1,)),
        ],
        compiler_params=params(50),
        cost_estimate=pl.CostEstimate(
            flops=4 * keys * model * DH, bytes_accessed=2 * keys * model, transcendentals=0
        ),
        name="weight_grad",
    )(kvgrad_own, kvgrad_got, prompt_rows, resp_rows)
    keeps, gives = pieces[:NX], pieces[NX:]
    got = [lax.ppermute(give, "c", SWAP) for give in gives]
    line = keeps[0] + got[0].astype(F32)
    for k in range(1, NX):
        piece = (keeps[k] + got[k].astype(F32)).astype(BF16)
        line = line + lax.ppermute(piece, "x", shift(-k)).astype(F32)
    line = line.astype(BF16).reshape(16, shard, 2 * DH)
    line, back = lax.optimization_barrier((line, back))
    shares = lax.all_to_all(line, PLANE, 0, 0, tiled=True)
    weight_grad = jnp.sum(shares.astype(F32), 0)

    attended, query_grad = pl.pallas_call(
        finish_kernel,
        in_specs=[vmem],
        out_specs=[vmem] * 2,
        out_shape=[jax.ShapeDtypeStruct((slots, width), BF16)] * 2,
        compiler_params=params(16),
        name="finish",
    )(back)
    return attended[None], query_grad[None], prompt_grad[None], weight_grad


def solution(mesh):
    fine = Mesh(mesh.devices.reshape(4, 2, 2, 4, 2), AXES)
    return jax.shard_map(
        per_device,
        mesh=fine,
        in_specs=(
            P(GRP, SEQ, None),
            P(GRP, SEQ, None),
            P(GRP, SEQ, None),
            P(GRP, SEQ, None),
            P(AXES, None),
            P(GRP),
            P(GRP, None),
        ),
        out_specs=(
            P(GRP, SEQ, None),
            P(GRP, SEQ, None),
            P(GRP, SEQ, None),
            P(AXES, None),
        ),
        check_vma=False,
    )
```

```python
import functools

import jax
import jax.numpy as jnp
from jax import lax
from jax.experimental import pallas as pl
from jax.experimental.pallas import tpu as pltpu
from jax.sharding import Mesh
from jax.sharding import PartitionSpec as P

AXES = ("x", "zh", "c", "y", "zl")
GRP = ("x", "zh", "c")
SEQ = ("y", "zl")
PLANE = ("zh", "y", "zl")
N_SEQ = 8
NX = 4
NY = 4
HEADS = 8
HALF = 4
DH = 128
SLOTS = 128
ROWS = HALF * SLOTS
NEG = -1e30
LOG2E = 1.4426950408889634
NT = (((1,), (1,)), ((), ()))
TN = (((0,), (0,)), ((), ()))
F32 = jnp.float32
BF16 = jnp.bfloat16
SWAP = [(0, 1), (1, 0)]


def params(mib):
    return pltpu.CompilerParams(vmem_limit_bytes=mib << 20)


def shift(k):
    return [((i + k) % 4, i) for i in range(4)]


def stack_heads(ref):
    return jnp.concatenate([ref[:, h * DH : (h + 1) * DH] for h in range(HALF)], 0)


def copies_kernel(block_ref, out_ref):
    for i in range(out_ref.shape[0]):
        out_ref[i] = block_ref[...]


def halves_kernel(q_ref, g_ref, out_ref, buf, sems):
    half = q_ref.shape[1] // 2
    for side in range(2):
        cols = slice(side * half, (side + 1) * half)
        buf[side, :, :half] = q_ref[:, cols]
        buf[side, :, half:] = g_ref[:, cols]
    copies = [
        pltpu.make_async_copy(buf, out_ref.at[2 * k : 2 * k + 2], sems.at[k]) for k in range(NY)
    ]
    for copy in copies:
        copy.start()
    for copy in copies:
        copy.wait()


def project_kernel(steps, first, last, prompt_ref, resp_ref, *refs):
    refs = list(refs)
    nears = [refs.pop(0) for _ in steps]
    fars = [refs.pop(0) for _ in steps]
    prev_ref = None if first else refs.pop(0)
    kv_ref, weight = refs
    plen = prompt_ref.shape[0]
    wide = prompt_ref.shape[1] // NX
    half = wide // 2
    part = wide // 4
    x, core = lax.axis_index("x"), lax.axis_index("c")
    tops, ends = [], []
    for n, k in enumerate(steps):
        for z in range(2):
            base = n * wide + z * half
            weight[pl.ds(pl.multiple_of(base + core * part, part), part)] = nears[n][z]
            weight[pl.ds(pl.multiple_of(base + (1 - core) * part, part), part)] = fars[n][z]
        cols = pl.ds(pl.multiple_of(lax.rem(x + k, NX) * wide, DH), wide)
        w = weight[n * wide : (n + 1) * wide]
        tops.append(jnp.dot(prompt_ref[:, cols], w, preferred_element_type=F32))
        ends.append(jnp.dot(resp_ref[:, cols], w, preferred_element_type=F32))
    top, end = sum(tops[1:], tops[0]), sum(ends[1:], ends[0])
    if not first:
        top, end = top + prev_ref[:plen], end + prev_ref[plen:]
    kv_ref[:plen] = top.astype(kv_ref.dtype)
    kv_ref[plen:] = end.astype(kv_ref.dtype)


def one_hot(start_ref, r, block):
    row = lax.broadcasted_iota(jnp.int32, (SLOTS, SLOTS), 1) + block * SLOTS
    slot = lax.broadcasted_iota(jnp.int32, (SLOTS, SLOTS), 0) + start_ref[r]
    return jnp.where((row == slot) & (row < start_ref[r + 1]), 1.0, 0.0).astype(BF16)


def first_pass(coef, last, bound_ref, *refs):
    if last:
        q_ref, kv_ref, g_ref, prev_out_ref, prev_stat_ref, out_ref, stat_ref, bias, values = refs
    else:
        q_ref, kv_ref, out_ref, stat_ref, bias, values = refs
    plen = kv_ref.shape[0] - DH

    @pl.when(pl.program_id(0) == 0)
    def _():
        place = lax.broadcasted_iota(jnp.int32, (plen, DH), 0)
        bias[...] = jnp.where(place < bound_ref[8:9], 0.0, NEG)
        values[...] = kv_ref[:, DH:].T

    slot = lax.broadcasted_iota(jnp.int32, (DH, SLOTS), 0)
    causal = jnp.where(slot <= bound_ref[0:1], 0.0, NEG)
    bias_all = jnp.concatenate([bias[...], causal], 0)
    bias_all = jnp.concatenate([bias_all] * 2, 1)
    keys = kv_ref[:, :DH]

    def scores(i):
        q = jnp.concatenate([q_ref[:, h * DH : (h + 1) * DH] for h in (2 * i, 2 * i + 1)], 0)
        return lax.dot_general(keys, q, NT, preferred_element_type=F32)

    following = scores(0)
    for i in range(HALF // 2):
        s = following * coef + bias_all
        if i + 1 < HALF // 2:
            following = scores(i + 1)
        lanes = slice(2 * i * SLOTS, 2 * (i + 1) * SLOTS)
        top = jnp.max(s, 0, keepdims=True)
        if last:
            before = prev_stat_ref[0:1, lanes]
            top = jnp.maximum(top, before)
        p = jnp.exp2(s - top)
        total = jnp.sum(p, 0, keepdims=True)
        o = jnp.dot(values[...], p.astype(BF16), preferred_element_type=F32)
        if last:
            alpha = jnp.exp2(before - top)
            total = total + prev_stat_ref[1:2, lanes] * alpha
            o = (o + prev_out_ref[:, lanes] * alpha) / total
            for j in range(2):
                h = 2 * i + j
                cols = slice(h * DH, (h + 1) * DH)
                part = o[:, j * SLOTS : (j + 1) * SLOTS]
                d = jnp.sum(part * g_ref[:, cols].astype(F32).T, 0, keepdims=True)
                stat_ref[2:3, h * SLOTS : (h + 1) * SLOTS] = d
                out_ref[:, cols] = part.T.astype(BF16)
        else:
            out_ref[:, lanes] = o
        stat_ref[0:1, lanes] = top
        stat_ref[1:2, lanes] = total


def second_pass(coef, scale, last, bound_ref, q_ref, g_ref, kv_ref, *refs):
    stat_refs, refs = refs[:NY], refs[NY:]
    if last:
        layout_hbm, out_ref, prev_ref, back_hbm, kvgrad_hbm = refs[:5]
        acc, bias, back_ref, layout_ref, sems = refs[5:]
        bring = pltpu.make_async_copy(layout_hbm, layout_ref, sems.at[N_SEQ + 1])
    else:
        back_ref, kvgrad_ref, acc, bias = refs
    step = pl.program_id(0)
    plen = kv_ref.shape[0] - DH
    tops = [ref[0:1] for ref in stat_refs]
    top = functools.reduce(jnp.maximum, tops)
    share = [ref[1:2] * jnp.exp2(t - top) for ref, t in zip(stat_refs, tops)]
    inv = 1.0 / sum(share)
    delta = sum(w * ref[2:3] for w, ref in zip(share, stat_refs)) * inv
    row = lax.broadcasted_iota(jnp.int32, (8, ROWS), 0)
    weight = share[0] * inv
    columns = jnp.where(row == 0, top, jnp.where(row == 1, inv, jnp.where(row == 2, delta, weight)))
    columns = jnp.concatenate([columns] * 16, 0).T

    @pl.when(step == 0)
    def _():
        if last:
            bring.start()
        acc[...] = jnp.zeros_like(acc)
        place = lax.broadcasted_iota(jnp.int32, (8, plen), 1)
        bias[...] = jnp.where(place < bound_ref[8:16, 0:1], 0.0, NEG)

    c_top, c_inv, c_delta = columns[:, 0:1], columns[:, 1:2], columns[:, 2:3]
    q = stack_heads(q_ref)
    g = stack_heads(g_ref)
    qt = q.T
    gt = g.T
    slot = lax.broadcasted_iota(jnp.int32, (DH, SLOTS), 0)
    hidden_slots = jnp.where(slot <= bound_ref[0:1], 0.0, NEG).T
    causal = jnp.concatenate([hidden_slots] * HALF, 0)
    chunk = 256
    cuts = [slice(i, i + chunk) for i in range(0, plen, chunk)] + [slice(plen, plen + DH)]

    def products(keys):
        s = lax.dot_general(q, kv_ref[keys, :DH], NT, preferred_element_type=F32)
        return s, lax.dot_general(g, kv_ref[keys, DH:], NT, preferred_element_type=F32)

    def weights(keys, s, dp):
        hidden = bias[0:1, keys] if keys.start < plen else causal
        p = jnp.exp2(s * coef - c_top + hidden) * c_inv
        return p.astype(BF16), (p * (dp - c_delta) * scale).astype(BF16)

    def gradients(keys, p, ds):
        acc[:DH, keys] += jnp.dot(qt, ds, preferred_element_type=F32)
        acc[DH:, keys] += jnp.dot(gt, p, preferred_element_type=F32)
        return jnp.dot(ds, kv_ref[keys, :DH], preferred_element_type=F32)

    dq = jnp.zeros((ROWS, DH), F32)
    following = products(cuts[0])
    for i, keys in enumerate(cuts):
        current = following
        if i + 1 < len(cuts):
            following = products(cuts[i + 1])
        if i:
            dq = dq + gradients(cuts[i - 1], *ready)
        ready = weights(keys, *current)
    dq = dq + gradients(cuts[-1], *ready)
    parts = [slice(h * SLOTS, (h + 1) * SLOTS) for h in range(HALF)]
    if last:
        att = [out_ref[:, r].astype(F32) * columns[r, 3:4] for r in parts]
        grad = [dq[r] + prev_ref[:, r] for r in parts]
        back = jnp.concatenate(att + grad, 1).astype(BF16)

        @pl.when(step == 0)
        def _():
            bring.wait()
            back_ref[...] = jnp.zeros_like(back_ref)

        def leave(r):
            slots = pl.ds(pl.multiple_of(r * SLOTS, SLOTS), SLOTS)
            return pltpu.make_async_copy(back_ref.at[slots], back_hbm.at[slots], sems.at[r])

        def place(r, _):
            slots = pl.ds(pl.multiple_of(r * SLOTS, SLOTS), SLOTS)
            onehot = one_hot(layout_ref, r, step)
            back_ref[slots] += jnp.dot(onehot, back, preferred_element_type=F32).astype(BF16)

            @pl.when(layout_ref[r + 1] <= (step + 1) * SLOTS)
            def _():
                leave(r).start()

            return 0

        base = N_SEQ + 1 + 2 * step
        lax.fori_loop(layout_ref[base], layout_ref[base + 1], place, 0)
    else:
        for r in parts:
            back_ref[:, r] = dq[r]

    @pl.when(step == pl.num_programs(0) - 1)
    def _():
        if last:
            copy = pltpu.make_async_copy(acc, kvgrad_hbm, sems.at[N_SEQ])
            copy.start()
            for r in range(N_SEQ):
                leave(r).wait()
            copy.wait()
        else:
            kvgrad_ref[...] = acc[...].astype(BF16)


def weight_kernel(cuts, own_ref, got_ref, prompt_ref, resp_ref, *refs):
    keeps, gives = refs[:NX], refs[NX : 2 * NX]
    prompt_grad_ref, buf, whole, sems = refs[2 * NX :]
    plen = prompt_ref.shape[0]
    wide = prompt_ref.shape[1] // NX
    part = wide // 4
    copies = [
        pltpu.make_async_copy(prompt_ref.at[lo:hi], buf.at[lo:hi], sems.at[n])
        for n, (lo, hi) in enumerate(cuts)
    ]
    copies.append(pltpu.make_async_copy(resp_ref, buf.at[plen:], sems.at[len(cuts)]))
    for copy in copies:
        copy.start()
    x, core = lax.axis_index("x"), lax.axis_index("c")
    grad = (own_ref[...] + got_ref[...].astype(F32)).astype(BF16)
    prompt_grad_ref[...] = grad[:, :plen].T
    spans = list(cuts[:-1]) + [(cuts[-1][0], buf.shape[0])]
    swapped = core == 1
    for n, (lo, hi) in enumerate(spans):
        copies[n].wait()
        if n + 1 == len(spans):
            copies[n + 1].wait()
        for k in range(NX):
            cols = pl.ds(pl.multiple_of(lax.rem(x + k, NX) * wide, DH), wide)
            t = jnp.dot(grad[:, lo:hi], buf[lo:hi, cols], preferred_element_type=F32)
            if n:
                t = t + whole[k]
            if n + 1 < len(spans):
                whole[k] = t
                continue
            t = t.T
            for z in range(2):
                low = t[2 * z * part : (2 * z + 1) * part]
                high = t[(2 * z + 1) * part : (2 * z + 2) * part]
                keeps[k][z] = jnp.where(swapped, high, low)
                gives[k][z] = jnp.where(swapped, low, high).astype(BF16)


def finish_kernel(back_ref, attended_ref, query_grad_ref):
    width = back_ref.shape[2] // 2
    for side in range(2):
        total = sum(back_ref[2 * k + side].astype(F32) for k in range(NY)).astype(BF16)
        there = slice(side * width, (side + 1) * width)
        attended_ref[:, there] = total[:, :width]
        query_grad_ref[:, there] = total[:, width:]


def per_device(
    prompt_hidden, resp_hidden, queries, grad_out, kv_weight, prompt_lengths, response_lengths
):
    rank = lax.axis_index(SEQ)
    x = lax.axis_index("x")
    slots = resp_hidden.shape[1]
    plen = prompt_hidden.shape[1]
    model = prompt_hidden.shape[2]
    width = queries.shape[2]
    half = width // 2
    scale = DH ** (-0.5)
    coef = scale * LOG2E
    prompt_rows = prompt_hidden[0]
    resp_rows = resp_hidden[0]
    keys = plen + slots
    shard = kv_weight.shape[0]
    vmem = pl.BlockSpec(memory_space=pltpu.VMEM)
    hbm = pl.BlockSpec(memory_space=pltpu.HBM)

    lengths = response_lengths[0]
    live_all = slots * N_SEQ * 5 // 8
    ends = jnp.cumsum(lengths)
    packed = jnp.arange(live_all)
    past = packed[:, None] >= ends[None, :]
    source = packed + jnp.sum(jnp.where(past, slots - lengths[None, :], 0), 1)
    starts = jnp.concatenate([jnp.zeros((1,), jnp.int32), ends.astype(jnp.int32)])
    lows = jnp.arange(live_all // SLOTS)[:, None] * SLOTS
    first = jnp.sum(ends[None, :] <= lows, 1)
    behind = jnp.sum((ends - lengths)[None, :] < lows + SLOTS, 1)
    spans = jnp.stack([first, behind], 1).astype(jnp.int32).reshape(-1)
    layout = jnp.concatenate([starts, spans])
    layout = jnp.pad(layout, (0, 3 * N_SEQ - layout.shape[0]))

    def bounds(owner):
        offset = source - owner * slots
        limit = jnp.where((offset >= 0) & (offset < slots), offset, -1)
        live = jnp.broadcast_to(prompt_lengths[0] - plen * owner, (8, live_all))
        return jnp.concatenate([jnp.broadcast_to(limit[None, :], (8, live_all)), live], 0).astype(jnp.int32)

    mine, others = bounds(rank), bounds(rank ^ 1)

    block = pl.pallas_call(
        copies_kernel,
        in_specs=[vmem],
        out_specs=vmem,
        out_shape=jax.ShapeDtypeStruct((16,) + kv_weight.shape, BF16),
        compiler_params=params(16),
        name="weight_copies",
    )(kv_weight)
    block = lax.all_to_all(block, PLANE, 0, 0, tiled=True).reshape(2, 8 * shard, 2 * DH)

    qg = pl.pallas_call(
        halves_kernel,
        in_specs=[vmem] * 2,
        out_specs=pl.BlockSpec(memory_space=pl.ANY),
        out_shape=jax.ShapeDtypeStruct((N_SEQ, slots, 2 * half), BF16),
        scratch_shapes=[pltpu.VMEM((2, slots, 2 * half), BF16), pltpu.SemaphoreType.DMA((NY,))],
        compiler_params=params(16),
        cost_estimate=pl.CostEstimate(flops=0, bytes_accessed=8 << 20, transcendentals=0),
        name="query_halves",
    )(queries[0], grad_out[0])
    small = (source, layout, mine, others)
    qg, block, small = lax.optimization_barrier((qg, block, small))
    source, layout, mine, others = small
    opposite = lax.ppermute(block, "x", shift(2))
    nears = [block, lax.ppermute(block, "x", shift(1)), opposite, lax.ppermute(block, "x", shift(3))]
    fars = [lax.ppermute(block, "c", SWAP)]
    qg_all = lax.all_to_all(qg, SEQ, 0, 0, tiled=True).reshape(N_SEQ * slots, 2 * half)

    def project(steps, prev, last):
        count = len(steps)
        return pl.pallas_call(
            functools.partial(project_kernel, steps, prev is None, last),
            in_specs=[vmem] * (2 + 2 * count + (prev is not None)),
            out_specs=vmem,
            out_shape=jax.ShapeDtypeStruct((keys, 2 * DH), BF16 if last else F32),
            scratch_shapes=[pltpu.VMEM((count * model // NX, 2 * DH), BF16)],
            compiler_params=params(20),
            cost_estimate=pl.CostEstimate(
                flops=2 * keys * model * DH * count // 2,
                bytes_accessed=keys * model * count // 2,
                transcendentals=0,
            ),
            name="project_last" if last else "project",
        )(
            prompt_rows, resp_rows, *[nears[k] for k in steps], *[fars[k] for k in steps],
            *(() if prev is None else (prev,)),
        )

    kv = project((0,), None, False)
    nears[3], kv = lax.optimization_barrier((nears[3], kv))
    fars = fars + [lax.ppermute(piece, "c", SWAP) for piece in nears[1:]]
    kv = project((3,), kv, False)
    kv = project((1, 2), kv, True)
    kv_other = lax.ppermute(kv, "zl", SWAP)

    steps = live_all // SLOTS
    rows = live_all * HALF
    whole = pl.BlockSpec((keys, 2 * DH), lambda i: (0, 0))
    slot_block = pl.BlockSpec((SLOTS, half), lambda i: (i, 0))
    g_block = pl.BlockSpec((SLOTS, half), lambda i: (i, 1))
    lane_block = pl.BlockSpec((DH, ROWS), lambda i: (0, i))
    stat_block = pl.BlockSpec((3, ROWS), lambda i: (0, i))


    def forward(owner, kv, more):
        last = bool(more)
        return pl.pallas_call(
            functools.partial(first_pass, coef, last),
            grid=(steps,),
            in_specs=[pl.BlockSpec((16, SLOTS), lambda i: (0, i)), slot_block, whole]
            + [g_block, lane_block, stat_block] * last,
            out_specs=[slot_block if last else lane_block, stat_block],
            out_shape=[
                jax.ShapeDtypeStruct((live_all, half), BF16)
                if last
                else jax.ShapeDtypeStruct((DH, rows), F32),
                jax.ShapeDtypeStruct((3, rows), F32),
            ],
            scratch_shapes=[pltpu.VMEM((plen, DH), F32), pltpu.VMEM((DH, keys), BF16)],
            compiler_params=params(20),
            cost_estimate=pl.CostEstimate(
                flops=4 * rows * keys * DH, bytes_accessed=4 << 20, transcendentals=rows * keys
            ),
            name="attend_more" if last else "attend_own",
        )(owner, qg, kv, *more)

    pick = (source[:, None] == jnp.arange(N_SEQ * slots)[None, :]).astype(BF16)
    qg = jnp.dot(pick, qg_all, preferred_element_type=F32).astype(BF16)
    state = forward(mine, kv, ())
    out, stat = forward(others, kv_other, (qg, *state))
    stats = [stat] + [lax.ppermute(stat, "y", shift(k)) for k in range(1, NY)]

    def backward(owner, kv, more):
        last = bool(more)
        return pl.pallas_call(
            functools.partial(second_pass, coef, scale, last),
            grid=(steps,),
            in_specs=[
                pl.BlockSpec((16, SLOTS), lambda i: (0, i)), slot_block, g_block, whole,
            ] + [stat_block] * NY + [hbm, slot_block, slot_block] * last,
            out_specs=[hbm, hbm]
            if last
            else [slot_block, pl.BlockSpec((2 * DH, keys), lambda i: (0, 0))],
            out_shape=[
                pltpu.HBM((N_SEQ * slots, 2 * half), BF16),
                pltpu.HBM((2 * DH, keys), F32),
            ]
            if last
            else [
                jax.ShapeDtypeStruct((live_all, half), F32),
                jax.ShapeDtypeStruct((2 * DH, keys), BF16),
            ],
            scratch_shapes=[pltpu.VMEM((2 * DH, keys), F32), pltpu.VMEM((8, plen), F32)]
            + [
                pltpu.VMEM((N_SEQ * slots, 2 * half), BF16),
                pltpu.SMEM((3 * N_SEQ,), jnp.int32),
                pltpu.SemaphoreType.DMA((N_SEQ + 2,)),
            ]
            * last,
            compiler_params=params(20),
            cost_estimate=pl.CostEstimate(
                flops=10 * rows * keys * DH, bytes_accessed=8 << 20, transcendentals=rows * keys
            ),
            name="grads_own" if last else "grads_other",
        )(owner, qg, qg, kv, *stats, *more)

    qgrad_part, kvgrad_other = backward(others, kv_other, ())
    kvgrad_got = lax.ppermute(kvgrad_other, "zl", SWAP)
    back, kvgrad_own = backward(mine, kv, (layout, out, qgrad_part))

    back, kvgrad_own = lax.optimization_barrier((back, kvgrad_own))
    back = lax.all_to_all(back.reshape(N_SEQ, slots, 2 * half), SEQ, 0, 0, tiled=True)

    cuts = ((0, plen // 2), (plen // 2, plen))
    piece = (2, 8 * shard, 2 * DH)
    *pieces, prompt_grad = pl.pallas_call(
        functools.partial(weight_kernel, cuts),
        in_specs=[vmem] * 2 + [pl.BlockSpec(memory_space=pltpu.HBM)] * 2,
        out_specs=[vmem] * (2 * NX + 1),
        out_shape=[jax.ShapeDtypeStruct(piece, F32)] * NX
        + [jax.ShapeDtypeStruct(piece, BF16)] * NX
        + [jax.ShapeDtypeStruct((plen, 2 * DH), BF16)],
        scratch_shapes=[
            pltpu.VMEM((keys, model), BF16),
            pltpu.VMEM((NX, 2 * DH, model // NX), F32),
            pltpu.SemaphoreType.DMA((len(cuts) + 1,)),
        ],
        compiler_params=params(50),
        cost_estimate=pl.CostEstimate(
            flops=4 * keys * model * DH, bytes_accessed=2 * keys * model, transcendentals=0
        ),
        name="weight_grad",
    )(kvgrad_own, kvgrad_got, prompt_rows, resp_rows)
    keeps, gives = pieces[:NX], pieces[NX:]
    got = {k: lax.ppermute(gives[k], "c", SWAP) for k in (2, 1, 3, 0)}
    moved = []
    for k in (2, 1, 3):
        piece = (keeps[k] + got[k].astype(F32)).astype(BF16)
        moved.append(lax.ppermute(piece, "x", shift(-k)))
    line = keeps[0] + got[0].astype(F32)
    line = line + moved[0].astype(F32) + moved[1].astype(F32) + moved[2].astype(F32)
    line = line.astype(BF16).reshape(16, shard, 2 * DH)
    line, back = lax.optimization_barrier((line, back))
    shares = lax.all_to_all(line, PLANE, 0, 0, tiled=True)
    weight_grad = jnp.sum(shares.astype(F32), 0)

    attended, query_grad = pl.pallas_call(
        finish_kernel,
        in_specs=[vmem],
        out_specs=[vmem] * 2,
        out_shape=[jax.ShapeDtypeStruct((slots, width), BF16)] * 2,
        compiler_params=params(16),
        name="finish",
    )(back)
    return attended[None], query_grad[None], prompt_grad[None], weight_grad


def solution(mesh):
    fine = Mesh(mesh.devices.reshape(4, 2, 2, 4, 2), AXES)
    return jax.shard_map(
        per_device,
        mesh=fine,
        in_specs=(
            P(GRP, SEQ, None),
            P(GRP, SEQ, None),
            P(GRP, SEQ, None),
            P(GRP, SEQ, None),
            P(AXES, None),
            P(GRP),
            P(GRP, None),
        ),
        out_specs=(
            P(GRP, SEQ, None),
            P(GRP, SEQ, None),
            P(GRP, SEQ, None),
            P(AXES, None),
        ),
        check_vma=False,
    )
```

```python
import functools

import jax
import jax.numpy as jnp
from jax import lax
from jax.experimental import pallas as pl
from jax.experimental.pallas import tpu as pltpu
from jax.sharding import Mesh
from jax.sharding import PartitionSpec as P

AXES = ("x", "zh", "c", "y", "zl")
GRP = ("x", "zh", "c")
SEQ = ("y", "zl")
PLANE = ("zh", "y", "zl")
N_SEQ = 8
NX = 4
NY = 4
HEADS = 8
HALF = 4
DH = 128
SLOTS = 128
ROWS = HALF * SLOTS
NEG = -1e30
LOG2E = 1.4426950408889634
NT = (((1,), (1,)), ((), ()))
TN = (((0,), (0,)), ((), ()))
F32 = jnp.float32
BF16 = jnp.bfloat16
SWAP = [(0, 1), (1, 0)]


def params(mib):
    return pltpu.CompilerParams(vmem_limit_bytes=mib << 20)


def shift(k):
    return [((i + k) % 4, i) for i in range(4)]


def stack_heads(ref):
    return jnp.concatenate([ref[:, h * DH : (h + 1) * DH] for h in range(HALF)], 0)


def copies_kernel(block_ref, out_ref):
    for i in range(out_ref.shape[0]):
        out_ref[i] = block_ref[...]


def halves_kernel(q_ref, g_ref, out_ref, buf, sems):
    half = q_ref.shape[1] // 2
    for side in range(2):
        cols = slice(side * half, (side + 1) * half)
        buf[side, :, :half] = q_ref[:, cols]
        buf[side, :, half:] = g_ref[:, cols]
    copies = [
        pltpu.make_async_copy(buf, out_ref.at[2 * k : 2 * k + 2], sems.at[k]) for k in range(NY)
    ]
    for copy in copies:
        copy.start()
    for copy in copies:
        copy.wait()


def project_kernel(steps, first, last, prompt_ref, resp_ref, *refs):
    refs = list(refs)
    nears = [refs.pop(0) for _ in steps]
    fars = [refs.pop(0) for _ in steps]
    prev_ref = None if first else refs.pop(0)
    kv_ref, weight = refs
    plen = prompt_ref.shape[0]
    wide = prompt_ref.shape[1] // NX
    half = wide // 2
    part = wide // 4
    x, core = lax.axis_index("x"), lax.axis_index("c")
    tops, ends = [], []
    for n, k in enumerate(steps):
        for z in range(2):
            base = n * wide + z * half
            weight[pl.ds(pl.multiple_of(base + core * part, part), part)] = nears[n][z]
            weight[pl.ds(pl.multiple_of(base + (1 - core) * part, part), part)] = fars[n][z]
        cols = pl.ds(pl.multiple_of(lax.rem(x + k, NX) * wide, DH), wide)
        w = weight[n * wide : (n + 1) * wide]
        tops.append(jnp.dot(prompt_ref[:, cols], w, preferred_element_type=F32))
        ends.append(jnp.dot(resp_ref[:, cols], w, preferred_element_type=F32))
    top, end = sum(tops[1:], tops[0]), sum(ends[1:], ends[0])
    if not first:
        top, end = top + prev_ref[:plen], end + prev_ref[plen:]
    kv_ref[:plen] = top.astype(kv_ref.dtype)
    kv_ref[plen:] = end.astype(kv_ref.dtype)


def first_pass(coef, last, bound_ref, *refs):
    if last:
        q_ref, kv_ref, g_ref, prev_out_ref, prev_stat_ref, out_ref, stat_ref, bias, values = refs
    else:
        q_ref, kv_ref, out_ref, stat_ref, bias, values = refs
    plen = kv_ref.shape[0] - DH

    @pl.when(pl.program_id(0) == 0)
    def _():
        place = lax.broadcasted_iota(jnp.int32, (plen, DH), 0)
        bias[...] = jnp.where(place < bound_ref[8:9], 0.0, NEG)
        values[...] = kv_ref[:, DH:].T

    slot = lax.broadcasted_iota(jnp.int32, (DH, SLOTS), 0)
    causal = jnp.where(slot <= bound_ref[0:1], 0.0, NEG)
    bias_all = jnp.concatenate([bias[...], causal], 0)
    bias_all = jnp.concatenate([bias_all] * 2, 1)
    keys = kv_ref[:, :DH]

    def scores(i):
        q = jnp.concatenate([q_ref[:, h * DH : (h + 1) * DH] for h in (2 * i, 2 * i + 1)], 0)
        return lax.dot_general(keys, q, NT, preferred_element_type=F32)

    following = scores(0)
    for i in range(HALF // 2):
        s = following * coef + bias_all
        if i + 1 < HALF // 2:
            following = scores(i + 1)
        lanes = slice(2 * i * SLOTS, 2 * (i + 1) * SLOTS)
        top = jnp.max(s, 0, keepdims=True)
        if last:
            before = prev_stat_ref[0:1, lanes]
            top = jnp.maximum(top, before)
        p = jnp.exp2(s - top)
        total = jnp.sum(p, 0, keepdims=True)
        o = jnp.dot(values[...], p.astype(BF16), preferred_element_type=F32)
        if last:
            alpha = jnp.exp2(before - top)
            total = total + prev_stat_ref[1:2, lanes] * alpha
            o = (o + prev_out_ref[:, lanes] * alpha) / total
            for j in range(2):
                h = 2 * i + j
                cols = slice(h * DH, (h + 1) * DH)
                part = o[:, j * SLOTS : (j + 1) * SLOTS]
                d = jnp.sum(part * g_ref[:, cols].astype(F32).T, 0, keepdims=True)
                stat_ref[2:3, h * SLOTS : (h + 1) * SLOTS] = d
                out_ref[:, cols] = part.T.astype(BF16)
        else:
            out_ref[:, lanes] = o
        stat_ref[0:1, lanes] = top
        stat_ref[1:2, lanes] = total


def second_pass(coef, scale, last, bound_ref, q_ref, g_ref, kv_ref, *refs):
    stat_refs, refs = refs[:NY], refs[NY:]
    if last:
        layout_hbm, out_ref, prev_ref, back_hbm, kvgrad_hbm = refs[:5]
        acc, bias, packed, back_ref, layout_ref, sems = refs[5:]
        bring = pltpu.make_async_copy(layout_hbm, layout_ref, sems.at[N_SEQ + 1])
    else:
        back_ref, kvgrad_ref, acc, bias = refs
    step = pl.program_id(0)
    plen = kv_ref.shape[0] - DH
    tops = [ref[0:1] for ref in stat_refs]
    top = functools.reduce(jnp.maximum, tops)
    share = [ref[1:2] * jnp.exp2(t - top) for ref, t in zip(stat_refs, tops)]
    inv = 1.0 / sum(share)
    delta = sum(w * ref[2:3] for w, ref in zip(share, stat_refs)) * inv
    row = lax.broadcasted_iota(jnp.int32, (8, ROWS), 0)
    weight = share[0] * inv
    columns = jnp.where(row == 0, top, jnp.where(row == 1, inv, jnp.where(row == 2, delta, weight)))
    columns = jnp.concatenate([columns] * 16, 0).T

    @pl.when(step == 0)
    def _():
        if last:
            bring.start()
        acc[...] = jnp.zeros_like(acc)
        place = lax.broadcasted_iota(jnp.int32, (8, plen), 1)
        bias[...] = jnp.where(place < bound_ref[8:16, 0:1], 0.0, NEG)

    c_top, c_inv, c_delta = columns[:, 0:1], columns[:, 1:2], columns[:, 2:3]
    q = stack_heads(q_ref)
    g = stack_heads(g_ref)
    qt = q.T
    gt = g.T
    slot = lax.broadcasted_iota(jnp.int32, (DH, SLOTS), 0)
    hidden_slots = jnp.where(slot <= bound_ref[0:1], 0.0, NEG).T
    causal = jnp.concatenate([hidden_slots] * HALF, 0)
    chunk = 256
    cuts = [slice(i, i + chunk) for i in range(0, plen, chunk)] + [slice(plen, plen + DH)]

    def products(keys):
        s = lax.dot_general(q, kv_ref[keys, :DH], NT, preferred_element_type=F32)
        return s, lax.dot_general(g, kv_ref[keys, DH:], NT, preferred_element_type=F32)

    def weights(keys, s, dp):
        hidden = bias[0:1, keys] if keys.start < plen else causal
        p = jnp.exp2(s * coef - c_top + hidden) * c_inv
        return p.astype(BF16), (p * (dp - c_delta) * scale).astype(BF16)

    def gradients(keys, p, ds):
        acc[:DH, keys] += jnp.dot(qt, ds, preferred_element_type=F32)
        acc[DH:, keys] += jnp.dot(gt, p, preferred_element_type=F32)
        return jnp.dot(ds, kv_ref[keys, :DH], preferred_element_type=F32)

    dq = jnp.zeros((ROWS, DH), F32)
    following = products(cuts[0])
    for i, keys in enumerate(cuts):
        current = following
        if i + 1 < len(cuts):
            following = products(cuts[i + 1])
        if i:
            dq = dq + gradients(cuts[i - 1], *ready)
        ready = weights(keys, *current)
    dq = dq + gradients(cuts[-1], *ready)
    parts = [slice(h * SLOTS, (h + 1) * SLOTS) for h in range(HALF)]
    if last:
        att = [out_ref[:, r].astype(F32) * columns[r, 3:4] for r in parts]
        grad = [dq[r] + prev_ref[:, r] for r in parts]
        here = pl.ds(pl.multiple_of(step * SLOTS, SLOTS), SLOTS)
        for i, part in enumerate(att + grad):
            packed[here, i * DH : (i + 1) * DH] = part

        @pl.when(step == 0)
        def _():
            bring.wait()

        def leave(r):
            slots = pl.ds(pl.multiple_of(r * SLOTS, SLOTS), SLOTS)
            return pltpu.make_async_copy(back_ref.at[slots], back_hbm.at[slots], sems.at[r])

        def place(r, _):
            slots = pl.ds(pl.multiple_of(r * SLOTS, SLOTS), SLOTS)
            start = layout_ref[r]
            even = pl.multiple_of(lax.div(start, 8) * 8, 8)
            back_by = SLOTS + 8 - (start - even)
            live = lax.broadcasted_iota(jnp.int32, (SLOTS, DH), 0) < layout_ref[r + 1] - start
            for i in range(2 * HALF):
                cols = slice(i * DH, (i + 1) * DH)
                window = pltpu.roll(packed[pl.ds(even, SLOTS + 8), cols], back_by, 0)[:SLOTS]
                back_ref[slots, cols] = jnp.where(live, window, 0.0).astype(BF16)
            leave(r).start()
            return 0

        base = N_SEQ + 1 + step
        lax.fori_loop(layout_ref[base], layout_ref[base + 1], place, 0)
    else:
        for r in parts:
            back_ref[:, r] = dq[r]

    @pl.when(step == pl.num_programs(0) - 1)
    def _():
        if last:
            copy = pltpu.make_async_copy(acc, kvgrad_hbm, sems.at[N_SEQ])
            copy.start()
            for r in range(N_SEQ):
                leave(r).wait()
            copy.wait()
        else:
            kvgrad_ref[...] = acc[...].astype(BF16)


def weight_kernel(cuts, own_ref, got_ref, prompt_ref, resp_ref, *refs):
    keeps, gives = refs[:NX], refs[NX : 2 * NX]
    prompt_grad_ref, buf, whole, sems = refs[2 * NX :]
    plen = prompt_ref.shape[0]
    wide = prompt_ref.shape[1] // NX
    part = wide // 4
    copies = [
        pltpu.make_async_copy(prompt_ref.at[lo:hi], buf.at[lo:hi], sems.at[n])
        for n, (lo, hi) in enumerate(cuts)
    ]
    copies.append(pltpu.make_async_copy(resp_ref, buf.at[plen:], sems.at[len(cuts)]))
    for copy in copies:
        copy.start()
    x, core = lax.axis_index("x"), lax.axis_index("c")
    grad = (own_ref[...] + got_ref[...].astype(F32)).astype(BF16)
    prompt_grad_ref[...] = grad[:, :plen].T
    spans = list(cuts[:-1]) + [(cuts[-1][0], buf.shape[0])]
    swapped = core == 1
    for n, (lo, hi) in enumerate(spans):
        copies[n].wait()
        if n + 1 == len(spans):
            copies[n + 1].wait()
        for k in range(NX):
            cols = pl.ds(pl.multiple_of(lax.rem(x + k, NX) * wide, DH), wide)
            t = jnp.dot(grad[:, lo:hi], buf[lo:hi, cols], preferred_element_type=F32)
            if n:
                t = t + whole[k]
            if n + 1 < len(spans):
                whole[k] = t
                continue
            t = t.T
            for z in range(2):
                low = t[2 * z * part : (2 * z + 1) * part]
                high = t[(2 * z + 1) * part : (2 * z + 2) * part]
                keeps[k][z] = jnp.where(swapped, high, low)
                gives[k][z] = jnp.where(swapped, low, high).astype(BF16)


def finish_kernel(back_ref, attended_ref, query_grad_ref):
    width = back_ref.shape[2] // 2
    for side in range(2):
        total = sum(back_ref[2 * k + side].astype(F32) for k in range(NY)).astype(BF16)
        there = slice(side * width, (side + 1) * width)
        attended_ref[:, there] = total[:, :width]
        query_grad_ref[:, there] = total[:, width:]


def per_device(
    prompt_hidden, resp_hidden, queries, grad_out, kv_weight, prompt_lengths, response_lengths
):
    rank = lax.axis_index(SEQ)
    x = lax.axis_index("x")
    slots = resp_hidden.shape[1]
    plen = prompt_hidden.shape[1]
    model = prompt_hidden.shape[2]
    width = queries.shape[2]
    half = width // 2
    scale = DH ** (-0.5)
    coef = scale * LOG2E
    prompt_rows = prompt_hidden[0]
    resp_rows = resp_hidden[0]
    keys = plen + slots
    shard = kv_weight.shape[0]
    vmem = pl.BlockSpec(memory_space=pltpu.VMEM)
    hbm = pl.BlockSpec(memory_space=pltpu.HBM)

    lengths = response_lengths[0]
    live_all = slots * N_SEQ * 5 // 8
    ends = jnp.cumsum(lengths)
    packed = jnp.arange(live_all)
    past = packed[:, None] >= ends[None, :]
    source = packed + jnp.sum(jnp.where(past, slots - lengths[None, :], 0), 1)
    starts = jnp.concatenate([jnp.zeros((1,), jnp.int32), ends.astype(jnp.int32)])
    lows = jnp.arange(live_all // SLOTS + 1)[:, None] * SLOTS
    before = jnp.sum(ends[None, :] <= lows, 1).astype(jnp.int32)
    layout = jnp.concatenate([starts, before])
    layout = jnp.pad(layout, (0, 3 * N_SEQ - layout.shape[0]))

    def bounds(owner):
        offset = source - owner * slots
        limit = jnp.where((offset >= 0) & (offset < slots), offset, -1)
        live = jnp.broadcast_to(prompt_lengths[0] - plen * owner, (8, live_all))
        return jnp.concatenate([jnp.broadcast_to(limit[None, :], (8, live_all)), live], 0).astype(jnp.int32)

    mine, others = bounds(rank), bounds(rank ^ 1)

    block = pl.pallas_call(
        copies_kernel,
        in_specs=[vmem],
        out_specs=vmem,
        out_shape=jax.ShapeDtypeStruct((16,) + kv_weight.shape, BF16),
        compiler_params=params(16),
        name="weight_copies",
    )(kv_weight)
    block = lax.all_to_all(block, PLANE, 0, 0, tiled=True).reshape(2, 8 * shard, 2 * DH)

    qg = pl.pallas_call(
        halves_kernel,
        in_specs=[vmem] * 2,
        out_specs=pl.BlockSpec(memory_space=pl.ANY),
        out_shape=jax.ShapeDtypeStruct((N_SEQ, slots, 2 * half), BF16),
        scratch_shapes=[pltpu.VMEM((2, slots, 2 * half), BF16), pltpu.SemaphoreType.DMA((NY,))],
        compiler_params=params(16),
        cost_estimate=pl.CostEstimate(flops=0, bytes_accessed=8 << 20, transcendentals=0),
        name="query_halves",
    )(queries[0], grad_out[0])
    small = (source, layout, mine, others)
    qg, block, small = lax.optimization_barrier((qg, block, small))
    source, layout, mine, others = small
    opposite = lax.ppermute(block, "x", shift(2))
    nears = [block, lax.ppermute(block, "x", shift(1)), opposite, lax.ppermute(block, "x", shift(3))]
    fars = [lax.ppermute(block, "c", SWAP)]
    qg_all = lax.all_to_all(qg, SEQ, 0, 0, tiled=True).reshape(N_SEQ * slots, 2 * half)

    def project(steps, prev, last):
        count = len(steps)
        return pl.pallas_call(
            functools.partial(project_kernel, steps, prev is None, last),
            in_specs=[vmem] * (2 + 2 * count + (prev is not None)),
            out_specs=vmem,
            out_shape=jax.ShapeDtypeStruct((keys, 2 * DH), BF16 if last else F32),
            scratch_shapes=[pltpu.VMEM((count * model // NX, 2 * DH), BF16)],
            compiler_params=params(20),
            cost_estimate=pl.CostEstimate(
                flops=2 * keys * model * DH * count // 2,
                bytes_accessed=keys * model * count // 2,
                transcendentals=0,
            ),
            name="project_last" if last else "project",
        )(
            prompt_rows, resp_rows, *[nears[k] for k in steps], *[fars[k] for k in steps],
            *(() if prev is None else (prev,)),
        )

    kv = project((0,), None, False)
    nears[3], kv = lax.optimization_barrier((nears[3], kv))
    fars = fars + [lax.ppermute(piece, "c", SWAP) for piece in nears[1:]]
    kv = project((3,), kv, False)
    kv = project((1, 2), kv, True)
    kv_other = lax.ppermute(kv, "zl", SWAP)

    steps = live_all // SLOTS
    rows = live_all * HALF
    whole = pl.BlockSpec((keys, 2 * DH), lambda i: (0, 0))
    slot_block = pl.BlockSpec((SLOTS, half), lambda i: (i, 0))
    g_block = pl.BlockSpec((SLOTS, half), lambda i: (i, 1))
    lane_block = pl.BlockSpec((DH, ROWS), lambda i: (0, i))
    stat_block = pl.BlockSpec((3, ROWS), lambda i: (0, i))


    def forward(owner, kv, more):
        last = bool(more)
        return pl.pallas_call(
            functools.partial(first_pass, coef, last),
            grid=(steps,),
            in_specs=[pl.BlockSpec((16, SLOTS), lambda i: (0, i)), slot_block, whole]
            + [g_block, lane_block, stat_block] * last,
            out_specs=[slot_block if last else lane_block, stat_block],
            out_shape=[
                jax.ShapeDtypeStruct((live_all, half), BF16)
                if last
                else jax.ShapeDtypeStruct((DH, rows), F32),
                jax.ShapeDtypeStruct((3, rows), F32),
            ],
            scratch_shapes=[pltpu.VMEM((plen, DH), F32), pltpu.VMEM((DH, keys), BF16)],
            compiler_params=params(20),
            cost_estimate=pl.CostEstimate(
                flops=4 * rows * keys * DH, bytes_accessed=4 << 20, transcendentals=rows * keys
            ),
            name="attend_more" if last else "attend_own",
        )(owner, qg, kv, *more)

    pick = (source[:, None] == jnp.arange(N_SEQ * slots)[None, :]).astype(BF16)
    qg = jnp.dot(pick, qg_all, preferred_element_type=F32).astype(BF16)
    state = forward(mine, kv, ())
    out, stat = forward(others, kv_other, (qg, *state))
    stats = [stat] + [lax.ppermute(stat, "y", shift(k)) for k in range(1, NY)]

    def backward(owner, kv, more):
        last = bool(more)
        return pl.pallas_call(
            functools.partial(second_pass, coef, scale, last),
            grid=(steps,),
            in_specs=[
                pl.BlockSpec((16, SLOTS), lambda i: (0, i)), slot_block, g_block, whole,
            ] + [stat_block] * NY + [hbm, slot_block, slot_block] * last,
            out_specs=[hbm, hbm]
            if last
            else [slot_block, pl.BlockSpec((2 * DH, keys), lambda i: (0, 0))],
            out_shape=[
                pltpu.HBM((N_SEQ * slots, 2 * half), BF16),
                pltpu.HBM((2 * DH, keys), F32),
            ]
            if last
            else [
                jax.ShapeDtypeStruct((live_all, half), F32),
                jax.ShapeDtypeStruct((2 * DH, keys), BF16),
            ],
            scratch_shapes=[pltpu.VMEM((2 * DH, keys), F32), pltpu.VMEM((8, plen), F32)]
            + [
                pltpu.VMEM((live_all + slots, 2 * half), F32),
                pltpu.VMEM((N_SEQ * slots, 2 * half), BF16),
                pltpu.SMEM((3 * N_SEQ,), jnp.int32),
                pltpu.SemaphoreType.DMA((N_SEQ + 2,)),
            ]
            * last,
            compiler_params=params(20),
            cost_estimate=pl.CostEstimate(
                flops=10 * rows * keys * DH, bytes_accessed=8 << 20, transcendentals=rows * keys
            ),
            name="grads_own" if last else "grads_other",
        )(owner, qg, qg, kv, *stats, *more)

    qgrad_part, kvgrad_other = backward(others, kv_other, ())
    kvgrad_got = lax.ppermute(kvgrad_other, "zl", SWAP)
    back, kvgrad_own = backward(mine, kv, (layout, out, qgrad_part))

    back, kvgrad_own = lax.optimization_barrier((back, kvgrad_own))
    back = lax.all_to_all(back.reshape(N_SEQ, slots, 2 * half), SEQ, 0, 0, tiled=True)

    cuts = ((0, plen // 2), (plen // 2, plen))
    piece = (2, 8 * shard, 2 * DH)
    *pieces, prompt_grad = pl.pallas_call(
        functools.partial(weight_kernel, cuts),
        in_specs=[vmem] * 2 + [pl.BlockSpec(memory_space=pltpu.HBM)] * 2,
        out_specs=[vmem] * (2 * NX + 1),
        out_shape=[jax.ShapeDtypeStruct(piece, F32)] * NX
        + [jax.ShapeDtypeStruct(piece, BF16)] * NX
        + [jax.ShapeDtypeStruct((plen, 2 * DH), BF16)],
        scratch_shapes=[
            pltpu.VMEM((keys, model), BF16),
            pltpu.VMEM((NX, 2 * DH, model // NX), F32),
            pltpu.SemaphoreType.DMA((len(cuts) + 1,)),
        ],
        compiler_params=params(50),
        cost_estimate=pl.CostEstimate(
            flops=4 * keys * model * DH, bytes_accessed=2 * keys * model, transcendentals=0
        ),
        name="weight_grad",
    )(kvgrad_own, kvgrad_got, prompt_rows, resp_rows)
    keeps, gives = pieces[:NX], pieces[NX:]
    got = {k: lax.ppermute(gives[k], "c", SWAP) for k in (2, 1, 3, 0)}
    moved = []
    for k in (2, 1, 3):
        piece = (keeps[k] + got[k].astype(F32)).astype(BF16)
        moved.append(lax.ppermute(piece, "x", shift(-k)))
    line = keeps[0] + got[0].astype(F32)
    line = line + moved[0].astype(F32) + moved[1].astype(F32) + moved[2].astype(F32)
    line = line.astype(BF16).reshape(16, shard, 2 * DH)
    line, back = lax.optimization_barrier((line, back))
    shares = lax.all_to_all(line, PLANE, 0, 0, tiled=True)
    weight_grad = jnp.sum(shares.astype(F32), 0)

    attended, query_grad = pl.pallas_call(
        finish_kernel,
        in_specs=[vmem],
        out_specs=[vmem] * 2,
        out_shape=[jax.ShapeDtypeStruct((slots, width), BF16)] * 2,
        compiler_params=params(16),
        name="finish",
    )(back)
    return attended[None], query_grad[None], prompt_grad[None], weight_grad


def solution(mesh):
    fine = Mesh(mesh.devices.reshape(4, 2, 2, 4, 2), AXES)
    return jax.shard_map(
        per_device,
        mesh=fine,
        in_specs=(
            P(GRP, SEQ, None),
            P(GRP, SEQ, None),
            P(GRP, SEQ, None),
            P(GRP, SEQ, None),
            P(AXES, None),
            P(GRP),
            P(GRP, None),
        ),
        out_specs=(
            P(GRP, SEQ, None),
            P(GRP, SEQ, None),
            P(GRP, SEQ, None),
            P(AXES, None),
        ),
        check_vma=False,
    )
```
